32 devices in a mesh: grp: 2 (over y), row: 4 (over z), col: 2 (over x), lay: 2 (over core).
Axes of the slice: x: 2, y: 2, z: 4, core: 2. Of those that a mesh axis runs over, the one named last changes fastest.
Arguments:
- earlier_heat_level: float32 [16, 96, 1536], P('grp', 'row', ('col', 'lay')), parts along dimension 0, may hold values from 0 to 2
- substance_per_heat_node: int32 [16, 96, 1536], P('grp', 'row', ('col', 'lay')), parts along dimension 0, may hold values from 0 to 15
- die_heating_source: float32 [192, 1536], P(('grp', 'row'), ('col', 'lay')), parts along dimension 0, may hold values from 0.2 to 5
- substance_per_solid_element: int32 [12, 32, 512], P('grp', ('row', 'lay'), 'col'), parts along dimension 0, may hold values from 0 to 15
- earlier_solid_offset: float32 [3, 12, 32, 512], P(None, 'grp', ('row', 'lay'), 'col'), parts along dimension 1, may hold values from -2.5 to 2.5
- heat_transfer_per_substance: float32 [16], replicated, may hold values from 0.5 to 8
- growth_rate_per_substance: float32 [16], replicated, may hold values from 0.2 to 2
- elastic_modulus_per_substance: float32 [16], replicated, may hold values from 0.5 to 5
Outputs:
- temperature: float32 [16, 96, 1536], P('grp', 'row', ('col', 'lay')), parts along dimension 0
- displacement: float32 [3, 12, 32, 512], P(None, 'grp', ('row', 'lay'), 'col'), parts along dimension 1
- slowdown_factor: float32 [192, 1536], P(('grp', 'row'), ('col', 'lay')), parts along dimension 0
The draws below stay inside these ranges and needn't reach their ends.
There are 2 independent parts, one for each index of `grp`. The reference program is written for one: setup_inputs(seed, part) draws one part's arguments, and reference() takes and returns one part's arrays. A program takes and returns all parts, laid end to end along the dimension named above; an argument that names none is the same for every part. Nothing has to cross between parts.
All inputs are finite; a program needn't handle non-finite values.
Results may differ from the reference program's by a relative error of at most 0.00002.
Values sent between devices are 32-bit elements; how exact they have to be, the bound alone decides.
No kernel may reach another device: no remote copies, remote signals or barrier semaphores. Data moves between devices by JAX's collectives and lax.ppermute only.
A program may use at most 64 MiB of HBM per device.

```python
import math
import jax
import jax.numpy as jnp
import numpy as np
from jax import lax

HEAT_GRID_DEPTH = 8
ML = 6
NMAT = 16
THERMAL_SWEEPS = 2
MECH_SWEEPS = 2
HEAT_GRID_HEIGHT = 96
HEAT_GRID_WIDTH = 1536
MX = 32
MY = 512


def plant(entries, rng, smallest, high):
    longest = entries.shape.index(max(entries.shape))
    spots = []
    for shift in (0, 1):
        where = [jax.random.randint(jax.random.fold_in(rng, axis), (), 0, length) for axis, length in enumerate(entries.shape)]
        where[longest] = (where[longest] + shift) % entries.shape[longest]
        spots.append(tuple(where))
    return entries.at[spots[0]].set(smallest).at[spots[1]].set(high)


def shard_levels(rng, shape, shards, low, top_value):
    gain, own = 1.0, jax.random.fold_in(rng, 6)
    for dim, parts in shards:
        draws = jnp.exp(jax.random.uniform(jax.random.fold_in(own, dim), (parts,), jnp.float32, low / len(shards), top_value / len(shards)))
        gain = gain * jnp.repeat(draws, shape[dim] // parts).reshape([-1 if axis == dim else 1 for axis in range(len(shape))])
    return gain


def normal_values(rng, shape, spread, limit, pieces=(), dtype=jnp.bfloat16):
    entries = spread * jax.random.normal(rng, shape, jnp.float32)
    if pieces:
        entries = entries * shard_levels(rng, shape, pieces, -0.22, 0.18)
    return jnp.clip(entries, -limit, limit).astype(dtype)


def setup_inputs(seed: int = 0, part: int = 0) -> dict:
    key_of = jax.random.split(jax.random.key(seed), 9)
    own_keys = jax.random.split(jax.random.fold_in(key_of[8], part), 9)
    return {
        "earlier_heat_level": jnp.clip(2.0 * jax.random.uniform(own_keys[0], (HEAT_GRID_DEPTH, HEAT_GRID_HEIGHT, HEAT_GRID_WIDTH), jnp.float32) ** shard_levels(own_keys[0], (HEAT_GRID_DEPTH, HEAT_GRID_HEIGHT, HEAT_GRID_WIDTH), ((1, 4), (2, 4)), -0.2, 0.2), 0.0, 2.0),
        "substance_per_heat_node": plant(jax.random.randint(own_keys[1], (HEAT_GRID_DEPTH, HEAT_GRID_HEIGHT, HEAT_GRID_WIDTH), 0, NMAT), jax.random.fold_in(own_keys[1], 1), 0, NMAT - 1).astype(jnp.int32),
        "die_heating_source": jnp.clip(jnp.exp(math.log(5.0) - 3.218876 * jax.random.uniform(own_keys[2], (HEAT_GRID_HEIGHT, HEAT_GRID_WIDTH), jnp.float32) ** shard_levels(own_keys[2], (HEAT_GRID_HEIGHT, HEAT_GRID_WIDTH), ((0, 4), (1, 4)), -0.2, 0.2)), 0.2, 5.0),
        "substance_per_solid_element": plant(jax.random.randint(own_keys[3], (ML, MX, MY), 0, NMAT), jax.random.fold_in(own_keys[3], 1), 0, NMAT - 1).astype(jnp.int32),
        "earlier_solid_offset": normal_values(own_keys[4], (3, ML, MX, MY), 0.3, 2.5, ((2, 8), (3, 2)), jnp.float32),
        "heat_transfer_per_substance": jnp.clip(jnp.exp(jax.random.uniform(key_of[5], (NMAT,), jnp.float32, math.log(0.5), math.log(8.0))), 0.5, 8.0),
        "growth_rate_per_substance": jnp.clip(jnp.exp(jax.random.uniform(key_of[6], (NMAT,), jnp.float32, math.log(0.2), math.log(2.0))), 0.2, 2.0),
        "elastic_modulus_per_substance": jnp.clip(jnp.exp(jax.random.uniform(key_of[7], (NMAT,), jnp.float32, math.log(0.5), math.log(5.0))), 0.5, 5.0),
    }


STIFF_DIAG = 12.0
LOWER_BOUND = 0.25
UPPER_BOUND = 1.75

def lookup(material, table):
    result = jnp.zeros(material.shape, jnp.float32)
    for m in range(table.shape[0]):
        result = jnp.where(material == m, table[m], result)
    return result

def smoothing_update(widened_heat_level, widened_heat_transfer, forcing_term, cooling_boundary):
    rows = widened_heat_level.shape[1] - 2
    cols = widened_heat_level.shape[2] - 2
    k_mid = widened_heat_transfer[:, 1:1 + rows, 1:1 + cols]
    numerator = forcing_term
    denominator = cooling_boundary + jnp.zeros_like(k_mid)
    for row_off, col_off in ((2, 1), (0, 1), (1, 2), (1, 0)):
        conduct = jnp.sqrt(k_mid * widened_heat_transfer[:, row_off:row_off + rows, col_off:col_off + cols])
        numerator = numerator + conduct * widened_heat_level[:, row_off:row_off + rows, col_off:col_off + cols]
        denominator = denominator + conduct
    t_mid = widened_heat_level[:, 1:1 + rows, 1:1 + cols]
    k_pad = jnp.pad(k_mid, ((1, 1), (0, 0), (0, 0)))
    t_pad = jnp.pad(t_mid, ((1, 1), (0, 0), (0, 0)))
    depth = k_mid.shape[0]
    for layer_off in (2, 0):
        conduct = jnp.sqrt(k_mid * k_pad[layer_off:layer_off + depth])
        numerator = numerator + conduct * t_pad[layer_off:layer_off + depth]
        denominator = denominator + conduct
    return numerator / denominator

def shifted(padded, axis_id, offset):
    selector = [slice(None)] * (padded.ndim - 3)
    for grid_dim in range(3):
        extent = padded.shape[padded.ndim - 3 + grid_dim] - 2
        start_at = 1 + offset if grid_dim == axis_id else 1
        selector.append(slice(start_at, start_at + extent))
    return padded[tuple(selector)]

def block_coef(d, i, j):
    if i == j:
        return 1.0 if i == d else 0.5
    if (i == d) != (j == d):
        return 0.25
    return 0.0

def load_force(s_pad):
    return jnp.stack([0.5 * (shifted(s_pad, d, 1) - shifted(s_pad, d, -1)) for d in range(3)])

def apply_stiff(v_pad, e_pad):
    e_mid = shifted(e_pad, 0, 0)
    outputs = [STIFF_DIAG * e_mid * shifted(v_pad[i], 0, 0) for i in range(3)]
    for d in range(3):
        for offset in (1, -1):
            couple = jnp.sqrt(e_mid * shifted(e_pad, d, offset))
            near = [shifted(v_pad[j], d, offset) for j in range(3)]
            for i in range(3):
                mixed = jnp.zeros_like(e_mid)
                for j in range(3):
                    weight = block_coef(d, i, j)
                    if weight != 0.0:
                        mixed = mixed + weight * near[j]
                outputs[i] = outputs[i] - couple * mixed
    return jnp.stack(outputs)

def divergence(u_pad):
    total = jnp.zeros_like(shifted(u_pad[0], 0, 0))
    for d in range(3):
        total = total + (shifted(u_pad[d], d, 1) - shifted(u_pad[d], d, -1))
    return 0.5 * total

def chebyshev(start, resid, diagonal, apply_fn, sweeps):
    theta = 0.5 * (UPPER_BOUND + LOWER_BOUND)
    delta = 0.5 * (UPPER_BOUND - LOWER_BOUND)
    sigma = theta / delta
    rho_now = 1.0 / sigma
    direction = resid / diagonal / theta
    shifted_copy = start
    for sweep in range(sweeps):
        shifted_copy = shifted_copy + direction
        if sweep < sweeps - 1:
            resid = resid - apply_fn(direction)
            rho_next = 1.0 / (2.0 * sigma - rho_now)
            direction = rho_next * rho_now * direction + 2.0 * rho_next / delta * (resid / diagonal)
            rho_now = rho_next
    return shifted_copy

def reference(earlier_heat_level, substance_per_heat_node, die_heating_source, substance_per_solid_element, earlier_solid_offset, heat_transfer_per_substance, growth_rate_per_substance, elastic_modulus_per_substance):
    layer = jnp.arange(HEAT_GRID_DEPTH).reshape(HEAT_GRID_DEPTH, 1, 1)
    cooling_boundary = jnp.where(layer == HEAT_GRID_DEPTH - 1, 2.0, 0.2).astype(jnp.float32)
    forcing_term = jnp.where(layer == 0, die_heating_source[None], 0.0).astype(jnp.float32)
    local_heat_transfer = lookup(substance_per_heat_node, heat_transfer_per_substance)
    linear_growth_rate = lookup(substance_per_heat_node, growth_rate_per_substance)
    bordered_plane = ((0, 0), (1, 1), (1, 1))
    widened_heat_transfer = jnp.pad(local_heat_transfer, bordered_plane)
    present_heat_level = earlier_heat_level
    for sweep in range(THERMAL_SWEEPS):
        present_heat_level = smoothing_update(jnp.pad(present_heat_level, bordered_plane), widened_heat_transfer, forcing_term, cooling_boundary)
    heating_strain = (linear_growth_rate * present_heat_level).reshape(HEAT_GRID_DEPTH, HEAT_GRID_HEIGHT // 3, 3, HEAT_GRID_WIDTH // 3, 3).sum(axis=(2, 4)) / 9.0
    layer_map = np.arange(ML) * HEAT_GRID_DEPTH // ML
    strain_mech = heating_strain[layer_map]
    modulus = lookup(substance_per_solid_element, elastic_modulus_per_substance)
    grid_pad = ((1, 1), (1, 1), (1, 1))
    field_pad = ((0, 0), (1, 1), (1, 1), (1, 1))
    e_pad = jnp.pad(modulus, grid_pad)
    force = load_force(jnp.pad(modulus * strain_mech, grid_pad))
    diagonal = STIFF_DIAG * modulus

    def apply_fn(field):
        return apply_stiff(jnp.pad(field, field_pad), e_pad)
    resid = force - apply_fn(earlier_solid_offset)
    shifted_copy = chebyshev(earlier_solid_offset, resid, diagonal, apply_fn, MECH_SWEEPS)
    stress = modulus * (divergence(jnp.pad(shifted_copy, field_pad)) - 3.0 * strain_mech)
    weights = ((ML - jnp.arange(ML)).astype(jnp.float32) / (ML * (ML + 1) / 2.0)).reshape(ML, 1, 1)
    die_stress = lax.optimization_barrier(jnp.sum(weights * stress, axis=0))
    diffusion_update = jnp.repeat(jnp.repeat(die_stress, 3, axis=0), 3, axis=1)
    slowdown_factor = 1.0 + 0.2 * present_heat_level[0] + 0.5 * diffusion_update
    return (present_heat_level, shifted_copy, slowdown_factor)
```

```python
import functools

import jax
import jax.numpy as jnp
from jax import lax
from jax.experimental import pallas as pl
from jax.experimental.pallas import tpu as pltpu
from jax.sharding import PartitionSpec as P

DEPTH = 8
ML = 6
LANES = 128
HALO = 11
MHALO = 3

STIFF_DIAG = 12.0
THETA = 1.0
DELTA = 0.75
SIGMA = THETA / DELTA
RHO0 = 1.0 / SIGMA
RHO1 = 1.0 / (2.0 * SIGMA - RHO0)

VMEM = pl.BlockSpec(memory_space=pltpu.VMEM)
SMEM = pl.BlockSpec(memory_space=pltpu.SMEM)


def call(kernel, outs, args, scratch=(), smem=0):
    return pl.pallas_call(
        kernel,
        out_shape=[jax.ShapeDtypeStruct(s, jnp.float32) for s in outs],
        in_specs=[SMEM] * smem + [VMEM] * (len(args) - smem),
        out_specs=[VMEM] * len(outs),
        scratch_shapes=[pltpu.VMEM(s, jnp.float32) for s in scratch],
        compiler_params=pltpu.CompilerParams(vmem_limit_bytes=16 * 1024 * 1024),
    )(*args)


def lane_iota(rows=8):
    return lax.broadcasted_iota(jnp.int32, (rows, LANES), 1)


def sub_iota(width):
    return lax.broadcasted_iota(jnp.int32, (8, width), 0)


def tiles(x):
    return [x[:, LANES * t : LANES * (t + 1)] for t in range(x.shape[1] // LANES)]


def gather_lanes(table, index):
    return jnp.take_along_axis(table, index, axis=1, mode="promise_in_bounds")


def lookup(table, code):
    return jnp.concatenate([gather_lanes(table, c.astype(jnp.int32)) for c in tiles(code)], axis=1)


def prev_lane(x):
    return pltpu.roll(x, 1, 1)


def next_lane(x):
    return pltpu.roll(x, x.shape[1] - 1, 1)


def prev_sub(x):
    return pltpu.roll(x, 1, 0)


def next_sub(x):
    return pltpu.roll(x, 7, 0)


def row8(ref, i):
    return ref[8 * i : 8 * i + 8, :]


def k_rows(t_ref, id_ref, src_ref, u_ref, mat_ref, a_ref, m_ref):
    rows = t_ref.shape[1]
    for t in range(t_ref.shape[2] // LANES):
        at = 17 * rows * t
        lanes = slice(LANES * t, LANES * (t + 1))
        for l in range(DEPTH):
            a_ref[pl.ds(at + l, rows, stride=16), :] = t_ref[l, :, lanes]
            a_ref[pl.ds(at + 8 + l, rows, stride=16), :] = (id_ref[l, :, lanes] + 1).astype(jnp.float32)
        a_ref[at + 16 * rows : at + 17 * rows, :] = src_ref[:, lanes]
    mrows = mat_ref.shape[1]
    m_ref[...] = jnp.zeros(m_ref.shape, jnp.float32)
    for t in range(mat_ref.shape[2] // LANES):
        at = 32 * mrows * t
        lanes = slice(LANES * t, LANES * (t + 1))
        for l in range(ML):
            for f in range(3):
                m_ref[pl.ds(at + 8 * f + l, mrows, stride=32), :] = u_ref[f, l, :, lanes]
            m_ref[pl.ds(at + 24 + l, mrows, stride=32), :] = (mat_ref[l, :, lanes] + 1).astype(jnp.float32)


def k_chip(n_edges, rows, flags, a_ref, b_ref, m_ref, n_ref, z_ref, w_ref, src_ref, mw_ref, *edge_refs):
    n_t = a_ref.shape[0] // (17 * rows)
    half = LANES * n_t
    mcols = mw_ref.shape[1]
    m_t = mcols // LANES
    mrows = m_ref.shape[0] // (32 * m_t)

    def build(left, right, rev):
        for t in range(2 * n_t):
            part = left if t < n_t else right
            base = 17 * rows * (t % n_t)
            lanes = slice(LANES * t, LANES * (t + 1))
            for g in range(rows - 1):
                i = base + 16 * (rows - 1 - g if rev else g)
                dst, at = (z_ref, 16 * g) if g < HALO else (w_ref, 16 * (g - HALO))
                dst[at : at + 16, lanes] = part[i : i + 16, :]
            for g in range(rows):
                i = base + 16 * rows + (rows - 1 - g if rev else g)
                src_ref[g : g + 1, lanes] = part[i : i + 1, :]
        for t in range(m_t):
            lanes = slice(LANES * t, LANES * (t + 1))
            for g in range(mrows + MHALO):
                if g < mrows:
                    i = mrows - 1 - g if rev else g
                    part = m_ref
                else:
                    i = 2 * mrows - 1 - g if rev else g - mrows
                    part = n_ref
                i = 32 * (mrows * t + i)
                mw_ref[32 * g : 32 * g + 32, lanes] = part[i : i + 32, :]

    @pl.when(flags[0] == 0)
    def _():
        build(a_ref, b_ref, False)

    @pl.when(flags[0] != 0)
    def _():
        build(b_ref, a_ref, True)

    for g in range(MHALO):
        z_ref[16 * HALO : 16 * HALO + 32, mcols * g : mcols * (g + 1)] = mw_ref[32 * g : 32 * g + 32, :]
    z_ref[16 * HALO + 32 : 16 * HALO + 48, :] = src_ref[0:16, :]

    lane = lane_iota()
    near = (lane < HALO) | (lane >= LANES - HALO)
    groups = [((lane - 32 * f + MHALO) & (LANES - 1)) < 2 * MHALO for f in range(4)]
    for e in range(n_edges):
        c_ref, d_ref = edge_refs[2 * e], edge_refs[2 * e + 1]
        right_edge = flags[1 + e]
        start = pl.multiple_of(right_edge * (2 * half - LANES), LANES)
        mstart = pl.multiple_of(right_edge * (mcols - LANES), LANES)
        lanes = pl.ds(start, LANES)
        mlanes = pl.ds(mstart, LANES)
        for g in range(rows - 1):
            src, at = (z_ref, 16 * g) if g < HALO else (w_ref, 16 * (g - HALO))
            t = src[at : at + 8, lanes]
            code = src[at + 8 : at + 16, lanes]
            merged = jnp.where(near, t, pltpu.roll(code, 64, 1))
            c_ref[8 * g : 8 * g + 8, :] = merged
            if g < HALO:
                d_ref[8 * g : 8 * g + 8, :] = merged
        at = 8 * (rows - 1)
        c_ref[at : at + rows, :] = src_ref[:, lanes]
        d_ref[8 * HALO : 8 * HALO + 16, :] = src_ref[0:16, lanes]
        for g in range(mrows + MHALO):
            merged = jnp.zeros((8, LANES), jnp.float32)
            for f in range(4):
                field = mw_ref[32 * g + 8 * f : 32 * g + 8 * f + 8, mlanes]
                merged = jnp.where(groups[f], pltpu.roll(field, 32 * f, 1) if f else field, merged)
            c_ref[at + rows + 8 * g : at + rows + 8 * g + 8, :] = merged
            if g < MHALO:
                d_ref[8 * HALO + 16 + 8 * g : 8 * HALO + 24 + 8 * g, :] = merged


class Sides:
    def __init__(self, flags, from_left, from_right):
        self.left = from_left
        self.right = from_right
        lane = lane_iota()
        has_left = flags[3] != 0
        has_right = flags[4] != 0
        self.masks = {
            w: ((lane < w) & has_right, (lane >= LANES - w) & has_left) for w in (HALO, MHALO)
        }

    def tile(self, at, count, width, turn=0):
        right_mask, left_mask = (m[:count] for m in self.masks[width])
        r = self.right[at : at + count, :]
        l = r if self.left is self.right else self.left[at : at + count, :]
        if turn:
            r = pltpu.roll(r, turn, 1)
            l = r if self.left is self.right else pltpu.roll(l, turn, 1)
        return jnp.where(right_mask, r, jnp.where(left_mask, l, 0.0))


def conduct_sum(ref, i, below, above):
    x = row8(ref, i)
    width = x.shape[1]
    sub = sub_iota(width)
    total = row8(ref, below) + row8(ref, above) + prev_lane(x) + next_lane(x)
    total = total + jnp.where(sub < DEPTH - 1, next_sub(x), 0.0)
    return total + jnp.where(sub > 0, prev_sub(x), 0.0)


def sink(width):
    return jnp.where(sub_iota(width) == DEPTH - 1, 2.0, 0.2).astype(jnp.float32)


def restrict_columns(x):
    width = x.shape[1]
    x = x + pltpu.roll(x, width - 1, 1) + pltpu.roll(x, width - 2, 1)
    pieces = tiles(x)
    lane = lane_iota()
    out = []
    for j in range((len(pieces) - 1) // 3):
        got = None
        for t in range(3):
            g = gather_lanes(pieces[3 * j + t], (3 * lane) & (LANES - 1))
            got = g if got is None else jnp.where((3 * lane) >= LANES * t, g, got)
        out.append(got)
    first = LANES - MHALO
    index = jnp.where(lane < MHALO, 3 * lane, jnp.where(lane >= first, LANES - 9 + 3 * (lane - first), 64))
    out.append(gather_lanes(pieces[-1], index))
    y = jnp.concatenate(out, axis=1)
    y = jnp.where(sub_iota(y.shape[1]) < 3, y, next_sub(y))
    return y * (1.0 / 9.0)


def k_inner(n_sides, rows, flags, tab, z_ref, w_ref, src_ref, *refs):
    sides = Sides(flags, refs[0], refs[n_sides - 1])
    s_ref, al_ref, q0_ref, q1_ref, di_ref, t_ref, ea_ref, strain_ref = refs[n_sides:]
    own = rows - 1
    wide = src_ref.shape[1]
    width = wide + LANES
    t_s = jnp.sqrt(tab[0:8, :])
    t_al = tab[8:16, :]
    for g in range(own):
        src, at = (z_ref, 16 * g) if g < HALO else (w_ref, 16 * (g - HALO))
        temp = jnp.concatenate([src[at : at + 8, :], sides.tile(8 * g, 8, HALO)], axis=1)
        code = jnp.concatenate([src[at + 8 : at + 16, :], sides.tile(8 * g, 8, HALO, 64)], axis=1)
        s = lookup(t_s, code)
        s_ref[8 * g : 8 * g + 8, :] = s
        al_ref[8 * g : 8 * g + 8, :] = lookup(t_al, code)
        q0_ref[8 * g : 8 * g + 8, :] = s * temp
    top = sub_iota(width) == 0
    h = sink(width)
    for g in range(1, own - 1):
        s = row8(s_ref, g)
        inv = 1.0 / (h + s * conduct_sum(s_ref, g, g - 1, g + 1))
        di_ref[8 * g : 8 * g + 8, :] = inv
        power = jnp.concatenate([src_ref[g : g + 1, :], sides.tile(8 * own + g, 1, HALO)], axis=1)
        power = jnp.where(top, jnp.broadcast_to(power, (8, width)), 0.0)
        t1 = (power + s * conduct_sum(q0_ref, g, g - 1, g + 1)) * inv
        q1_ref[8 * g : 8 * g + 8, :] = s * t1
    for g in range(2, own - 2):
        power = jnp.concatenate([src_ref[g : g + 1, :], sides.tile(8 * own + g, 1, HALO)], axis=1)
        power = jnp.where(top, jnp.broadcast_to(power, (8, width)), 0.0)
        t2 = (power + row8(s_ref, g) * conduct_sum(q1_ref, g, g - 1, g + 1)) * row8(di_ref, g)
        t_ref[8 * g : 8 * g + 8, :] = t2
        ea_ref[8 * g : 8 * g + 8, :] = row8(al_ref, g) * t2
    for m in range(1, (own - 2) // 3):
        x = row8(ea_ref, 3 * m) + row8(ea_ref, 3 * m + 1) + row8(ea_ref, 3 * m + 2)
        strain_ref[8 * m : 8 * m + 8, :] = restrict_columns(x)


def couple_sum(rows3):
    near = [[None] * 3 for _ in range(3)]
    for j in range(3):
        below, mid, above = rows3[j]
        near[0][j] = next_sub(mid) + prev_sub(mid)
        near[1][j] = above + below
        near[2][j] = next_lane(mid) + prev_lane(mid)
    out = []
    for i in range(3):
        j, k = [x for x in range(3) if x != i]
        main = near[i][i] + 0.5 * (near[j][i] + near[k][i])
        side = (near[i][j] + near[j][j]) + (near[i][k] + near[k][k])
        out.append(main + 0.25 * side)
    return out


def k_outer(n_sides, rows, flags, tab, zr_ref, mw_ref, *refs):
    sides = Sides(flags, refs[0], refs[n_sides - 1])
    corners = Sides(flags, refs[n_sides], refs[2 * n_sides - 1])
    rest = refs[2 * n_sides :]
    s_in, al_in, q0_in, q1_in, di_in, t_in, ea_in, strain_in, src_ref = rest[:9]
    x_ref, keep_ref, u_ref = rest[9:12]
    s_ref, q0_ref, q1_ref, di_ref, al_ref, ea_ref, st_ref = rest[12:19]
    ms_ref, mi_ref, mod_ref, sf_ref = rest[19:23]
    uu_refs = rest[23:26]
    p_refs = rest[26:29]
    d_refs = rest[29:32]
    own = rows - 1
    wide = zr_ref.shape[1]
    half = wide // 2
    width = wide + LANES
    t_s = jnp.sqrt(tab[0:8, :])
    t_al = tab[8:16, :]
    zsrc = 16 * HALO + 32
    for j in range(HALO):
        i = HALO - 1 - j
        temp = jnp.concatenate([zr_ref[16 * j : 16 * j + 8, :], corners.tile(8 * j, 8, HALO)], axis=1)
        code = jnp.concatenate([zr_ref[16 * j + 8 : 16 * j + 16, :], corners.tile(8 * j, 8, HALO, 64)], axis=1)
        s = lookup(t_s, code)
        s_ref[8 * i : 8 * i + 8, :] = s
        al_ref[8 * i : 8 * i + 8, :] = lookup(t_al, code)
        q0_ref[8 * i : 8 * i + 8, :] = s * temp
    for g in range(3):
        i = 8 * (HALO + g)
        s_ref[i : i + 8, :] = row8(s_in, g)
        al_ref[i : i + 8, :] = row8(al_in, g)
        q0_ref[i : i + 8, :] = row8(q0_in, g)
        if g > 0:
            q1_ref[i : i + 8, :] = row8(q1_in, g)
            di_ref[i : i + 8, :] = row8(di_in, g)
    top = sub_iota(width) == 0
    h = sink(width)

    def power_of(g):
        if g < 0:
            j = -1 - g
            p = [zr_ref[zsrc + j : zsrc + j + 1, :], corners.tile(8 * HALO + j, 1, HALO)]
        else:
            p = [src_ref[g : g + 1, :], sides.tile(8 * own + g, 1, HALO)]
        p = jnp.concatenate(p, axis=1)
        return jnp.where(top, jnp.broadcast_to(p, (8, width)), 0.0)

    for g in range(1 - HALO, 1):
        i = HALO + g
        s = row8(s_ref, i)
        inv = 1.0 / (h + s * conduct_sum(s_ref, i, i - 1, i + 1))
        di_ref[8 * i : 8 * i + 8, :] = inv
        t1 = (power_of(g) + s * conduct_sum(q0_ref, i, i - 1, i + 1)) * inv
        q1_ref[8 * i : 8 * i + 8, :] = s * t1
    ea_ref[8 * (HALO + 2) : 8 * (HALO + 3), :] = row8(ea_in, 2)

    core = flags[0]

    def other_half(x):
        return jnp.where(core == 0, x[:, half:wide], x[:, 0:half])

    def own_half(x):
        return jnp.where(core == 0, x[:, 0:half], x[:, half:wide])

    for g in range(2 - HALO, 2):
        i = HALO + g
        t2 = (power_of(g) + row8(s_ref, i) * conduct_sum(q1_ref, i, i - 1, i + 1)) * row8(di_ref, i)
        ea_ref[8 * i : 8 * i + 8, :] = row8(al_ref, i) * t2
        if g >= 0:
            keep_ref[8 * g : 8 * g + 8, :] = own_half(t2)
            x_ref[8 * g : 8 * g + 8, :] = other_half(t2)
    x_ref[16:24, :] = other_half(row8(t_in, 2))

    mrows = mw_ref.shape[0] // 32 - MHALO
    mcols = mw_ref.shape[1]
    mwidth = mcols + LANES
    n_m = mrows + 2 * MHALO
    for m in range(MHALO + 1):
        i = 3 * m + 2
        x = row8(ea_ref, i) + row8(ea_ref, i + 1) + row8(ea_ref, i + 2)
        st_ref[8 * m : 8 * m + 8, :] = restrict_columns(x)
    for m in range(1, mrows + MHALO):
        i = MHALO + m
        st_ref[8 * i : 8 * i + 8, :] = row8(strain_in, m)
    t_mod = tab[16:24, :]
    t_m = jnp.sqrt(t_mod)
    t_mi = jnp.where(t_mod > 0.0, 1.0 / jnp.where(t_mod > 0.0, t_m, 1.0), 0.0)
    at_own = 8 * own + rows
    at_corner = 8 * HALO + 16
    for i in range(n_m):
        m = i - MHALO
        fields = []
        for f in range(4):
            turn = (LANES - 32 * f) % LANES
            if m < 0:
                j = -1 - m
                body = zr_ref[16 * HALO + 8 * f : 16 * HALO + 8 * f + 8, mcols * j : mcols * (j + 1)]
                side = corners.tile(at_corner + 8 * j, 8, MHALO, turn)
            else:
                body = mw_ref[32 * m + 8 * f : 32 * m + 8 * f + 8, :]
                side = sides.tile(at_own + 8 * m, 8, MHALO, turn)
            fields.append(jnp.concatenate([body, side], axis=1))
        at = slice(8 * i, 8 * i + 8)
        code = fields[3]
        root = lookup(t_m, code)
        mod = lookup(t_mod, code)
        ms_ref[at, :] = root
        mi_ref[at, :] = lookup(t_mi, code)
        mod_ref[at, :] = mod
        sf_ref[at, :] = mod * row8(st_ref, i)
        for f in range(3):
            uu_refs[f][at, :] = root * fields[f]
    sign = jnp.where(core == 0, 0.5, -0.5).astype(jnp.float32)
    for i in range(1, n_m - 1):
        at = slice(8 * i, 8 * i + 8)
        load = row8(sf_ref, i)
        force = [
            0.5 * (next_sub(load) - prev_sub(load)),
            sign * (row8(sf_ref, i + 1) - row8(sf_ref, i - 1)),
            0.5 * (next_lane(load) - prev_lane(load)),
        ]
        near = couple_sum([[row8(r, i - 1), row8(r, i), row8(r, i + 1)] for r in uu_refs])
        inv = row8(mi_ref, i)
        for d in range(3):
            p = (force[d] * inv + near[d]) * (1.0 / STIFF_DIAG) - row8(uu_refs[d], i)
            p_refs[d][at, :] = jnp.where(inv > 0.0, p, 0.0)
    c_near = 2.0 * RHO1 / DELTA / STIFF_DIAG
    c_self = 1.0 + RHO1 * RHO0
    for i in range(2, n_m - 2):
        at = slice(8 * i, 8 * i + 8)
        near = couple_sum([[row8(r, i - 1), row8(r, i), row8(r, i + 1)] for r in p_refs])
        inv = row8(mi_ref, i)
        for d in range(3):
            moved = row8(uu_refs[d], i) + c_self * row8(p_refs[d], i) + c_near * near[d]
            d_refs[d][at, :] = moved * inv
    sub = sub_iota(mwidth)
    weight = jnp.where(sub < ML, (ML - sub).astype(jnp.float32) * (1.0 / (ML * (ML + 1) / 2.0)), 0.0)
    x_ref[24:32, :] = jnp.zeros((8, x_ref.shape[1]), jnp.float32)
    for g in range(mrows):
        i = MHALO + g
        u0, u2 = row8(d_refs[0], i), row8(d_refs[2], i)
        div = 0.5 * (next_sub(u0) - prev_sub(u0)) + 0.5 * (next_lane(u2) - prev_lane(u2))
        div = div + sign * (row8(d_refs[1], i + 1) - row8(d_refs[1], i - 1))
        stress = row8(mod_ref, i) * (div - 3.0 * row8(st_ref, i))
        die = jnp.sum(weight * stress, axis=0, keepdims=True)
        first, second = die[:, 0:LANES], die[:, LANES : 2 * LANES]
        keep_ref[16 + g : 17 + g, 0:LANES] = jnp.where(core == 0, first, second)
        x_ref[24 + g : 25 + g, 0:LANES] = jnp.where(core == 0, second, first)
        for d in range(3):
            u_ref[8 * (mrows * d + g) : 8 * (mrows * d + g) + 8, :] = row8(d_refs[d], i)[:, 0:mcols]


def k_out(rows, mrows, flags, t_in, keep_ref, xr_ref, u_in, t_out, u_out, slow_ref, buf, die, wide_die, ubuf):
    half = slow_ref.shape[1]
    mcols = u_in.shape[1]
    core = flags[0]

    def put(ref, at, x):
        count = ref.shape[0] * LANES // x.shape[1]
        for t, piece in enumerate(tiles(x)):
            ref[count * t + at : count * t + at + piece.shape[0], :] = piece

    def build(rev):
        lo = half if rev else 0
        for g in range(rows):
            i = rows - 1 - g if rev else g
            if g < 2:
                x = keep_ref[8 * g : 8 * g + 8, :]
            elif g < rows - 3:
                x = t_in[8 * g : 8 * g + 8, lo : lo + half]
            else:
                k = rows - 1 - g
                x = xr_ref[8 * k : 8 * k + 8, :]
            put(buf, 8 * i, x)
        for g in range(mrows):
            mine = 2 * mrows - 1 - g if rev else g
            theirs = g if rev else 2 * mrows - 1 - g
            die[mine : mine + 1, :] = keep_ref[16 + g : 17 + g, 0:LANES]
            die[theirs : theirs + 1, :] = xr_ref[24 + g : 25 + g, 0:LANES]
            for d in range(3):
                i = mrows - 1 - g if rev else g
                put(ubuf, 8 * (mrows * d + i), row8(u_in, mrows * d + g))

    @pl.when(core == 0)
    def _():
        build(False)

    @pl.when(core != 0)
    def _():
        build(True)

    for t in range(half // LANES):
        at = 8 * rows * t
        lanes = slice(LANES * t, LANES * (t + 1))
        for l in range(DEPTH):
            t_out[l, :, lanes] = buf[pl.ds(at + l, rows, stride=8), :]
    for t in range(mcols // LANES):
        lanes = slice(LANES * t, LANES * (t + 1))
        for d in range(3):
            for l in range(ML):
                u_out[d, l, :, lanes] = ubuf[pl.ds(8 * mrows * (3 * t + d) + l, mrows, stride=8), :]
    lane = lane_iota(2 * mrows)
    for t in range(half // LANES):
        x = gather_lanes(die[...], (lane + LANES * t) // 3)
        for b in range(3):
            wide_die[pl.ds(b, 2 * mrows, stride=3), :] = x
        lanes = slice(LANES * t, LANES * (t + 1))
        slow_ref[:, lanes] = 1.0 + 0.2 * buf[pl.ds(8 * rows * t, rows, stride=8), :] + 0.5 * wide_die[...]


def pairs(dims, sends):
    index = {}
    for r in range(dims[0]):
        for c in range(dims[1]):
            for a in range(dims[2]):
                index[(r, c, a)] = (r * dims[1] + c) * dims[2] + a
    out = []
    for source in index:
        target = sends(*source)
        if target in index:
            out.append((index[source], index[target]))
    return out


def per_device(temp, ids, power, mat, offset, heat_table, growth_table, modulus_table):
    axes = ("row", "col", "lay")
    dims = tuple(lax.axis_size(x) for x in axes)
    n_col = dims[1]
    depth, rows, half = temp.shape
    _, _, mrows, mcols = offset.shape
    a = lax.axis_index("lay")
    c = lax.axis_index("col")
    n_edges = 1 if n_col == 2 else 2
    first_edge = jnp.where(c == 0, 1, 0) if n_col == 2 else jnp.int32(1)
    flags = jnp.stack([a, first_edge, jnp.int32(0), c > 0, c < n_col - 1]).astype(jnp.int32)
    tab = jnp.stack([heat_table, growth_table, modulus_table])
    tab = jnp.pad(tab, ((0, 0), (1, LANES - 1 - tab.shape[1])))
    tab = jnp.broadcast_to(tab[:, None, :], (3, 8, LANES)).reshape(24, LANES)

    def send(x, sends):
        return lax.ppermute(x, axes, pairs(dims, sends))

    def swap(r, c, a):
        return (r, c, 1 - a)

    def along(r, c, a):
        return (r + 1, c, 0) if a == 1 else (r - 1, c, 1)

    mine, mech = call(k_rows, [(17 * rows * half // LANES, LANES), (32 * mrows * mcols // LANES, LANES)], [temp, ids, power, offset, mat])
    theirs = send(mine, swap)
    mech2 = send(mech, swap)
    wide = 2 * half
    own = rows - 1
    n_c = 8 * own + rows + 8 * (mrows + MHALO)
    n_d = 8 * HALO + 16 + 8 * MHALO
    z, w, src, mw, *edges = call(
        functools.partial(k_chip, n_edges, rows),
        [(16 * HALO + 48, wide), (16 * (own - HALO), wide), (rows, wide), (32 * (mrows + MHALO), mcols)]
        + [(n_c, LANES), (n_d, LANES)] * n_edges,
        [flags, mine, theirs, mech, mech2],
        smem=1,
    )
    zr = send(z, along)
    if n_edges == 1:
        sides = [send(edges[0], lambda r, c, a: (r, 1 - c, a))]
        corners = [send(edges[1], lambda r, c, a: along(r, 1 - c, a))]
    else:
        sides = [send(edges[0], lambda r, c, a: (r, c + 1, a)), send(edges[2], lambda r, c, a: (r, c - 1, a))]
        corners = [
            send(edges[1], lambda r, c, a: along(r, c + 1, a)),
            send(edges[3], lambda r, c, a: along(r, c - 1, a)),
        ]
    width = wide + LANES
    mwidth = mcols + LANES
    inner = call(
        functools.partial(k_inner, n_edges, rows),
        [(8 * own, width)] * 7 + [(8 * (mrows + MHALO), mwidth)],
        [flags, tab, z, w, src] + sides,
        smem=1,
    )
    t2 = inner[5]
    n_h = 8 * (HALO + 3)
    n_m = 8 * (mrows + 2 * MHALO)
    x, keep, u = call(
        functools.partial(k_outer, n_edges, rows),
        [(32, half), (24, half), (24 * mrows, mcols)],
        [flags, tab, zr, mw] + sides + corners + list(inner) + [src],
        scratch=[(n_h, width)] * 6 + [(n_m, mwidth)] * 14,
        smem=1,
    )
    xr = send(x, swap)
    t_out, u_out, slow = call(
        functools.partial(k_out, rows, mrows),
        [temp.shape, offset.shape, power.shape],
        [flags, t2, keep, xr, u],
        scratch=[
            (8 * rows * half // LANES, LANES),
            (2 * mrows, LANES),
            (rows, LANES),
            (24 * mrows * mcols // LANES, LANES),
        ],
        smem=1,
    )
    return t_out, u_out, slow


def solution(mesh):
    placed = (
        P("grp", "row", ("col", "lay")),
        P("grp", "row", ("col", "lay")),
        P(("grp", "row"), ("col", "lay")),
        P("grp", ("row", "lay"), "col"),
        P(None, "grp", ("row", "lay"), "col"),
        P(),
        P(),
        P(),
    )
    return jax.shard_map(
        per_device,
        mesh=mesh,
        in_specs=placed,
        out_specs=(
            P("grp", "row", ("col", "lay")),
            P(None, "grp", ("row", "lay"), "col"),
            P(("grp", "row"), ("col", "lay")),
        ),
        check_vma=False,
    )
```

```python
import functools

import jax
import jax.numpy as jnp
from jax import lax
from jax.experimental import pallas as pl
from jax.experimental.pallas import tpu as pltpu
from jax.sharding import PartitionSpec as P

DEPTH = 8
ML = 6
LANES = 128
HALO = 11
MHALO = 3

STIFF_DIAG = 12.0
THETA = 1.0
DELTA = 0.75
SIGMA = THETA / DELTA
RHO0 = 1.0 / SIGMA
RHO1 = 1.0 / (2.0 * SIGMA - RHO0)

VMEM = pl.BlockSpec(memory_space=pltpu.VMEM)
FRONT = 9
AHEAD = 5
STEP = 3
SPAN = 16
MSPAN = 8
ZMECH = 4 * ML
CORE = "lay"
UNROLL_STRAIN = 3


def call(kernel, outs, args, scratch=(), specs=None):
    return pl.pallas_call(
        kernel,
        out_shape=[jax.ShapeDtypeStruct(s, jnp.float32) for s in outs],
        in_specs=specs or [VMEM] * len(args),
        out_specs=[VMEM] * len(outs),
        scratch_shapes=[pltpu.VMEM(s, jnp.float32) if isinstance(s, tuple) else s for s in scratch],
        compiler_params=pltpu.CompilerParams(vmem_limit_bytes=16 * 1024 * 1024),
    )(*args)


def lane_iota(rows=8):
    return lax.broadcasted_iota(jnp.int32, (rows, LANES), 1)


def sub_iota(width):
    return lax.broadcasted_iota(jnp.int32, (8, width), 0)


def tile_lanes(t):
    return slice(LANES * t, LANES * (t + 1))


def tiles(x):
    return [x[:, tile_lanes(t)] for t in range(x.shape[1] // LANES)]


def table_of(ref, k):
    return jnp.broadcast_to(ref[k : k + 1, :], (8, LANES))


def gather_lanes(table, index):
    return jnp.take_along_axis(table, index, axis=1, mode="promise_in_bounds")


def lookup(table, code):
    return jnp.concatenate([gather_lanes(table, c.astype(jnp.int32)) for c in tiles(code)], axis=1)


def prev_lane(x):
    return pltpu.roll(x, 1, 1)


def next_lane(x):
    return pltpu.roll(x, x.shape[1] - 1, 1)


def prev_sub(x):
    return pltpu.roll(x, 1, 0)


def next_sub(x):
    return pltpu.roll(x, 7, 0)


def at8(i):
    return pl.ds(8 * i, 8) if isinstance(i, int) else pl.ds(pl.multiple_of(8 * i, 8), 8)


def row8(ref, i):
    return ref[at8(i), :]


def turned(core, last, g):
    return core * last + (1 - 2 * core) * g


def k_rows(in_ref, id_ref, a_ref, one_ref):
    other = 1 - lax.axis_index(CORE)
    rows = in_ref.shape[2]
    n_t = in_ref.shape[3] // LANES
    for t in range(n_t):
        at = 16 * rows * t
        for l in range(DEPTH):
            a_ref[pl.ds(at + l, rows, stride=16), :] = in_ref[0, l, :, tile_lanes(t)]
            a_ref[pl.ds(at + DEPTH + l, rows, stride=16), :] = (id_ref[l, :, tile_lanes(t)] + 1).astype(jnp.float32)
    for t in range(n_t):
        to = 17 * rows * t
        for g in range(rows):
            i = 16 * (rows * t + turned(other, rows - 1, g))
            one_ref[to + 16 * g : to + 16 * g + 16, :] = a_ref[pl.ds(pl.multiple_of(i, 16), 16), :]
        for b in range(rows // 8):
            k = to + 16 * rows + 8 * b
            one_ref[k : k + 8, :] = power_rows(in_ref, other, b, t)


def k_solid(u_ref, mat_ref, mg_ref, next_ref, m_ref):
    core = lax.axis_index(CORE)
    mrows = mat_ref.shape[1]
    m_t = mat_ref.shape[2] // LANES
    m_ref[...] = jnp.zeros(m_ref.shape, jnp.float32)
    for t in range(m_t):
        at = 32 * mrows * t
        for l in range(ML):
            for f in range(3):
                m_ref[pl.ds(at + 8 * f + l, mrows, stride=32), :] = u_ref[f, l, :, tile_lanes(t)]
            m_ref[pl.ds(at + 24 + l, mrows, stride=32), :] = (mat_ref[l, :, tile_lanes(t)] + 1).astype(jnp.float32)
        for g in range(mrows):
            i = 32 * (mrows * t + turned(core, mrows - 1, g))
            mg_ref[32 * g : 32 * g + 32, tile_lanes(t)] = m_ref[pl.ds(pl.multiple_of(i, 32), 32), :]
        for g in range(MHALO):
            i = 32 * (mrows * t + turned(core, mrows - 1, mrows - 1 - g))
            next_ref[32 * g : 32 * g + 32, tile_lanes(t)] = m_ref[pl.ds(pl.multiple_of(i, 32), 32), :]


def power_rows(in_ref, turn, b, t):
    rows = in_ref.shape[2]
    x = in_ref[1, 0, at8(turned(turn, rows // 8 - 1, b)), tile_lanes(t)]
    return jnp.take_along_axis(x, turned(turn, 7, sub_iota(LANES)), axis=0, mode="promise_in_bounds")


def k_edge(n_edges, p_ref, a_ref, got_ref, mg_ref, z_ref, *edge_refs):
    core = lax.axis_index(CORE)
    n_t = z_ref.shape[1] // LANES // 2
    rows = p_ref.shape[2]
    mcols = mg_ref.shape[1]
    n = 16 * HALO

    def build(first):
        for t in range(n_t):
            lanes = tile_lanes(t if first else n_t + t)
            for g in range(HALO):
                i = 16 * (rows * t + (g if first else rows - 1 - g))
                z_ref[16 * g : 16 * g + 16, lanes] = a_ref[i : i + 16, :]
            for b in range(2):
                z_ref[n + ZMECH + 8 * b : n + ZMECH + 8 * b + 8, lanes] = power_rows(p_ref, 0 if first else 1, b, t)
            lanes = tile_lanes(n_t + t if first else t)
            at = 17 * rows * t
            z_ref[0:n, lanes] = got_ref[at : at + n, :]
            at += 16 * rows
            z_ref[n + ZMECH : n + ZMECH + 16, lanes] = got_ref[at : at + 16, :]

    @pl.when(core == 0)
    def _():
        build(True)

    @pl.when(core != 0)
    def _():
        build(False)

    for g in range(MHALO):
        for f in range(4):
            at = n + ML * f
            z_ref[at : at + ML, mcols * g : mcols * (g + 1)] = mg_ref[32 * g + 8 * f : 32 * g + 8 * f + ML, :]
    for e in range(n_edges):
        side, lanes, mlanes = edge_lanes(n_edges, e, z_ref.shape[1], mcols)
        cells = [z_ref[8 * i : 8 * i + 8, lanes] for i in range(2 * HALO)]
        cells += [z_ref[n + ZMECH + 8 * b : n + ZMECH + 8 * b + 8, lanes] for b in range(2)]
        fields = [mg_ref[8 * i : 8 * i + 8, mlanes] for i in range(4 * MHALO)]
        pack_edge(edge_refs[e], side, cells, fields)


def edge_lanes(n_edges, e, wide, mcols):
    if n_edges == 1:
        side = 1 - lax.axis_index("col")
        lanes = pl.ds(pl.multiple_of(side * (wide - LANES), LANES), LANES)
        mlanes = pl.ds(pl.multiple_of(side * (mcols - LANES), LANES), LANES)
        return side, lanes, mlanes
    side = 1 - e
    return side, tile_lanes(side * (wide // LANES - 1)), tile_lanes(side * (mcols // LANES - 1))


def pack_edge(ref, side, cells, fields):
    lane = lane_iota()
    at = 0
    for blocks, span, keep in ((cells, SPAN, HALO), (fields, MSPAN, MHALO)):
        per = LANES // span
        for i in range(0, len(blocks), per):
            acc = jnp.zeros((8, LANES), jnp.float32)
            for k, x in enumerate(blocks[i : i + per]):
                acc = jnp.where(lane // span == k, pltpu.roll(x, span * k + side * keep, 1), acc)
            ref[at : at + 8, :] = acc
            at += 8


def edge_size(cells, fields):
    return 8 * (-(-cells * SPAN // LANES) - (-fields * MSPAN // LANES))


def k_chip(n_edges, rows, p_ref, a_ref, got_ref, mg_ref, next_ref, z_ref, w_ref, src_ref, mw_ref, *edge_refs):
    core = lax.axis_index(CORE)
    wide = w_ref.shape[1]
    n_t = wide // LANES // 2
    mcols = mw_ref.shape[1]
    mrows = mg_ref.shape[0] // 32
    n = 16 * HALO
    w_ref[0:n, :] = z_ref[0:n, :]
    src_ref[0:16, :] = z_ref[n + ZMECH : n + ZMECH + 16, :]
    rest = 16 * (rows - HALO)

    def build(first):
        for t in range(n_t):
            lanes = tile_lanes(t if first else n_t + t)
            for g in range(HALO, rows):
                i = 16 * (rows * t + (g if first else rows - 1 - g))
                w_ref[16 * g : 16 * g + 16, lanes] = a_ref[i : i + 16, :]
            for b in range(2, rows // 8):
                src_ref[8 * b : 8 * b + 8, lanes] = power_rows(p_ref, 0 if first else 1, b, t)
            lanes = tile_lanes(n_t + t if first else t)
            at = 17 * rows * t
            w_ref[n : n + rest, lanes] = got_ref[at + n : at + n + rest, :]
            at += 16 * rows
            src_ref[16:rows, lanes] = got_ref[at + 16 : at + rows, :]

    @pl.when(core == 0)
    def _():
        build(True)

    @pl.when(core != 0)
    def _():
        build(False)

    mw_ref[0 : 32 * mrows, :] = mg_ref[...]
    mw_ref[32 * mrows : 32 * (mrows + MHALO), :] = next_ref[...]

    for e in range(n_edges):
        side, lanes, mlanes = edge_lanes(n_edges, e, wide, mcols)
        cells = [w_ref[8 * i : 8 * i + 8, lanes] for i in range(2 * (rows - 1))]
        cells += [src_ref[8 * b : 8 * b + 8, lanes] for b in range(rows // 8)]
        fields = [mw_ref[8 * i : 8 * i + 8, mlanes] for i in range(4 * (mrows + MHALO))]
        pack_edge(edge_refs[e], side, cells, fields)


class Sides:
    def __init__(self, n_col, count, from_left, from_right):
        self.left = from_left
        self.right = from_right
        self.count = count
        lane = lane_iota()
        col = lax.axis_index("col")
        self.masks = {
            w: ((lane < w) & (col < n_col - 1), (lane >= LANES - w) & (col > 0)) for w in (HALO, MHALO)
        }
        self.only = self.left is self.right
        self.side = col

    def take(self, v, k, span, width):
        right_mask, left_mask = self.masks[width]
        x = row8(self.right, v)
        if self.only:
            x = pltpu.roll(x, LANES - span * k - self.side * width, 1)
            return jnp.where(right_mask | left_mask, x, 0.0)
        r = pltpu.roll(x, (LANES - span * k) % LANES, 1)
        l = pltpu.roll(row8(self.left, v), LANES - span * k - width, 1)
        return jnp.where(right_mask, r, jnp.where(left_mask, l, 0.0))

    def tile(self, i):
        per = LANES // SPAN
        return self.take(i // per, i % per, SPAN, HALO)

    def field(self, i):
        per = LANES // MSPAN
        first = -(-self.count * SPAN // LANES)
        return self.take(first + i // per, i % per, MSPAN, MHALO)


def spread_power(ref, n, blocks):
    ref[...] = jnp.zeros(ref.shape, jnp.float32)
    count = ref.shape[0] // (n * 8)
    for first, x in blocks:
        for t, piece in enumerate(tiles(x)):
            ref[pl.ds(8 * (n * t + first), piece.shape[0], stride=8), :] = piece
    return count


def power_row(ref, n, i):
    count = ref.shape[0] // (n * 8)
    return jnp.concatenate([row8(ref, n * t + i) for t in range(count)], axis=1)


def conduct_sum(ref, i):
    x = row8(ref, i)
    sub = sub_iota(x.shape[1])
    total = row8(ref, i - 1) + row8(ref, i + 1) + prev_lane(x) + next_lane(x)
    total = total + jnp.where(sub < DEPTH - 1, next_sub(x), 0.0)
    return total + jnp.where(sub > 0, prev_sub(x), 0.0)


def sink(width):
    return jnp.where(sub_iota(width) == DEPTH - 1, 2.0, 0.2).astype(jnp.float32)


def restrict_columns(x):
    width = x.shape[1]
    x = x + pltpu.roll(x, width - 1, 1) + pltpu.roll(x, width - 2, 1)
    pieces = tiles(x)
    lane = lane_iota()
    out = []
    for j in range((len(pieces) - 1) // 3):
        got = None
        for t in range(3):
            g = gather_lanes(pieces[3 * j + t], (3 * lane) & (LANES - 1))
            got = g if got is None else jnp.where((3 * lane) >= LANES * t, g, got)
        out.append(got)
    first = LANES - MHALO
    index = jnp.where(lane < MHALO, 3 * lane, jnp.where(lane >= first, LANES - 9 + 3 * (lane - first), 64))
    out.append(gather_lanes(pieces[-1], index))
    y = jnp.concatenate(out, axis=1)
    y = jnp.where(sub_iota(y.shape[1]) < 3, y, next_sub(y))
    return y * (1.0 / 9.0)


def first_sweep(s_ref, q0_ref, i, power, h):
    s = row8(s_ref, i)
    inv = 1.0 / (h + s * conduct_sum(s_ref, i))
    return inv, s * ((power + s * conduct_sum(q0_ref, i)) * inv)


def second_sweep(s_ref, q1_ref, di_ref, i, power):
    return (power + row8(s_ref, i) * conduct_sum(q1_ref, i)) * row8(di_ref, i)


def k_inner(n_edges, n_col, rows, tab, w_ref, src_ref, *refs):
    sides = Sides(n_col, 2 * (rows - 1) + rows // 8, refs[0], refs[n_edges - 1])
    s_ref, al_ref, q0_ref, q1_ref, di_ref, t_ref, ea_ref, strain_ref, pw_ref = refs[n_edges:]
    own = rows - 1
    width = src_ref.shape[1] + LANES
    t_s = jnp.sqrt(table_of(tab, 0))
    t_al = table_of(tab, 1)
    side_power = jnp.concatenate([sides.tile(2 * own + k) for k in range(rows // 8)], axis=0)
    n_p = s_ref.shape[0] // 8
    spread_power(pw_ref, n_p, [(FRONT, jnp.concatenate([src_ref[...], side_power], axis=1))])
    h = sink(width)

    for i in range(0, own + 2 * STEP + 2, STEP):
        later = []
        for g in range(i, min(i + STEP, own)):
            temp = jnp.concatenate([w_ref[16 * g : 16 * g + 8, :], sides.tile(2 * g)], axis=1)
            code = jnp.concatenate([w_ref[16 * g + 8 : 16 * g + 16, :], sides.tile(2 * g + 1)], axis=1)
            s = lookup(t_s, code)
            later += [(s_ref, FRONT + g, s), (q0_ref, FRONT + g, s * temp)]
            later += [(al_ref, FRONT + g, lookup(t_al, code))]
        for g in range(max(1, i - STEP - 1), min(i - 1, own - 1)):
            r = FRONT + g
            inv, q1 = first_sweep(s_ref, q0_ref, r, power_row(pw_ref, n_p, r), h)
            later += [(di_ref, r, inv), (q1_ref, r, q1)]
        for g in range(max(2, i - 2 * STEP - 2), min(i - STEP - 2, own - 2)):
            r = FRONT + g
            t2 = second_sweep(s_ref, q1_ref, di_ref, r, power_row(pw_ref, n_p, r))
            later += [(t_ref, r, t2), (ea_ref, r, row8(al_ref, r) * t2)]
        for ref, r, x in later:
            ref[at8(r), :] = x

    def strain(m, carry):
        i = FRONT + 3 * m
        x = row8(ea_ref, i) + row8(ea_ref, i + 1) + row8(ea_ref, i + 2)
        strain_ref[at8(m), :] = restrict_columns(x)
        return carry

    lax.fori_loop(1, (own - 2) // 3, strain, 0, unroll=UNROLL_STRAIN)


def couple_sum(rows3):
    near = [[None] * 3 for _ in range(3)]
    for j in range(3):
        below, mid, above = rows3[j]
        near[0][j] = next_sub(mid) + prev_sub(mid)
        near[1][j] = above + below
        near[2][j] = next_lane(mid) + prev_lane(mid)
    out = []
    for i in range(3):
        j, k = [x for x in range(3) if x != i]
        main = near[i][i] + 0.5 * (near[j][i] + near[k][i])
        side = (near[i][j] + near[j][j]) + (near[i][k] + near[k][k])
        out.append(main + 0.25 * side)
    return out


def mech_tables(tab):
    t_mod = table_of(tab, 2)
    t_m = jnp.sqrt(t_mod)
    return t_m, jnp.where(t_mod > 0.0, 1.0 / jnp.where(t_mod > 0.0, t_m, 1.0), 0.0), t_mod


def k_mech(n_edges, n_col, rows, tab, mw_ref, *refs):
    sides = Sides(n_col, 2 * (rows - 1) + rows // 8, refs[0], refs[n_edges - 1])
    mi_ref, mod_ref = refs[n_edges : n_edges + 2]
    uu_refs = refs[n_edges + 2 : n_edges + 5]
    pre_refs = refs[n_edges + 5 : n_edges + 8]
    t_m, t_mi, t_mod = mech_tables(tab)
    count = mw_ref.shape[0] // 32
    for m in range(count):
        fields = []
        for f in range(4):
            side = sides.field(4 * m + f)
            fields.append(jnp.concatenate([mw_ref[32 * m + 8 * f : 32 * m + 8 * f + 8, :], side], axis=1))
        root = lookup(t_m, fields[3])
        mi_ref[at8(m), :] = lookup(t_mi, fields[3])
        mod_ref[at8(m), :] = lookup(t_mod, fields[3])
        for f in range(3):
            uu_refs[f][at8(m), :] = root * fields[f]
    for m in range(1, count - 1):
        near = couple_sum([[row8(r, m - 1), row8(r, m), row8(r, m + 1)] for r in uu_refs])
        for d in range(3):
            pre_refs[d][at8(m), :] = near[d] * (1.0 / STIFF_DIAG) - row8(uu_refs[d], m)


def k_outer(n_edges, n_col, rows, tab, zr_ref, *refs):
    sides = Sides(n_col, 2 * (rows - 1) + rows // 8, refs[0], refs[n_edges - 1])
    corners = Sides(n_col, 2 * HALO + 2, refs[n_edges], refs[2 * n_edges - 1])
    rest = refs[2 * n_edges :]
    s_in, al_in, q0_in, q1_in, di_in, t_in, ea_in, strain_in, src_ref = rest[:9]
    mi_in, mod_in = rest[9:11]
    uu_in, pre_in = rest[11:14], rest[14:17]
    x_ref, keep_ref, u_ref = rest[17:20]
    s_ref, q0_ref, q1_ref, di_ref, al_ref, ea_ref, t_keep, pw_ref = rest[20:28]
    st_ref, mi_ref, mod_ref, sf_ref = rest[28:32]
    uu_refs, p_refs, d_refs = rest[32:35], rest[35:38], rest[38:41]
    own = rows - 1
    wide = zr_ref.shape[1]
    half = wide // 2
    width = wide + LANES
    t_s = jnp.sqrt(table_of(tab, 0))
    t_al = table_of(tab, 1)
    zsrc = 16 * HALO + ZMECH
    for g in range(3):
        k = AHEAD - 1 - g
        for dst, src in ((s_ref, s_in), (al_ref, al_in), (q0_ref, q0_in)):
            dst[at8(k), :] = row8(src, FRONT + g)
    ea_ref[at8(AHEAD - 3), :] = row8(ea_in, FRONT + 2)
    for g in (1, 2):
        q1_ref[at8(AHEAD - 1 - g), :] = row8(q1_in, FRONT + g)
    di_ref[at8(AHEAD - 2), :] = row8(di_in, FRONT + 1)
    n_p = s_ref.shape[0] // 8
    near = jnp.concatenate([src_ref[0:8, :], sides.tile(2 * own)], axis=1)
    far = jnp.concatenate([corners.tile(2 * HALO), corners.tile(2 * HALO + 1)], axis=0)
    far = jnp.concatenate([zr_ref[zsrc : zsrc + 16, :], far], axis=1)
    spread_power(
        pw_ref,
        n_p,
        [(AHEAD - 1, near[0:1, :]), (AHEAD - 2, near[1:2, :]), (AHEAD, far[0:8, :]), (AHEAD + 8, far[8:HALO, :])],
    )
    h = sink(width)

    for i in range(0, HALO + 2 * STEP + 1, STEP):
        later = []
        for j in range(i, min(i + STEP, HALO)):
            temp = jnp.concatenate([zr_ref[16 * j : 16 * j + 8, :], corners.tile(2 * j)], axis=1)
            code = jnp.concatenate([zr_ref[16 * j + 8 : 16 * j + 16, :], corners.tile(2 * j + 1)], axis=1)
            s = lookup(t_s, code)
            later += [(s_ref, AHEAD + j, s), (q0_ref, AHEAD + j, s * temp)]
            if j < HALO - 2:
                later += [(al_ref, AHEAD + j, lookup(t_al, code))]
        for j in range(max(-1, i - STEP - 1), min(i - 1, HALO - 1)):
            r = AHEAD + j
            inv, q1 = first_sweep(s_ref, q0_ref, r, power_row(pw_ref, n_p, r), h)
            later += [(di_ref, r, inv), (q1_ref, r, q1)]
        for j in range(max(-2, i - 2 * STEP - 2), min(i - STEP - 2, HALO - 2)):
            r = AHEAD + j
            t2 = second_sweep(s_ref, q1_ref, di_ref, r, power_row(pw_ref, n_p, r))
            later += [(t_keep, r, t2), (ea_ref, r, row8(al_ref, r) * t2)]
        for ref, r, x in later:
            ref[at8(r), :] = x

    core = lax.axis_index(CORE)

    def other_half(x):
        return jnp.where(core == 0, x[:, half:wide], x[:, 0:half])

    def own_half(x):
        return jnp.where(core == 0, x[:, 0:half], x[:, half:wide])

    for g in range(2):
        t2 = row8(t_keep, AHEAD - 1 - g)
        keep_ref[8 * g : 8 * g + 8, :] = own_half(t2)
        x_ref[8 * g : 8 * g + 8, :] = other_half(t2)
    x_ref[16:24, :] = other_half(row8(t_in, FRONT + 2))

    count = mod_in.shape[0] // 8
    mrows = count - MHALO
    mwidth = mod_in.shape[1]
    mcols = mwidth - LANES
    n_m = count + MHALO
    for m in range(MHALO + 1):
        i = AHEAD - 3 + 3 * m
        x = row8(ea_ref, i) + row8(ea_ref, i + 1) + row8(ea_ref, i + 2)
        st_ref[at8(MHALO - m), :] = restrict_columns(x)
    for m in range(1, count):
        st_ref[at8(MHALO + m), :] = row8(strain_in, m)
    t_m, t_mi, t_mod = mech_tables(tab)
    for i in range(MHALO):
        j = MHALO - 1 - i
        fields = []
        for f in range(4):
            body = zr_ref[16 * HALO + ML * f : 16 * HALO + ML * f + 8, mcols * j : mcols * (j + 1)]
            body = jnp.where(sub_iota(mcols) < ML, body, 0.0)
            side = corners.field(4 * j + f)
            fields.append(jnp.concatenate([body, side], axis=1))
        root = lookup(t_m, fields[3])
        mi_ref[at8(i), :] = lookup(t_mi, fields[3])
        mod_ref[at8(i), :] = lookup(t_mod, fields[3])
        for f in range(3):
            uu_refs[f][at8(i), :] = root * fields[f]
    for ref, src in zip((mi_ref, mod_ref, *uu_refs), (mi_in, mod_in, *uu_in)):
        ref[8 * MHALO : 8 * n_m, :] = src[...]
    for i in range(n_m):
        sf_ref[at8(i), :] = row8(mod_ref, i) * row8(st_ref, i)
    sign = jnp.where(core == 0, 0.5, -0.5).astype(jnp.float32)
    for i in range(1, n_m - 1):
        load = row8(sf_ref, i)
        force = [
            0.5 * (next_sub(load) - prev_sub(load)),
            sign * (row8(sf_ref, i + 1) - row8(sf_ref, i - 1)),
            0.5 * (next_lane(load) - prev_lane(load)),
        ]
        inv = row8(mi_ref, i)
        inside = inv > 0.0
        if i <= MHALO:
            near = couple_sum([[row8(r, i - 1), row8(r, i), row8(r, i + 1)] for r in uu_refs])
            pre = [near[d] * (1.0 / STIFF_DIAG) - row8(uu_refs[d], i) for d in range(3)]
        else:
            pre = [row8(r, i - MHALO) for r in pre_in]
        inv = inv * (1.0 / STIFF_DIAG)
        for d in range(3):
            p_refs[d][at8(i), :] = jnp.where(inside, force[d] * inv + pre[d], 0.0)
    c_near = 2.0 * RHO1 / DELTA / STIFF_DIAG
    c_self = 1.0 + RHO1 * RHO0
    for i in range(2, n_m - 2):
        near = couple_sum([[row8(r, i - 1), row8(r, i), row8(r, i + 1)] for r in p_refs])
        inv = row8(mi_ref, i)
        for d in range(3):
            moved = row8(uu_refs[d], i) + c_self * row8(p_refs[d], i) + c_near * near[d]
            d_refs[d][at8(i), :] = moved * inv
    sub = sub_iota(mwidth)
    weight = jnp.where(sub < ML, (ML - sub).astype(jnp.float32) * (1.0 / (ML * (ML + 1) / 2.0)), 0.0)
    x_ref[24:32, :] = jnp.zeros((8, x_ref.shape[1]), jnp.float32)
    for g in range(mrows):
        i = MHALO + g
        u0, u2 = row8(d_refs[0], i), row8(d_refs[2], i)
        div = 0.5 * (next_sub(u0) - prev_sub(u0)) + 0.5 * (next_lane(u2) - prev_lane(u2))
        div = div + sign * (row8(d_refs[1], i + 1) - row8(d_refs[1], i - 1))
        stress = row8(mod_ref, i) * (div - 3.0 * row8(st_ref, i))
        die = jnp.sum(weight * stress, axis=0, keepdims=True)
        first, second = die[:, 0:LANES], die[:, LANES : 2 * LANES]
        keep_ref[16 + g : 17 + g, 0:LANES] = jnp.where(core == 0, first, second)
        x_ref[24 + g : 25 + g, 0:LANES] = jnp.where(core == 0, second, first)
        for d in range(3):
            u_ref[8 * (mrows * d + g) : 8 * (mrows * d + g) + 8, :] = row8(d_refs[d], i)[:, 0:mcols]


def k_out(rows, mrows, t_in, keep_ref, xr_ref, u_in, t_out, u_out, slow_ref, buf, die, wide_die, ubuf):
    half = slow_ref.shape[1]
    mcols = u_in.shape[1]
    core = lax.axis_index(CORE)

    def put(ref, at, x):
        count = ref.shape[0] * LANES // x.shape[1]
        for t, piece in enumerate(tiles(x)):
            ref[count * t + at : count * t + at + piece.shape[0], :] = piece

    def build(rev):
        lo = half if rev else 0
        for g in range(rows):
            i = rows - 1 - g if rev else g
            if g < 2:
                x = keep_ref[8 * g : 8 * g + 8, :]
            elif g < rows - 3:
                x = t_in[8 * (FRONT + g) : 8 * (FRONT + g) + 8, lo : lo + half]
            else:
                k = rows - 1 - g
                x = xr_ref[8 * k : 8 * k + 8, :]
            put(buf, 8 * i, x)
        for g in range(mrows):
            mine = 2 * mrows - 1 - g if rev else g
            theirs = g if rev else 2 * mrows - 1 - g
            die[mine : mine + 1, :] = keep_ref[16 + g : 17 + g, 0:LANES]
            die[theirs : theirs + 1, :] = xr_ref[24 + g : 25 + g, 0:LANES]
            for d in range(3):
                i = mrows - 1 - g if rev else g
                put(ubuf, 8 * (mrows * d + i), row8(u_in, mrows * d + g))

    @pl.when(core == 0)
    def _():
        build(False)

    @pl.when(core != 0)
    def _():
        build(True)

    for t in range(half // LANES):
        at = 8 * rows * t
        for l in range(DEPTH):
            t_out[l, :, tile_lanes(t)] = buf[pl.ds(at + l, rows, stride=8), :]
    for t in range(mcols // LANES):
        for d in range(3):
            for l in range(ML):
                u_out[d, l, :, tile_lanes(t)] = ubuf[pl.ds(8 * mrows * (3 * t + d) + l, mrows, stride=8), :]
    lane = lane_iota(2 * mrows)
    for t in range(half // LANES):
        x = gather_lanes(die[...], (lane + LANES * t) // 3)
        for b in range(3):
            wide_die[pl.ds(b, 2 * mrows, stride=3), :] = x
        slow = 1.0 + 0.2 * buf[pl.ds(8 * rows * t, rows, stride=8), :] + 0.5 * wide_die[...]
        slow_ref[:, tile_lanes(t)] = slow


def pairs(dims, sends):
    index = {}
    for r in range(dims[0]):
        for c in range(dims[1]):
            for a in range(dims[2]):
                index[(r, c, a)] = (r * dims[1] + c) * dims[2] + a
    out = []
    for source in index:
        target = sends(*source)
        if target in index:
            out.append((index[source], index[target]))
    return out


def per_device(temp, ids, power, mat, offset, heat_table, growth_table, modulus_table):
    axes = ("row", "col", "lay")
    dims = tuple(lax.axis_size(x) for x in axes)
    n_col = dims[1]
    _, rows, half = temp.shape
    _, _, mrows, mcols = offset.shape
    n_edges = 1 if n_col == 2 else 2
    n_t = half // LANES
    m_t = mcols // LANES

    def send(x, sends):
        return lax.ppermute(x, axes, pairs(dims, sends))

    def swap(r, c, a):
        return (r, c, 1 - a)

    def along(r, c, a):
        return (r + 1, c, 0) if a == 1 else (r - 1, c, 1)

    kind = lax.broadcasted_iota(jnp.int32, (2, *temp.shape), 0)
    packed = jnp.where(kind == 0, temp[None], power[None, None])
    tab = jnp.stack([heat_table, growth_table, modulus_table])
    tab = jnp.pad(tab, ((0, 0), (1, LANES - 1 - tab.shape[1])))
    cells, one = call(k_rows, [(16 * rows * n_t, LANES), (17 * rows * n_t, LANES)], [packed, ids])
    got = send(one, swap)
    mg, ahead = call(
        k_solid,
        [(32 * mrows, mcols), (32 * MHALO, mcols)],
        [offset, mat],
        scratch=[(32 * mrows * m_t, LANES)],
    )
    ahead = send(ahead, swap)
    wide = 2 * half
    own = rows - 1
    z, *edges = call(
        functools.partial(k_edge, n_edges),
        [(16 * HALO + ZMECH + 16, wide)] + [(edge_size(2 * HALO + 2, 4 * MHALO), LANES)] * n_edges,
        [packed, cells, got, mg],
    )
    zr = send(z, along)
    if n_edges == 1:
        corners = [send(edges[0], lambda r, c, a: along(r, 1 - c, a))]
    else:
        corners = [
            send(edges[0], lambda r, c, a: along(r, c + 1, a)),
            send(edges[1], lambda r, c, a: along(r, c - 1, a)),
        ]
    w, src, mw, *edges = call(
        functools.partial(k_chip, n_edges, rows),
        [(16 * rows, wide), (rows, wide), (32 * (mrows + MHALO), mcols)]
        + [(edge_size(2 * own + rows // 8, 4 * (mrows + MHALO)), LANES)] * n_edges,
        [packed, cells, got, mg, ahead, z],
    )
    if n_edges == 1:
        sides = [send(edges[0], lambda r, c, a: (r, 1 - c, a))]
    else:
        sides = [send(edges[0], lambda r, c, a: (r, c + 1, a)), send(edges[1], lambda r, c, a: (r, c - 1, a))]
    width = wide + LANES
    mwidth = mcols + LANES
    n_w = 8 * (rows + FRONT + 4)
    inner = call(
        functools.partial(k_inner, n_edges, n_col, rows),
        [(n_w, width)] * 7 + [(8 * (mrows + MHALO), mwidth)],
        [tab, w, src] + sides,
        scratch=[(n_w * (width // LANES), LANES)],
    )
    t2 = inner[5]
    solid = call(
        functools.partial(k_mech, n_edges, n_col, rows), [(8 * (mrows + MHALO), mwidth)] * 8, [tab, mw] + sides
    )
    n_h = 8 * (AHEAD + HALO + 5)
    n_m = 8 * (mrows + 2 * MHALO)
    x, keep, u = call(
        functools.partial(k_outer, n_edges, n_col, rows),
        [(32, half), (24, half), (24 * mrows, mcols)],
        [tab, zr] + sides + corners + list(inner) + [src] + list(solid),
        scratch=[(n_h, width)] * 7 + [(n_h * (width // LANES), LANES)] + [(n_m, mwidth)] * 13,
    )
    xr = send(x, swap)
    t_out, u_out, slow = call(
        functools.partial(k_out, rows, mrows),
        [temp.shape, offset.shape, power.shape],
        [t2, keep, xr, u],
        scratch=[
            (8 * rows * n_t, LANES),
            (2 * mrows, LANES),
            (rows, LANES),
            (24 * mrows * m_t, LANES),
        ],
    )
    return t_out, u_out, slow


def solution(mesh):
    placed = (
        P("grp", "row", ("col", "lay")),
        P("grp", "row", ("col", "lay")),
        P(("grp", "row"), ("col", "lay")),
        P("grp", ("row", "lay"), "col"),
        P(None, "grp", ("row", "lay"), "col"),
        P(),
        P(),
        P(),
    )
    return jax.shard_map(
        per_device,
        mesh=mesh,
        in_specs=placed,
        out_specs=(
            P("grp", "row", ("col", "lay")),
            P(None, "grp", ("row", "lay"), "col"),
            P(("grp", "row"), ("col", "lay")),
        ),
        check_vma=False,
    )
```

```python
import functools

import jax
import jax.numpy as jnp
from jax import lax
from jax.experimental import pallas as pl
from jax.experimental.pallas import tpu as pltpu
from jax.sharding import PartitionSpec as P

DEPTH = 8
ML = 6
LANES = 128
HALO = 11
MHALO = 3

STIFF_DIAG = 12.0
THETA = 1.0
DELTA = 0.75
SIGMA = THETA / DELTA
RHO0 = 1.0 / SIGMA
RHO1 = 1.0 / (2.0 * SIGMA - RHO0)

VMEM = pl.BlockSpec(memory_space=pltpu.VMEM)
FRONT = 9
AHEAD = 5
STEP = 3
SPAN = 16
MSPAN = 8
NMAT = 16
FAR = 1
FAR_ROW = 9 - 3 * FAR
NEAR = FAR_ROW + 2
ZMECH = 4 * ML
CORE = "lay"
UNROLL_STRAIN = 3


def call(kernel, outs, args, scratch=(), specs=None):
    return pl.pallas_call(
        kernel,
        out_shape=[jax.ShapeDtypeStruct(s, jnp.float32) for s in outs],
        in_specs=specs or [VMEM] * len(args),
        out_specs=[VMEM] * len(outs),
        scratch_shapes=[pltpu.VMEM(s, jnp.float32) if isinstance(s, tuple) else s for s in scratch],
        compiler_params=pltpu.CompilerParams(vmem_limit_bytes=16 * 1024 * 1024),
    )(*args)


def lane_iota(rows=8):
    return lax.broadcasted_iota(jnp.int32, (rows, LANES), 1)


def sub_iota(width):
    return lax.broadcasted_iota(jnp.int32, (8, width), 0)


def tile_lanes(t):
    return slice(LANES * t, LANES * (t + 1))


def tiles(x):
    return [x[:, tile_lanes(t)] for t in range(x.shape[1] // LANES)]


def table_of(ref, k):
    return jnp.broadcast_to(ref[k : k + 1, :], (8, LANES))


def gather_lanes(table, index):
    return jnp.take_along_axis(table, index, axis=1, mode="promise_in_bounds")


def lookup(table, code):
    return jnp.concatenate([gather_lanes(table, c.astype(jnp.int32)) for c in tiles(code)], axis=1)


def splats(table, count):
    return [jnp.broadcast_to(table[:, m : m + 1], (8, LANES)) for m in range(count + 1)]


def choose(lists, code):
    out = [[] for _ in lists]
    for c in tiles(code):
        c = c.astype(jnp.int32)
        bits = [(c & (1 << k)) != 0 for k in range(5)]
        for n, values in enumerate(lists):
            level = values[:16]
            for k in range(4):
                level = [jnp.where(bits[k], b, a) for a, b in zip(level[::2], level[1::2])]
            out[n].append(jnp.where(bits[4], values[16], level[0]))
    return [jnp.concatenate(x, axis=1) for x in out]


def prev_lane(x):
    return pltpu.roll(x, 1, 1)


def next_lane(x):
    return pltpu.roll(x, x.shape[1] - 1, 1)


def prev_sub(x):
    return pltpu.roll(x, 1, 0)


def next_sub(x):
    return pltpu.roll(x, 7, 0)


def at8(i):
    return pl.ds(8 * i, 8) if isinstance(i, int) else pl.ds(pl.multiple_of(8 * i, 8), 8)


def row8(ref, i):
    return ref[at8(i), :]


def turned(core, last, g):
    return core * last + (1 - 2 * core) * g


def k_rows(in_ref, id_ref, a_ref, one_ref):
    core = lax.axis_index(CORE)
    other = 1 - core
    rows = in_ref.shape[2]
    n_t = in_ref.shape[3] // LANES
    n = 16 * HALO
    for t in range(n_t):
        at = 16 * rows * t
        for l in range(DEPTH):
            a_ref[pl.ds(at + l, rows, stride=16), :] = in_ref[0, l, :, tile_lanes(t)]
            a_ref[pl.ds(at + DEPTH + l, rows, stride=16), :] = (id_ref[l, :, tile_lanes(t)] + 1).astype(jnp.float32)
    for t in range(n_t):
        to = (n + 16) * t
        for g in range(HALO):
            i = 16 * (rows * t + turned(other, rows - 1, g))
            one_ref[to + 16 * g : to + 16 * g + 16, :] = a_ref[pl.ds(pl.multiple_of(i, 16), 16), :]
        for b in range(2):
            one_ref[to + n + 8 * b : to + n + 8 * b + 8, :] = power_rows(in_ref, other, b, t)
    for k, x in enumerate(far_strip(in_ref, a_ref, other, core * (n_t - 1), core)):
        to = (n + 16) * n_t + 8 * k
        one_ref[to : to + 8, :] = x


def k_rest(n_edges, in_ref, a_ref, u_ref, mat_ref, two_ref, mg_ref, strip_ref, m_ref):
    core = lax.axis_index(CORE)
    other = 1 - core
    rows = in_ref.shape[2]
    n_t = in_ref.shape[3] // LANES
    mrows = mat_ref.shape[1]
    mcols = mat_ref.shape[2]
    m_t = mcols // LANES
    m_ref[...] = jnp.zeros(m_ref.shape, jnp.float32)
    for t in range(m_t):
        at = 32 * mrows * t
        for l in range(ML):
            for f in range(3):
                m_ref[pl.ds(at + 8 * f + l, mrows, stride=32), :] = u_ref[f, l, :, tile_lanes(t)]
            m_ref[pl.ds(at + 24 + l, mrows, stride=32), :] = (mat_ref[l, :, tile_lanes(t)] + 1).astype(jnp.float32)
        for g in range(mrows):
            i = 32 * (mrows * t + turned(core, mrows - 1, g))
            mg_ref[32 * g : 32 * g + 32, tile_lanes(t)] = m_ref[pl.ds(pl.multiple_of(i, 32), 32), :]
    for e in range(n_edges):
        side = edge_side(n_edges, e)
        fields = []
        for g in range(MHALO):
            i = 32 * (mrows * side * (m_t - 1) + turned(core, mrows - 1, mrows - 1 - g))
            fields += [m_ref[pl.ds(pl.multiple_of(i + 8 * f, 8), 8), :] for f in range(4)]
        (strip_ref[8 * e : 8 * e + 8, :],) = packed(side, fields, MSPAN, MHALO)
    rest = 16 * (rows - HALO)
    for t in range(n_t):
        to = (rest + rows - 16) * t
        for g in range(HALO, rows):
            i = 16 * (rows * t + turned(other, rows - 1, g))
            k = to + 16 * (g - HALO)
            two_ref[k : k + 16, :] = a_ref[pl.ds(pl.multiple_of(i, 16), 16), :]
        for b in range(2, rows // 8):
            two_ref[to + rest + 8 * (b - 2) : to + rest + 8 * (b - 1), :] = power_rows(in_ref, other, b, t)
    for t in range(m_t):
        for g in range(MHALO):
            i = 32 * (mrows * t + turned(core, mrows - 1, mrows - 1 - g))
            k = (rest + rows - 16) * n_t + 32 * (MHALO * t + g)
            two_ref[k : k + 32, :] = m_ref[pl.ds(pl.multiple_of(i, 32), 32), :]


def power_rows(in_ref, turn, b, t):
    rows = in_ref.shape[2]
    lanes = tile_lanes(t) if isinstance(t, int) else pl.ds(pl.multiple_of(LANES * t, LANES), LANES)
    x = in_ref[1, 0, at8(turned(turn, rows // 8 - 1, b)), lanes]
    return jnp.take_along_axis(x, turned(turn, 7, sub_iota(LANES)), axis=0, mode="promise_in_bounds")


def far_strip(in_ref, a_ref, turn, t, side):
    rows = in_ref.shape[2]
    blocks = []
    for g in range(HALO, rows - 1):
        i = 16 * (rows * t + turned(turn, rows - 1, g))
        blocks += [a_ref[pl.ds(pl.multiple_of(i + k, 8), 8), :] for k in (0, 8)]
    blocks += [power_rows(in_ref, turn, b, t) for b in range(2, rows // 8)]
    return packed(side, blocks, SPAN, HALO)


def edge_side(n_edges, e):
    return 1 - lax.axis_index("col") if n_edges == 1 else 1 - e


def edge_tile(side, width):
    if isinstance(side, int):
        return tile_lanes(side * (width // LANES - 1))
    return pl.ds(pl.multiple_of(side * (width - LANES), LANES), LANES)


def packed(side, blocks, span, keep):
    lane = lane_iota()
    per = LANES // span
    out = []
    for i in range(0, len(blocks), per):
        acc = jnp.zeros((8, LANES), jnp.float32)
        for k, x in enumerate(blocks[i : i + per]):
            acc = jnp.where(lane // span == k, pltpu.roll(x, span * k + side * keep, 1), acc)
        out.append(acc)
    return out


def far_rows(rows):
    return -(-(2 * (rows - 1 - HALO) + rows // 8 - 2) * SPAN // LANES)


def k_edge(n_edges, tab, in_ref, a_ref, got_ref, mg_ref, strip_ref, z_ref, w_ref, *refs):
    core = lax.axis_index(CORE)
    wide = z_ref.shape[1]
    n_t = wide // LANES // 2
    rows = in_ref.shape[2]
    mcols = mg_ref.shape[1]
    mrows = mg_ref.shape[0] // 32
    n = 16 * HALO
    edge_refs, (s_ref, q0_ref, q1_ref, di_ref) = refs[: 2 * n_edges], refs[2 * n_edges :]

    def build(first):
        for t in range(n_t):
            lanes = tile_lanes(t if first else n_t + t)
            for g in range(HALO):
                i = 16 * (rows * t + (g if first else rows - 1 - g))
                w_ref[16 * g : 16 * g + 16, lanes] = a_ref[i : i + 16, :]
            for b in range(2):
                w_ref[n + 8 * b : n + 8 * b + 8, lanes] = power_rows(in_ref, 0 if first else 1, b, t)
            lanes = tile_lanes(n_t + t if first else t)
            at = (n + 16) * t
            w_ref[0 : n + 16, lanes] = got_ref[at : at + n + 16, :]

    @pl.when(core == 0)
    def _():
        build(True)

    @pl.when(core != 0)
    def _():
        build(False)

    m = 16 * NEAR
    z_ref[0:m, :] = w_ref[0:m, :]
    z_ref[m + ZMECH : m + ZMECH + 8, :] = w_ref[n : n + 8, :]
    z_ref[m + ZMECH + 8 : m + ZMECH + 16, :] = jnp.zeros((8, wide), jnp.float32)
    for g in range(MHALO):
        for f in range(4):
            at = m + ML * f
            z_ref[at : at + ML, mcols * g : mcols * (g + 1)] = mg_ref[32 * g + 8 * f : 32 * g + 8 * f + ML, :]
    for e in range(n_edges):
        c_ref, d_ref = edge_refs[2 * e], edge_refs[2 * e + 1]
        side = edge_side(n_edges, e)
        lanes, mlanes = edge_tile(side, wide), edge_tile(side, mcols)
        blocks = [w_ref[8 * i : 8 * i + 8, lanes] for i in range(2 * HALO)]
        blocks += [w_ref[n + 8 * b : n + 8 * b + 8, lanes] for b in range(2)]
        fields = [mg_ref[8 * i : 8 * i + 8, mlanes] for i in range(4 * mrows)]
        near = packed(side, blocks, SPAN, HALO) + packed(side, fields[: 4 * MHALO], MSPAN, MHALO)
        far = []
        for k, x in enumerate(far_strip(in_ref, a_ref, core, side * (n_t - 1), side)):
            at = (n + 16) * n_t + 8 * k
            far.append(jnp.where(core == side, x, got_ref[at : at + 8, :]))
        far += packed(side, fields[4 * MHALO :], MSPAN, MHALO)
        far.append(strip_ref[8 * e : 8 * e + 8, :])
        at = FAR * mcols + far_tiles() * LANES * e
        for k, x in enumerate(packed(side, blocks[2 * NEAR : 2 * HALO] + blocks[2 * HALO + 1 :], SPAN, HALO)):
            z_ref[m + ZMECH + 8 : m + ZMECH + 16, at + LANES * k : at + LANES * (k + 1)] = x
        for k, x in enumerate(near + far):
            c_ref[8 * k : 8 * k + 8, :] = x
        for k, x in enumerate(near):
            d_ref[8 * k : 8 * k + 8, :] = x
    t_s = jnp.sqrt(table_of(tab, 0))
    t_al = table_of(tab, 1)
    v_s = splats(t_s, NMAT)
    codes = {}
    for g in range(FAR_ROW - 2, HALO):
        codes[g] = w_ref[16 * g + 8 : 16 * g + 16, :]
        (x,) = choose([v_s], codes[g])
        s_ref[at8(g), :] = x
        q0_ref[at8(g), :] = x * w_ref[16 * g : 16 * g + 8, :]
    h = sink(wide)
    top = sub_iota(wide) == 0
    powers = {
        g: jnp.where(top, jnp.broadcast_to(w_ref[n + g : n + g + 1, :], (8, wide)), 0.0)
        for g in range(FAR_ROW - 1, HALO - 1)
    }
    for g in range(FAR_ROW - 1, HALO - 1):
        di_ref[at8(g), :], q1_ref[at8(g), :] = first_sweep(s_ref, q0_ref, g, powers[g], h, True)
    for f in range(FAR):
        x = None
        for g in range(FAR_ROW + 3 * f, FAR_ROW + 3 * f + 3):
            t2 = second_sweep(s_ref, q1_ref, di_ref, g, powers[g], True)
            ea = lookup(t_al, codes[g]) * t2
            x = ea if x is None else x + ea
        z_ref[m + ZMECH + 8 : m + ZMECH + 16, mcols * f : mcols * (f + 1)] = restrict_main(x)


def far_tiles():
    return -(-(2 * (HALO - NEAR) + 1) * SPAN // LANES)


def k_chip(rows, in_ref, a_ref, got_ref, mg_ref, z_ref, after_ref, w_ref, src_ref, mw_ref):
    core = lax.axis_index(CORE)
    n_t = w_ref.shape[1] // LANES // 2
    mrows = mg_ref.shape[0] // 32
    n = 16 * HALO
    w_ref[0:n, :] = z_ref[0:n, :]
    src_ref[0:16, :] = z_ref[n : n + 16, :]
    rest = 16 * (rows - HALO)

    def build(first):
        for t in range(n_t):
            lanes = tile_lanes(t if first else n_t + t)
            for g in range(HALO, rows):
                i = 16 * (rows * t + (g if first else rows - 1 - g))
                w_ref[16 * g : 16 * g + 16, lanes] = a_ref[i : i + 16, :]
            for b in range(2, rows // 8):
                src_ref[8 * b : 8 * b + 8, lanes] = power_rows(in_ref, 0 if first else 1, b, t)
            lanes = tile_lanes(n_t + t if first else t)
            at = (rest + rows - 16) * t
            w_ref[n : n + rest, lanes] = got_ref[at : at + rest, :]
            src_ref[16:rows, lanes] = got_ref[at + rest : at + rest + rows - 16, :]

    @pl.when(core == 0)
    def _():
        build(True)

    @pl.when(core != 0)
    def _():
        build(False)

    mw_ref[0 : 32 * mrows, :] = mg_ref[...]
    for t in range(mw_ref.shape[1] // LANES):
        at = (rest + rows - 16) * n_t + 32 * MHALO * t
        mw_ref[32 * mrows : 32 * (mrows + MHALO), tile_lanes(t)] = got_ref[at : at + 32 * MHALO, :]


class Sides:
    def __init__(self, n_col, rows, mrows, from_left, from_right):
        self.left = from_left
        self.right = from_right
        self.rows = rows
        self.mrows = mrows
        lane = lane_iota()
        col = lax.axis_index("col")
        self.masks = {
            w: ((lane < w) & (col < n_col - 1), (lane >= LANES - w) & (col > 0)) for w in (HALO, MHALO)
        }
        self.only = self.left is self.right
        self.side = col

    def take(self, v, k, span, width):
        right_mask, left_mask = self.masks[width]
        x = row8(self.right, v)
        if self.only:
            x = pltpu.roll(x, LANES - span * k - self.side * width, 1)
            return jnp.where(right_mask | left_mask, x, 0.0)
        r = pltpu.roll(x, (LANES - span * k) % LANES, 1)
        l = pltpu.roll(row8(self.left, v), LANES - span * k - width, 1)
        return jnp.where(right_mask, r, jnp.where(left_mask, l, 0.0))

    def block(self, first, i, span, width):
        per = LANES // span
        return self.take(first + i // per, i % per, span, width)

    def cell(self, g, kind):
        if g < HALO:
            return self.block(0, 2 * g + kind, SPAN, HALO)
        return self.block(4, 2 * (g - HALO) + kind, SPAN, HALO)

    def power(self, b):
        if b < 2:
            return self.block(0, 2 * HALO + b, SPAN, HALO)
        return self.block(4, 2 * (self.rows - 1 - HALO) + b - 2, SPAN, HALO)

    def field(self, m, f):
        if m < MHALO:
            return self.block(3, 4 * m + f, MSPAN, MHALO)
        first = 4 + far_rows(self.rows)
        if m < self.mrows:
            return self.block(first, 4 * (m - MHALO) + f, MSPAN, MHALO)
        first += -(-4 * (self.mrows - MHALO) * MSPAN // LANES)
        return self.block(first, 4 * (m - self.mrows) + f, MSPAN, MHALO)


def spread_power(ref, n, blocks):
    ref[...] = jnp.zeros(ref.shape, jnp.float32)
    count = ref.shape[0] // (n * 8)
    for first, x in blocks:
        for t, piece in enumerate(tiles(x)):
            ref[pl.ds(8 * (n * t + first), piece.shape[0], stride=8), :] = piece
    return count


def power_row(ref, n, i):
    count = ref.shape[0] // (n * 8)
    return jnp.concatenate([row8(ref, n * t + i) for t in range(count)], axis=1)


def conduct_sum(ref, i, closed=False):
    x = row8(ref, i)
    sub = sub_iota(x.shape[1])
    before, after = prev_lane(x), next_lane(x)
    if closed:
        lane = lax.broadcasted_iota(jnp.int32, x.shape, 1)
        before = jnp.where(lane > 0, before, 0.0)
        after = jnp.where(lane < x.shape[1] - 1, after, 0.0)
    total = row8(ref, i - 1) + row8(ref, i + 1) + before + after
    total = total + jnp.where(sub < DEPTH - 1, next_sub(x), 0.0)
    return total + jnp.where(sub > 0, prev_sub(x), 0.0)


def sink(width):
    return jnp.where(sub_iota(width) == DEPTH - 1, 2.0, 0.2).astype(jnp.float32)


def column_sums(x):
    width = x.shape[1]
    return x + pltpu.roll(x, width - 1, 1) + pltpu.roll(x, width - 2, 1)


def to_solid_layers(y):
    return jnp.where(sub_iota(y.shape[1]) < 3, y, next_sub(y)) * (1.0 / 9.0)


def gather_main(pieces):
    lane = lane_iota()
    out = []
    for j in range(len(pieces) // 3):
        got = None
        for t in range(3):
            g = gather_lanes(pieces[3 * j + t], (3 * lane) & (LANES - 1))
            got = g if got is None else jnp.where((3 * lane) >= LANES * t, g, got)
        out.append(got)
    return out


def gather_sides(piece):
    lane = lane_iota()
    first = LANES - MHALO
    index = jnp.where(lane < MHALO, 3 * lane, jnp.where(lane >= first, LANES - 9 + 3 * (lane - first), 64))
    return gather_lanes(piece, index)


def restrict_main(x):
    return to_solid_layers(jnp.concatenate(gather_main(tiles(column_sums(x))), axis=1))


def restrict_sides(x):
    return to_solid_layers(gather_sides(column_sums(x)))


def restrict_columns(x):
    pieces = tiles(column_sums(x))
    return to_solid_layers(jnp.concatenate(gather_main(pieces[:-1]) + [gather_sides(pieces[-1])], axis=1))


def first_sweep(s_ref, q0_ref, i, power, h, closed=False):
    s = row8(s_ref, i)
    inv = 1.0 / (h + s * conduct_sum(s_ref, i, closed))
    return inv, s * ((power + s * conduct_sum(q0_ref, i, closed)) * inv)


def second_sweep(s_ref, q1_ref, di_ref, i, power, closed=False):
    return (power + row8(s_ref, i) * conduct_sum(q1_ref, i, closed)) * row8(di_ref, i)


def k_inner(n_edges, n_col, rows, tab, w_ref, src_ref, *refs):
    sides = Sides(n_col, rows, rows // 6, refs[0], refs[n_edges - 1])
    s_ref, al_ref, q0_ref, q1_ref, di_ref, t_ref, ea_ref, strain_ref, pw_ref = refs[n_edges:]
    own = rows - 1
    width = src_ref.shape[1] + LANES
    t_s = jnp.sqrt(table_of(tab, 0))
    t_al = table_of(tab, 1)
    v_s = splats(t_s, NMAT)
    side_power = jnp.concatenate([sides.power(k) for k in range(rows // 8)], axis=0)
    n_p = s_ref.shape[0] // 8
    spread_power(pw_ref, n_p, [(FRONT, jnp.concatenate([src_ref[...], side_power], axis=1))])
    h = sink(width)

    for i in range(0, own + 2 * STEP + 2, STEP):
        later = []
        for g in range(i, min(i + STEP, own)):
            temp = jnp.concatenate([w_ref[16 * g : 16 * g + 8, :], sides.cell(g, 0)], axis=1)
            code = jnp.concatenate([w_ref[16 * g + 8 : 16 * g + 16, :], sides.cell(g, 1)], axis=1)
            s, al = choose([v_s], code)[0], lookup(t_al, code)
            later += [(s_ref, FRONT + g, s), (q0_ref, FRONT + g, s * temp), (al_ref, FRONT + g, al)]
        for g in range(max(1, i - STEP - 1), min(i - 1, own - 1)):
            r = FRONT + g
            inv, q1 = first_sweep(s_ref, q0_ref, r, power_row(pw_ref, n_p, r), h)
            later += [(di_ref, r, inv), (q1_ref, r, q1)]
        for g in range(max(2, i - 2 * STEP - 2), min(i - STEP - 2, own - 2)):
            r = FRONT + g
            t2 = second_sweep(s_ref, q1_ref, di_ref, r, power_row(pw_ref, n_p, r))
            later += [(t_ref, r, t2), (ea_ref, r, row8(al_ref, r) * t2)]
        for ref, r, x in later:
            ref[at8(r), :] = x

    def strain(m, carry):
        i = FRONT + 3 * m
        x = row8(ea_ref, i) + row8(ea_ref, i + 1) + row8(ea_ref, i + 2)
        strain_ref[at8(m), :] = restrict_columns(x)
        return carry

    lax.fori_loop(1, (own - 2) // 3, strain, 0, unroll=UNROLL_STRAIN)


def couple_sum(rows3):
    near = [[None] * 3 for _ in range(3)]
    for j in range(3):
        below, mid, above = rows3[j]
        near[0][j] = next_sub(mid) + prev_sub(mid)
        near[1][j] = above + below
        near[2][j] = next_lane(mid) + prev_lane(mid)
    out = []
    for i in range(3):
        j, k = [x for x in range(3) if x != i]
        main = near[i][i] + 0.5 * (near[j][i] + near[k][i])
        side = (near[i][j] + near[j][j]) + (near[i][k] + near[k][k])
        out.append(main + 0.25 * side)
    return out


def moduli(values, code):
    (mod,) = choose([values], code)
    inside = mod > 0.0
    root = jnp.sqrt(mod)
    return mod, root, jnp.where(inside, 1.0 / jnp.where(inside, root, 1.0), 0.0)


def k_mech(n_edges, n_col, rows, tab, mw_ref, *refs):
    sides = Sides(n_col, rows, rows // 6, refs[0], refs[n_edges - 1])
    mi_ref, mod_ref = refs[n_edges : n_edges + 2]
    uu_refs = refs[n_edges + 2 : n_edges + 5]
    pre_refs = refs[n_edges + 5 : n_edges + 8]
    values = splats(table_of(tab, 2), NMAT)
    count = mw_ref.shape[0] // 32
    for m in range(count):
        fields = []
        for f in range(4):
            side = sides.field(m, f)
            fields.append(jnp.concatenate([mw_ref[32 * m + 8 * f : 32 * m + 8 * f + 8, :], side], axis=1))
        mod_ref[at8(m), :], root, mi_ref[at8(m), :] = moduli(values, fields[3])
        for f in range(3):
            uu_refs[f][at8(m), :] = root * fields[f]
    for m in range(1, count - 1):
        near = couple_sum([[row8(r, m - 1), row8(r, m), row8(r, m + 1)] for r in uu_refs])
        for d in range(3):
            pre_refs[d][at8(m), :] = near[d] * (1.0 / STIFF_DIAG) - row8(uu_refs[d], m)


def edge_patch(n_edges, e, corners, zr_ref, mcols, v_s, t_al, scratch):
    s_ref, q0_ref, q1_ref, di_ref = scratch
    side = edge_side(n_edges, e)
    lanes = edge_tile(side, zr_ref.shape[1])
    lane = lane_iota()
    mine = ((lane >= LANES - HALO) & (side == 1)) | ((lane < HALO) & (side == 0))
    zsrc = 16 * NEAR + ZMECH
    per = LANES // SPAN

    def strip(i):
        at = FAR * mcols + LANES * (far_tiles() * e + i // per)
        x = zr_ref[zsrc + 8 : zsrc + 16, at : at + LANES]
        return pltpu.roll(x, LANES - SPAN * (i % per) - side * HALO, 1)

    def cell(j, kind):
        x = zr_ref[16 * j + 8 * kind : 16 * j + 8 * kind + 8, lanes] if j < NEAR else strip(2 * (j - NEAR) + kind)
        return jnp.where(mine, x, corners.cell(j, kind))

    first = FAR_ROW - 2
    codes = {}
    for j in range(first, HALO):
        codes[j] = cell(j, 1)
        (s,) = choose([v_s], codes[j])
        s_ref[at8(j - first), :] = s
        q0_ref[at8(j - first), :] = s * cell(j, 0)
    power = [
        jnp.where(mine, zr_ref[zsrc : zsrc + 8, lanes], corners.power(0)),
        jnp.where(mine, strip(2 * (HALO - NEAR)), corners.power(1)),
    ]
    top = sub_iota(LANES) == 0
    h = sink(LANES)

    def power_of(j):
        x = power[j // 8][j % 8 : j % 8 + 1, :]
        return jnp.where(top, jnp.broadcast_to(x, (8, LANES)), 0.0)

    for j in range(first + 1, HALO - 1):
        at = at8(j - first)
        di_ref[at, :], q1_ref[at, :] = first_sweep(s_ref, q0_ref, j - first, power_of(j), h)
    out = []
    for f in range(FAR):
        x = None
        for j in range(FAR_ROW + 3 * f, FAR_ROW + 3 * f + 3):
            ea = lookup(t_al, codes[j]) * second_sweep(s_ref, q1_ref, di_ref, j - first, power_of(j))
            x = ea if x is None else x + ea
        out.append(restrict_sides(x))
    return out


def k_outer(n_edges, n_col, rows, tab, zr_ref, *refs):
    sides = Sides(n_col, rows, rows // 6, refs[0], refs[n_edges - 1])
    corners = Sides(n_col, rows, rows // 6, refs[n_edges], refs[2 * n_edges - 1])
    rest = refs[2 * n_edges :]
    s_in, al_in, q0_in, q1_in, di_in, t_in, ea_in, strain_in, src_ref = rest[:9]
    mi_in, mod_in = rest[9:11]
    uu_in, pre_in = rest[11:14], rest[14:17]
    x_ref, keep_ref, u_ref = rest[17:20]
    s_ref, q0_ref, q1_ref, di_ref, al_ref, ea_ref, t_keep, pw_ref = rest[20:28]
    st_ref, mi_ref, mod_ref, sf_ref = rest[28:32]
    uu_refs, p_refs, d_refs = rest[32:35], rest[35:38], rest[38:41]
    own = rows - 1
    wide = zr_ref.shape[1]
    half = wide // 2
    width = wide + LANES
    t_s = jnp.sqrt(table_of(tab, 0))
    t_al = table_of(tab, 1)
    v_s = splats(t_s, NMAT)
    zmech = 16 * NEAR
    zsrc = zmech + ZMECH
    zfar = zsrc + 8
    for g in range(3):
        k = AHEAD - 1 - g
        for dst, src in ((s_ref, s_in), (al_ref, al_in), (q0_ref, q0_in)):
            dst[at8(k), :] = row8(src, FRONT + g)
    ea_ref[at8(AHEAD - 3), :] = row8(ea_in, FRONT + 2)
    for g in (1, 2):
        q1_ref[at8(AHEAD - 1 - g), :] = row8(q1_in, FRONT + g)
    di_ref[at8(AHEAD - 2), :] = row8(di_in, FRONT + 1)
    n_p = s_ref.shape[0] // 8
    near = jnp.concatenate([src_ref[0:8, :], sides.power(0)], axis=1)
    far = jnp.concatenate([zr_ref[zsrc : zsrc + 8, :], corners.power(0)], axis=1)
    spread_power(
        pw_ref,
        n_p,
        [(AHEAD - 1, near[0:1, :]), (AHEAD - 2, near[1:2, :]), (AHEAD, far)],
    )
    h = sink(width)

    for i in range(0, NEAR + 2 * STEP + 1, STEP):
        later = []
        for j in range(i, min(i + STEP, NEAR)):
            temp = jnp.concatenate([zr_ref[16 * j : 16 * j + 8, :], corners.cell(j, 0)], axis=1)
            code = jnp.concatenate([zr_ref[16 * j + 8 : 16 * j + 16, :], corners.cell(j, 1)], axis=1)
            s, al = choose([v_s], code)[0], lookup(t_al, code)
            later += [(s_ref, AHEAD + j, s), (q0_ref, AHEAD + j, s * temp), (al_ref, AHEAD + j, al)]
        for j in range(max(-1, i - STEP - 1), min(i - 1, NEAR - 1)):
            r = AHEAD + j
            inv, q1 = first_sweep(s_ref, q0_ref, r, power_row(pw_ref, n_p, r), h)
            later += [(di_ref, r, inv), (q1_ref, r, q1)]
        for j in range(max(-2, i - 2 * STEP - 2), min(i - STEP - 2, NEAR - 2)):
            r = AHEAD + j
            t2 = second_sweep(s_ref, q1_ref, di_ref, r, power_row(pw_ref, n_p, r))
            later += [(t_keep, r, t2), (ea_ref, r, row8(al_ref, r) * t2)]
        for ref, r, x in later:
            ref[at8(r), :] = x

    core = lax.axis_index(CORE)

    def other_half(x):
        return jnp.where(core == 0, x[:, half:wide], x[:, 0:half])

    def own_half(x):
        return jnp.where(core == 0, x[:, 0:half], x[:, half:wide])

    for g in range(2):
        t2 = row8(t_keep, AHEAD - 1 - g)
        keep_ref[8 * g : 8 * g + 8, :] = own_half(t2)
        x_ref[8 * g : 8 * g + 8, :] = other_half(t2)
    x_ref[16:24, :] = other_half(row8(t_in, FRONT + 2))

    count = mod_in.shape[0] // 8
    mrows = count - MHALO
    mwidth = mod_in.shape[1]
    mcols = mwidth - LANES
    n_m = count + MHALO
    for m in range(MHALO + 1 - FAR):
        i = AHEAD - 3 + 3 * m
        x = row8(ea_ref, i) + row8(ea_ref, i + 1) + row8(ea_ref, i + 2)
        st_ref[at8(MHALO - m), :] = restrict_columns(x)
    lane = lane_iota()
    has_left, has_right = sides.side > 0, sides.side < n_col - 1
    patches = [edge_patch(n_edges, e, corners, zr_ref, mcols, v_s, t_al, rest[41:45]) for e in range(n_edges)]
    for f in range(FAR):
        pieces = tiles(zr_ref[zfar : zfar + 8, mcols * f : mcols * (f + 1)])
        right, left = patches[0][f], patches[-1][f]
        pieces[0] = jnp.where((lane == 0) & has_left, left, pieces[0])
        pieces[-1] = jnp.where((lane == LANES - 1) & has_right, right, pieces[-1])
        beside = jnp.where((lane < MHALO) & has_right, right, jnp.where((lane >= LANES - MHALO) & has_left, left, 0.0))
        st_ref[at8(FAR - 1 - f), :] = jnp.concatenate(pieces + [beside], axis=1)
    for m in range(1, count):
        st_ref[at8(MHALO + m), :] = row8(strain_in, m)
    values = splats(table_of(tab, 2), NMAT)
    for i in range(MHALO):
        j = MHALO - 1 - i
        fields = []
        for f in range(4):
            body = zr_ref[zmech + ML * f : zmech + ML * f + 8, mcols * j : mcols * (j + 1)]
            body = jnp.where(sub_iota(mcols) < ML, body, 0.0)
            side = corners.field(j, f)
            fields.append(jnp.concatenate([body, side], axis=1))
        mod_ref[at8(i), :], root, mi_ref[at8(i), :] = moduli(values, fields[3])
        for f in range(3):
            uu_refs[f][at8(i), :] = root * fields[f]
    for ref, src in zip((mi_ref, mod_ref, *uu_refs), (mi_in, mod_in, *uu_in)):
        ref[8 * MHALO : 8 * n_m, :] = src[...]
    for i in range(n_m):
        sf_ref[at8(i), :] = row8(mod_ref, i) * row8(st_ref, i)
    sign = jnp.where(core == 0, 0.5, -0.5).astype(jnp.float32)
    for i in range(1, n_m - 1):
        load = row8(sf_ref, i)
        force = [
            0.5 * (next_sub(load) - prev_sub(load)),
            sign * (row8(sf_ref, i + 1) - row8(sf_ref, i - 1)),
            0.5 * (next_lane(load) - prev_lane(load)),
        ]
        inv = row8(mi_ref, i)
        inside = inv > 0.0
        if i <= MHALO:
            near = couple_sum([[row8(r, i - 1), row8(r, i), row8(r, i + 1)] for r in uu_refs])
            pre = [near[d] * (1.0 / STIFF_DIAG) - row8(uu_refs[d], i) for d in range(3)]
        else:
            pre = [row8(r, i - MHALO) for r in pre_in]
        inv = inv * (1.0 / STIFF_DIAG)
        for d in range(3):
            p_refs[d][at8(i), :] = jnp.where(inside, force[d] * inv + pre[d], 0.0)
    c_near = 2.0 * RHO1 / DELTA / STIFF_DIAG
    c_self = 1.0 + RHO1 * RHO0
    for i in range(2, n_m - 2):
        near = couple_sum([[row8(r, i - 1), row8(r, i), row8(r, i + 1)] for r in p_refs])
        inv = row8(mi_ref, i)
        for d in range(3):
            moved = row8(uu_refs[d], i) + c_self * row8(p_refs[d], i) + c_near * near[d]
            d_refs[d][at8(i), :] = moved * inv
    sub = sub_iota(mwidth)
    weight = jnp.where(sub < ML, (ML - sub).astype(jnp.float32) * (1.0 / (ML * (ML + 1) / 2.0)), 0.0)
    x_ref[24:32, :] = jnp.zeros((8, x_ref.shape[1]), jnp.float32)
    for g in range(mrows):
        i = MHALO + g
        u0, u2 = row8(d_refs[0], i), row8(d_refs[2], i)
        div = 0.5 * (next_sub(u0) - prev_sub(u0)) + 0.5 * (next_lane(u2) - prev_lane(u2))
        div = div + sign * (row8(d_refs[1], i + 1) - row8(d_refs[1], i - 1))
        stress = row8(mod_ref, i) * (div - 3.0 * row8(st_ref, i))
        die = jnp.sum(weight * stress, axis=0, keepdims=True)
        first, second = die[:, 0:LANES], die[:, LANES : 2 * LANES]
        keep_ref[16 + g : 17 + g, 0:LANES] = jnp.where(core == 0, first, second)
        x_ref[24 + g : 25 + g, 0:LANES] = jnp.where(core == 0, second, first)
        for d in range(3):
            u_ref[8 * (mrows * d + g) : 8 * (mrows * d + g) + 8, :] = row8(d_refs[d], i)[:, 0:mcols]


def k_out(rows, mrows, t_in, keep_ref, xr_ref, u_in, t_out, u_out, slow_ref, buf, die, wide_die, ubuf):
    half = slow_ref.shape[1]
    mcols = u_in.shape[1]
    core = lax.axis_index(CORE)

    def put(ref, at, x):
        count = ref.shape[0] * LANES // x.shape[1]
        for t, piece in enumerate(tiles(x)):
            ref[count * t + at : count * t + at + piece.shape[0], :] = piece

    def build(rev):
        lo = half if rev else 0
        for g in range(rows):
            i = rows - 1 - g if rev else g
            if g < 2:
                x = keep_ref[8 * g : 8 * g + 8, :]
            elif g < rows - 3:
                x = t_in[8 * (FRONT + g) : 8 * (FRONT + g) + 8, lo : lo + half]
            else:
                k = rows - 1 - g
                x = xr_ref[8 * k : 8 * k + 8, :]
            put(buf, 8 * i, x)
        for g in range(mrows):
            mine = 2 * mrows - 1 - g if rev else g
            theirs = g if rev else 2 * mrows - 1 - g
            die[mine : mine + 1, :] = keep_ref[16 + g : 17 + g, 0:LANES]
            die[theirs : theirs + 1, :] = xr_ref[24 + g : 25 + g, 0:LANES]
            for d in range(3):
                i = mrows - 1 - g if rev else g
                put(ubuf, 8 * (mrows * d + i), row8(u_in, mrows * d + g))

    @pl.when(core == 0)
    def _():
        build(False)

    @pl.when(core != 0)
    def _():
        build(True)

    for t in range(half // LANES):
        at = 8 * rows * t
        for l in range(DEPTH):
            t_out[l, :, tile_lanes(t)] = buf[pl.ds(at + l, rows, stride=8), :]
    for t in range(mcols // LANES):
        for d in range(3):
            for l in range(ML):
                u_out[d, l, :, tile_lanes(t)] = ubuf[pl.ds(8 * mrows * (3 * t + d) + l, mrows, stride=8), :]
    lane = lane_iota(2 * mrows)
    for t in range(half // LANES):
        x = gather_lanes(die[...], (lane + LANES * t) // 3)
        for b in range(3):
            wide_die[pl.ds(b, 2 * mrows, stride=3), :] = x
        slow = 1.0 + 0.2 * buf[pl.ds(8 * rows * t, rows, stride=8), :] + 0.5 * wide_die[...]
        slow_ref[:, tile_lanes(t)] = slow


def pairs(dims, sends):
    index = {}
    for r in range(dims[0]):
        for c in range(dims[1]):
            for a in range(dims[2]):
                index[(r, c, a)] = (r * dims[1] + c) * dims[2] + a
    out = []
    for source in index:
        target = sends(*source)
        if target in index:
            out.append((index[source], index[target]))
    return out


def per_device(temp, ids, power, mat, offset, heat_table, growth_table, modulus_table):
    axes = ("row", "col", "lay")
    dims = tuple(lax.axis_size(x) for x in axes)
    n_col = dims[1]
    _, rows, half = temp.shape
    _, _, mrows, mcols = offset.shape
    n_edges = 1 if n_col == 2 else 2
    n_t = half // LANES
    m_t = mcols // LANES

    def send(x, sends):
        return lax.ppermute(x, axes, pairs(dims, sends))

    def swap(r, c, a):
        return (r, c, 1 - a)

    def along(r, c, a):
        return (r + 1, c, 0) if a == 1 else (r - 1, c, 1)

    wide = 2 * half
    own = rows - 1
    kind = lax.broadcasted_iota(jnp.int32, (2, *temp.shape), 0)
    both = jnp.where(kind == 0, temp[None], power[None, None])
    tab = jnp.stack([heat_table, growth_table, modulus_table])
    tab = jnp.pad(tab, ((0, 0), (1, LANES - 1 - tab.shape[1])))
    n = 16 * HALO
    n_far = 8 * far_rows(rows)
    cells, one = call(k_rows, [(16 * rows * n_t, LANES), ((n + 16) * n_t + n_far, LANES)], [both, ids])
    got1 = send(one, swap)
    two, mg, strip = call(
        functools.partial(k_rest, n_edges),
        [
            ((16 * (rows - HALO) + rows - 16) * n_t + 32 * MHALO * m_t, LANES),
            (32 * mrows, mcols),
            (8 * n_edges, LANES),
        ],
        [both, cells, offset, mat],
        scratch=[(32 * mrows * m_t, LANES)],
    )
    strip = send(strip, swap)
    got2 = send(two, swap)
    n_c = 32 + n_far - 8 * (-4 * (mrows - MHALO) * MSPAN // LANES) + 8
    z, first_rows, *edges = call(
        functools.partial(k_edge, n_edges),
        [(16 * NEAR + ZMECH + 16, wide), (n + 16, wide)] + [(n_c, LANES), (32, LANES)] * n_edges,
        [tab, both, cells, got1, mg, strip],
        scratch=[(8 * HALO, wide)] * 4,
    )
    zr = send(z, along)
    if n_edges == 1:
        sides = [send(edges[0], lambda r, c, a: (r, 1 - c, a))]
        corners = [send(edges[1], lambda r, c, a: along(r, 1 - c, a))]
    else:
        sides = [send(edges[0], lambda r, c, a: (r, c + 1, a)), send(edges[2], lambda r, c, a: (r, c - 1, a))]
        corners = [
            send(edges[1], lambda r, c, a: along(r, c + 1, a)),
            send(edges[3], lambda r, c, a: along(r, c - 1, a)),
        ]
    w, src, mw = call(
        functools.partial(k_chip, rows),
        [(16 * rows, wide), (rows, wide), (32 * (mrows + MHALO), mcols)],
        [both, cells, got2, mg, first_rows, sides[0]],
    )
    width = wide + LANES
    mwidth = mcols + LANES
    n_w = 8 * (rows + FRONT + 4)
    inner = call(
        functools.partial(k_inner, n_edges, n_col, rows),
        [(n_w, width)] * 7 + [(8 * (mrows + MHALO), mwidth)],
        [tab, w, src] + sides,
        scratch=[(n_w * (width // LANES), LANES)],
    )
    t2 = inner[5]
    solid = call(
        functools.partial(k_mech, n_edges, n_col, rows), [(8 * (mrows + MHALO), mwidth)] * 8, [tab, mw] + sides
    )
    n_h = 8 * (AHEAD + HALO + 5)
    n_m = 8 * (mrows + 2 * MHALO)
    x, keep, u = call(
        functools.partial(k_outer, n_edges, n_col, rows),
        [(32, half), (24, half), (24 * mrows, mcols)],
        [tab, zr] + sides + corners + list(inner) + [src] + list(solid),
        scratch=[(n_h, width)] * 7
        + [(n_h * (width // LANES), LANES)]
        + [(n_m, mwidth)] * 13
        + [(8 * HALO, LANES)] * 4,
    )
    xr = send(x, swap)
    t_out, u_out, slow = call(
        functools.partial(k_out, rows, mrows),
        [temp.shape, offset.shape, power.shape],
        [t2, keep, xr, u],
        scratch=[
            (8 * rows * n_t, LANES),
            (2 * mrows, LANES),
            (rows, LANES),
            (24 * mrows * m_t, LANES),
        ],
    )
    return t_out, u_out, slow


def solution(mesh):
    placed = (
        P("grp", "row", ("col", "lay")),
        P("grp", "row", ("col", "lay")),
        P(("grp", "row"), ("col", "lay")),
        P("grp", ("row", "lay"), "col"),
        P(None, "grp", ("row", "lay"), "col"),
        P(),
        P(),
        P(),
    )
    return jax.shard_map(
        per_device,
        mesh=mesh,
        in_specs=placed,
        out_specs=(
            P("grp", "row", ("col", "lay")),
            P(None, "grp", ("row", "lay"), "col"),
            P(("grp", "row"), ("col", "lay")),
        ),
        check_vma=False,
    )
```

```python
import functools

import jax
import jax.numpy as jnp
from jax import lax
from jax.experimental import pallas as pl
from jax.experimental.pallas import tpu as pltpu
from jax.sharding import PartitionSpec as P

DEPTH = 8
ML = 6
LANES = 128
HALO = 11
MHALO = 3

STIFF_DIAG = 12.0
THETA = 1.0
DELTA = 0.75
SIGMA = THETA / DELTA
RHO0 = 1.0 / SIGMA
RHO1 = 1.0 / (2.0 * SIGMA - RHO0)

VMEM = pl.BlockSpec(memory_space=pltpu.VMEM)
FRONT = 9
AHEAD = 5
STEP = 3
SPAN = 16
MSPAN = 8
NMAT = 16
FAR = 2
EDGE_COST = 10**10
FAR_ROW = 9 - 3 * FAR
NEAR = FAR_ROW + 2
ZMECH = 4 * ML
CORE = "lay"
UNROLL_STRAIN = 3


def call(kernel, outs, args, scratch=(), specs=None, aliases=None, cost=0):
    return pl.pallas_call(
        kernel,
        out_shape=[jax.ShapeDtypeStruct(s, jnp.float32) for s in outs],
        in_specs=specs or [VMEM] * len(args),
        out_specs=[VMEM] * len(outs),
        input_output_aliases=aliases or {},
        cost_estimate=pl.CostEstimate(flops=cost, bytes_accessed=0, transcendentals=0) if cost else None,
        scratch_shapes=[pltpu.VMEM(s, jnp.float32) if isinstance(s, tuple) else s for s in scratch],
        compiler_params=pltpu.CompilerParams(vmem_limit_bytes=16 * 1024 * 1024),
    )(*args)


def lane_iota(rows=8):
    return lax.broadcasted_iota(jnp.int32, (rows, LANES), 1)


def sub_iota(width):
    return lax.broadcasted_iota(jnp.int32, (8, width), 0)


def tile_lanes(t):
    return slice(LANES * t, LANES * (t + 1))


def tiles(x):
    return [x[:, tile_lanes(t)] for t in range(x.shape[1] // LANES)]


def table_of(ref, k):
    return jnp.broadcast_to(ref[k : k + 1, :], (8, LANES))


def gather_lanes(table, index):
    return jnp.take_along_axis(table, index, axis=1, mode="promise_in_bounds")


def lookup(table, code):
    return jnp.concatenate([gather_lanes(table, c.astype(jnp.int32)) for c in tiles(code)], axis=1)


def splats(table, count):
    return [jnp.broadcast_to(table[:, m : m + 1], (8, LANES)) for m in range(count + 1)]


def choose(lists, code):
    out = [[] for _ in lists]
    for c in tiles(code):
        c = c.astype(jnp.int32)
        bits = [(c & (1 << k)) != 0 for k in range(5)]
        for n, values in enumerate(lists):
            level = values[:16]
            for k in range(4):
                level = [jnp.where(bits[k], b, a) for a, b in zip(level[::2], level[1::2])]
            out[n].append(jnp.where(bits[4], values[16], level[0]))
    return [jnp.concatenate(x, axis=1) for x in out]


def prev_lane(x):
    return pltpu.roll(x, 1, 1)


def next_lane(x):
    return pltpu.roll(x, x.shape[1] - 1, 1)


def prev_sub(x):
    return pltpu.roll(x, 1, 0)


def next_sub(x):
    return pltpu.roll(x, 7, 0)


def at8(i):
    return pl.ds(8 * i, 8) if isinstance(i, int) else pl.ds(pl.multiple_of(8 * i, 8), 8)


def row8(ref, i):
    return ref[at8(i), :]


def turned(core, last, g):
    return core * last + (1 - 2 * core) * g


def k_rows(in_ref, id_ref, a_ref, one_ref):
    core = lax.axis_index(CORE)
    other = 1 - core
    rows = in_ref.shape[2]
    n_t = in_ref.shape[3] // LANES
    n = 16 * HALO
    for t in range(n_t):
        at = 16 * rows * t
        for l in range(DEPTH):
            a_ref[pl.ds(at + l, rows, stride=16), :] = in_ref[0, l, :, tile_lanes(t)]
            a_ref[pl.ds(at + DEPTH + l, rows, stride=16), :] = (id_ref[l, :, tile_lanes(t)] + 1).astype(jnp.float32)
    for t in range(n_t):
        to = (n + 16) * t
        for g in range(HALO):
            i = 16 * (rows * t + turned(other, rows - 1, g))
            one_ref[to + 16 * g : to + 16 * g + 16, :] = a_ref[pl.ds(pl.multiple_of(i, 16), 16), :]
        for b in range(2):
            one_ref[to + n + 8 * b : to + n + 8 * b + 8, :] = power_rows(in_ref, other, b, t)
    for k, x in enumerate(far_strip(in_ref, a_ref, other, core * (n_t - 1), core)):
        to = (n + 16) * n_t + 8 * k
        one_ref[to : to + 8, :] = x


def k_rest(n_edges, in_ref, a_ref, u_ref, mat_ref, two_ref, mg_ref, strip_ref, m_ref):
    core = lax.axis_index(CORE)
    other = 1 - core
    rows = in_ref.shape[2]
    n_t = in_ref.shape[3] // LANES
    mrows = mat_ref.shape[1]
    mcols = mat_ref.shape[2]
    m_t = mcols // LANES
    m_ref[...] = jnp.zeros(m_ref.shape, jnp.float32)
    for t in range(m_t):
        at = 32 * mrows * t
        for l in range(ML):
            for f in range(3):
                m_ref[pl.ds(at + 8 * f + l, mrows, stride=32), :] = u_ref[f, l, :, tile_lanes(t)]
            m_ref[pl.ds(at + 24 + l, mrows, stride=32), :] = (mat_ref[l, :, tile_lanes(t)] + 1).astype(jnp.float32)
        for g in range(mrows):
            i = 32 * (mrows * t + turned(core, mrows - 1, g))
            mg_ref[32 * g : 32 * g + 32, tile_lanes(t)] = m_ref[pl.ds(pl.multiple_of(i, 32), 32), :]
    for e in range(n_edges):
        side = edge_side(n_edges, e)
        fields = []
        for g in range(MHALO):
            i = 32 * (mrows * side * (m_t - 1) + turned(core, mrows - 1, mrows - 1 - g))
            fields += [m_ref[pl.ds(pl.multiple_of(i + 8 * f, 8), 8), :] for f in range(4)]
        (strip_ref[8 * e : 8 * e + 8, :],) = packed(side, fields, MSPAN, MHALO)
    rest = 16 * (rows - HALO)
    for t in range(n_t):
        to = (rest + rows - 16) * t
        for g in range(HALO, rows):
            i = 16 * (rows * t + turned(other, rows - 1, g))
            k = to + 16 * (g - HALO)
            two_ref[k : k + 16, :] = a_ref[pl.ds(pl.multiple_of(i, 16), 16), :]
        for b in range(2, rows // 8):
            two_ref[to + rest + 8 * (b - 2) : to + rest + 8 * (b - 1), :] = power_rows(in_ref, other, b, t)
    for t in range(m_t):
        for g in range(MHALO):
            i = 32 * (mrows * t + turned(core, mrows - 1, mrows - 1 - g))
            k = (rest + rows - 16) * n_t + 32 * (MHALO * t + g)
            two_ref[k : k + 32, :] = m_ref[pl.ds(pl.multiple_of(i, 32), 32), :]


def power_rows(in_ref, turn, b, t):
    rows = in_ref.shape[2]
    lanes = tile_lanes(t) if isinstance(t, int) else pl.ds(pl.multiple_of(LANES * t, LANES), LANES)
    x = in_ref[1, 0, at8(turned(turn, rows // 8 - 1, b)), lanes]
    return jnp.take_along_axis(x, turned(turn, 7, sub_iota(LANES)), axis=0, mode="promise_in_bounds")


def far_strip(in_ref, a_ref, turn, t, side):
    rows = in_ref.shape[2]
    blocks = []
    for g in range(HALO, rows - 1):
        i = 16 * (rows * t + turned(turn, rows - 1, g))
        blocks += [a_ref[pl.ds(pl.multiple_of(i + k, 8), 8), :] for k in (0, 8)]
    blocks += [power_rows(in_ref, turn, b, t) for b in range(2, rows // 8)]
    return packed(side, blocks, SPAN, HALO)


def edge_side(n_edges, e):
    return 1 - lax.axis_index("col") if n_edges == 1 else 1 - e


def edge_tile(side, width):
    if isinstance(side, int):
        return tile_lanes(side * (width // LANES - 1))
    return pl.ds(pl.multiple_of(side * (width - LANES), LANES), LANES)


def packed(side, blocks, span, keep):
    lane = lane_iota()
    per = LANES // span
    out = []
    for i in range(0, len(blocks), per):
        acc = jnp.zeros((8, LANES), jnp.float32)
        for k, x in enumerate(blocks[i : i + per]):
            acc = jnp.where(lane // span == k, pltpu.roll(x, span * k + side * keep, 1), acc)
        out.append(acc)
    return out


def far_rows(rows):
    return -(-(2 * (rows - 1 - HALO) + rows // 8 - 2) * SPAN // LANES)


def k_edge(n_edges, tab, in_ref, a_ref, got_ref, mg_ref, strip_ref, z_ref, w_ref, *refs):
    core = lax.axis_index(CORE)
    wide = z_ref.shape[1]
    n_t = wide // LANES // 2
    rows = in_ref.shape[2]
    mcols = mg_ref.shape[1]
    mrows = mg_ref.shape[0] // 32
    n = 16 * HALO
    edge_refs, (s_ref, q0_ref, q1_ref, di_ref) = refs[: 2 * n_edges], refs[2 * n_edges :]

    def build(first):
        for t in range(n_t):
            lanes = tile_lanes(t if first else n_t + t)
            for g in range(HALO):
                i = 16 * (rows * t + (g if first else rows - 1 - g))
                w_ref[16 * g : 16 * g + 16, lanes] = a_ref[i : i + 16, :]
            for b in range(2):
                w_ref[n + 8 * b : n + 8 * b + 8, lanes] = power_rows(in_ref, 0 if first else 1, b, t)
            lanes = tile_lanes(n_t + t if first else t)
            at = (n + 16) * t
            w_ref[0 : n + 16, lanes] = got_ref[at : at + n + 16, :]

    @pl.when(core == 0)
    def _():
        build(True)

    @pl.when(core != 0)
    def _():
        build(False)

    m = 16 * NEAR
    z_ref[0:m, :] = w_ref[0:m, :]
    z_ref[m + ZMECH : m + ZMECH + 8, :] = w_ref[n : n + 8, :]
    z_ref[m + ZMECH + 8 :, :] = jnp.zeros((z_ref.shape[0] - m - ZMECH - 8, wide), jnp.float32)
    for g in range(MHALO):
        for f in range(4):
            at = m + ML * f
            z_ref[at : at + ML, mcols * g : mcols * (g + 1)] = mg_ref[32 * g + 8 * f : 32 * g + 8 * f + ML, :]
    for e in range(n_edges):
        c_ref, d_ref = edge_refs[2 * e], edge_refs[2 * e + 1]
        side = edge_side(n_edges, e)
        lanes, mlanes = edge_tile(side, wide), edge_tile(side, mcols)
        blocks = [w_ref[8 * i : 8 * i + 8, lanes] for i in range(2 * HALO)]
        blocks += [w_ref[n + 8 * b : n + 8 * b + 8, lanes] for b in range(2)]
        fields = [mg_ref[8 * i : 8 * i + 8, mlanes] for i in range(4 * mrows)]
        near = packed(side, blocks, SPAN, HALO) + packed(side, fields[: 4 * MHALO], MSPAN, MHALO)
        far = []
        for k, x in enumerate(far_strip(in_ref, a_ref, core, side * (n_t - 1), side)):
            at = (n + 16) * n_t + 8 * k
            far.append(jnp.where(core == side, x, got_ref[at : at + 8, :]))
        far += packed(side, fields[4 * MHALO :], MSPAN, MHALO)
        far.append(strip_ref[8 * e : 8 * e + 8, :])
        for k, x in enumerate(packed(side, blocks[2 * NEAR : 2 * HALO] + blocks[2 * HALO + 1 :], SPAN, HALO)):
            z_ref[far_place(e, k, wide, mcols)] = x
        for k, x in enumerate(near + far):
            c_ref[8 * k : 8 * k + 8, :] = x
        for k, x in enumerate(near):
            d_ref[8 * k : 8 * k + 8, :] = x
    t_s = jnp.sqrt(table_of(tab, 0))
    t_al = table_of(tab, 1)
    v_s = splats(t_s, NMAT)
    codes = {}
    for g in range(FAR_ROW - 2, HALO):
        codes[g] = w_ref[16 * g + 8 : 16 * g + 16, :]
        (x,) = choose([v_s], codes[g])
        s_ref[at8(g), :] = x
        q0_ref[at8(g), :] = x * w_ref[16 * g : 16 * g + 8, :]
    h = sink(wide)
    top = sub_iota(wide) == 0
    powers = {
        g: jnp.where(top, jnp.broadcast_to(w_ref[n + g : n + g + 1, :], (8, wide)), 0.0)
        for g in range(FAR_ROW - 1, HALO - 1)
    }
    for g in range(FAR_ROW - 1, HALO - 1):
        di_ref[at8(g), :], q1_ref[at8(g), :] = first_sweep(s_ref, q0_ref, g, powers[g], h, True)
    for f in range(FAR):
        x = None
        for g in range(FAR_ROW + 3 * f, FAR_ROW + 3 * f + 3):
            t2 = second_sweep(s_ref, q1_ref, di_ref, g, powers[g], True)
            ea = lookup(t_al, codes[g]) * t2
            x = ea if x is None else x + ea
        z_ref[m + ZMECH + 8 : m + ZMECH + 16, mcols * f : mcols * (f + 1)] = restrict_main(x)


def far_tiles():
    return -(-(2 * (HALO - NEAR) + 1) * SPAN // LANES)


def far_place(e, k, wide, mcols):
    q = FAR * mcols // LANES + far_tiles() * e + k
    at = 16 * NEAR + ZMECH + 8 + 8 * (q // (wide // LANES))
    return slice(at, at + 8), tile_lanes(q % (wide // LANES))


def k_chip(rows, in_ref, a_ref, got_ref, mg_ref, z_ref, *refs):
    count = (len(refs) - 3) // 2
    w_ref, src_ref, mw_ref = refs[count : count + 3]
    core = lax.axis_index(CORE)
    n_t = w_ref.shape[1] // LANES // 2
    mrows = mg_ref.shape[0] // 32
    n = 16 * HALO
    w_ref[0:n, :] = z_ref[0:n, :]
    src_ref[0:16, :] = z_ref[n : n + 16, :]
    rest = 16 * (rows - HALO)

    def build(first):
        for t in range(n_t):
            lanes = tile_lanes(t if first else n_t + t)
            for g in range(HALO, rows):
                i = 16 * (rows * t + (g if first else rows - 1 - g))
                w_ref[16 * g : 16 * g + 16, lanes] = a_ref[i : i + 16, :]
            for b in range(2, rows // 8):
                src_ref[8 * b : 8 * b + 8, lanes] = power_rows(in_ref, 0 if first else 1, b, t)
            lanes = tile_lanes(n_t + t if first else t)
            at = (rest + rows - 16) * t
            w_ref[n : n + rest, lanes] = got_ref[at : at + rest, :]
            src_ref[16:rows, lanes] = got_ref[at + rest : at + rest + rows - 16, :]

    @pl.when(core == 0)
    def _():
        build(True)

    @pl.when(core != 0)
    def _():
        build(False)

    mw_ref[0 : 32 * mrows, :] = mg_ref[...]
    for t in range(mw_ref.shape[1] // LANES):
        at = (rest + rows - 16) * n_t + 32 * MHALO * t
        mw_ref[32 * mrows : 32 * (mrows + MHALO), tile_lanes(t)] = got_ref[at : at + 32 * MHALO, :]


class Sides:
    def __init__(self, n_col, rows, mrows, from_left, from_right):
        self.left = from_left
        self.right = from_right
        self.rows = rows
        self.mrows = mrows
        lane = lane_iota()
        col = lax.axis_index("col")
        self.masks = {
            w: ((lane < w) & (col < n_col - 1), (lane >= LANES - w) & (col > 0)) for w in (HALO, MHALO)
        }
        self.only = self.left is self.right
        self.side = col

    def take(self, v, k, span, width):
        right_mask, left_mask = self.masks[width]
        x = row8(self.right, v)
        if self.only:
            x = pltpu.roll(x, LANES - span * k - self.side * width, 1)
            return jnp.where(right_mask | left_mask, x, 0.0)
        r = pltpu.roll(x, (LANES - span * k) % LANES, 1)
        l = pltpu.roll(row8(self.left, v), LANES - span * k - width, 1)
        return jnp.where(right_mask, r, jnp.where(left_mask, l, 0.0))

    def block(self, first, i, span, width):
        per = LANES // span
        return self.take(first + i // per, i % per, span, width)

    def cell(self, g, kind):
        if g < HALO:
            return self.block(0, 2 * g + kind, SPAN, HALO)
        return self.block(4, 2 * (g - HALO) + kind, SPAN, HALO)

    def power(self, b):
        if b < 2:
            return self.block(0, 2 * HALO + b, SPAN, HALO)
        return self.block(4, 2 * (self.rows - 1 - HALO) + b - 2, SPAN, HALO)

    def field(self, m, f):
        if m < MHALO:
            return self.block(3, 4 * m + f, MSPAN, MHALO)
        first = 4 + far_rows(self.rows)
        if m < self.mrows:
            return self.block(first, 4 * (m - MHALO) + f, MSPAN, MHALO)
        first += -(-4 * (self.mrows - MHALO) * MSPAN // LANES)
        return self.block(first, 4 * (m - self.mrows) + f, MSPAN, MHALO)


def spread_power(ref, n, blocks):
    ref[...] = jnp.zeros(ref.shape, jnp.float32)
    count = ref.shape[0] // (n * 8)
    for first, x in blocks:
        for t, piece in enumerate(tiles(x)):
            ref[pl.ds(8 * (n * t + first), piece.shape[0], stride=8), :] = piece
    return count


def power_row(ref, n, i):
    count = ref.shape[0] // (n * 8)
    return jnp.concatenate([row8(ref, n * t + i) for t in range(count)], axis=1)


def conduct_sum(ref, i, closed=False):
    x = row8(ref, i)
    sub = sub_iota(x.shape[1])
    before, after = prev_lane(x), next_lane(x)
    if closed:
        lane = lax.broadcasted_iota(jnp.int32, x.shape, 1)
        before = jnp.where(lane > 0, before, 0.0)
        after = jnp.where(lane < x.shape[1] - 1, after, 0.0)
    total = row8(ref, i - 1) + row8(ref, i + 1) + before + after
    total = total + jnp.where(sub < DEPTH - 1, next_sub(x), 0.0)
    return total + jnp.where(sub > 0, prev_sub(x), 0.0)


def sink(width):
    return jnp.where(sub_iota(width) == DEPTH - 1, 2.0, 0.2).astype(jnp.float32)


def column_sums(x):
    width = x.shape[1]
    return x + pltpu.roll(x, width - 1, 1) + pltpu.roll(x, width - 2, 1)


def to_solid_layers(y):
    return jnp.where(sub_iota(y.shape[1]) < 3, y, next_sub(y)) * (1.0 / 9.0)


def gather_main(pieces):
    lane = lane_iota()
    out = []
    for j in range(len(pieces) // 3):
        got = None
        for t in range(3):
            g = gather_lanes(pieces[3 * j + t], (3 * lane) & (LANES - 1))
            got = g if got is None else jnp.where((3 * lane) >= LANES * t, g, got)
        out.append(got)
    return out


def gather_sides(piece):
    lane = lane_iota()
    first = LANES - MHALO
    index = jnp.where(lane < MHALO, 3 * lane, jnp.where(lane >= first, LANES - 9 + 3 * (lane - first), 64))
    return gather_lanes(piece, index)


def restrict_main(x):
    return to_solid_layers(jnp.concatenate(gather_main(tiles(column_sums(x))), axis=1))


def restrict_sides(x):
    return to_solid_layers(gather_sides(column_sums(x)))


def restrict_columns(x):
    pieces = tiles(column_sums(x))
    return to_solid_layers(jnp.concatenate(gather_main(pieces[:-1]) + [gather_sides(pieces[-1])], axis=1))


def first_sweep(s_ref, q0_ref, i, power, h, closed=False):
    s = row8(s_ref, i)
    inv = 1.0 / (h + s * conduct_sum(s_ref, i, closed))
    return inv, s * ((power + s * conduct_sum(q0_ref, i, closed)) * inv)


def second_sweep(s_ref, q1_ref, di_ref, i, power, closed=False):
    return (power + row8(s_ref, i) * conduct_sum(q1_ref, i, closed)) * row8(di_ref, i)


def k_inner(n_edges, n_col, rows, tab, w_ref, src_ref, *refs):
    sides = Sides(n_col, rows, rows // 6, refs[0], refs[n_edges - 1])
    s_ref, al_ref, q0_ref, q1_ref, di_ref, t_ref, ea_ref, strain_ref, pw_ref = refs[n_edges:]
    own = rows - 1
    width = src_ref.shape[1] + LANES
    t_s = jnp.sqrt(table_of(tab, 0))
    t_al = table_of(tab, 1)
    v_s = splats(t_s, NMAT)
    side_power = jnp.concatenate([sides.power(k) for k in range(rows // 8)], axis=0)
    n_p = s_ref.shape[0] // 8
    spread_power(pw_ref, n_p, [(FRONT, jnp.concatenate([src_ref[...], side_power], axis=1))])
    h = sink(width)

    for i in range(0, own + 2 * STEP + 2, STEP):
        later = []
        for g in range(i, min(i + STEP, own)):
            temp = jnp.concatenate([w_ref[16 * g : 16 * g + 8, :], sides.cell(g, 0)], axis=1)
            code = jnp.concatenate([w_ref[16 * g + 8 : 16 * g + 16, :], sides.cell(g, 1)], axis=1)
            s, al = choose([v_s], code)[0], lookup(t_al, code)
            later += [(s_ref, FRONT + g, s), (q0_ref, FRONT + g, s * temp), (al_ref, FRONT + g, al)]
        for g in range(max(1, i - STEP - 1), min(i - 1, own - 1)):
            r = FRONT + g
            inv, q1 = first_sweep(s_ref, q0_ref, r, power_row(pw_ref, n_p, r), h)
            later += [(di_ref, r, inv), (q1_ref, r, q1)]
        for g in range(max(2, i - 2 * STEP - 2), min(i - STEP - 2, own - 2)):
            r = FRONT + g
            t2 = second_sweep(s_ref, q1_ref, di_ref, r, power_row(pw_ref, n_p, r))
            later += [(t_ref, r, t2), (ea_ref, r, row8(al_ref, r) * t2)]
        for ref, r, x in later:
            ref[at8(r), :] = x

    def strain(m, carry):
        i = FRONT + 3 * m
        x = row8(ea_ref, i) + row8(ea_ref, i + 1) + row8(ea_ref, i + 2)
        strain_ref[at8(m), :] = restrict_columns(x)
        return carry

    lax.fori_loop(1, (own - 2) // 3, strain, 0, unroll=UNROLL_STRAIN)


def couple_sum(rows3):
    near = [[None] * 3 for _ in range(3)]
    for j in range(3):
        below, mid, above = rows3[j]
        near[0][j] = next_sub(mid) + prev_sub(mid)
        near[1][j] = above + below
        near[2][j] = next_lane(mid) + prev_lane(mid)
    out = []
    for i in range(3):
        j, k = [x for x in range(3) if x != i]
        main = near[i][i] + 0.5 * (near[j][i] + near[k][i])
        side = (near[i][j] + near[j][j]) + (near[i][k] + near[k][k])
        out.append(main + 0.25 * side)
    return out


def moduli(values, code):
    (mod,) = choose([values], code)
    inside = mod > 0.0
    root = jnp.sqrt(mod)
    return mod, root, jnp.where(inside, 1.0 / jnp.where(inside, root, 1.0), 0.0)


def k_mech(n_edges, n_col, rows, tab, mw_ref, *refs):
    sides = Sides(n_col, rows, rows // 6, refs[0], refs[n_edges - 1])
    mi_ref, mod_ref = refs[n_edges : n_edges + 2]
    uu_refs = refs[n_edges + 2 : n_edges + 5]
    pre_refs = refs[n_edges + 5 : n_edges + 8]
    values = splats(table_of(tab, 2), NMAT)
    count = mw_ref.shape[0] // 32
    for m in range(count):
        fields = []
        for f in range(4):
            side = sides.field(m, f)
            fields.append(jnp.concatenate([mw_ref[32 * m + 8 * f : 32 * m + 8 * f + 8, :], side], axis=1))
        mod_ref[at8(m), :], root, mi_ref[at8(m), :] = moduli(values, fields[3])
        for f in range(3):
            uu_refs[f][at8(m), :] = root * fields[f]
    for m in range(1, count - 1):
        near = couple_sum([[row8(r, m - 1), row8(r, m), row8(r, m + 1)] for r in uu_refs])
        for d in range(3):
            pre_refs[d][at8(m), :] = near[d] * (1.0 / STIFF_DIAG) - row8(uu_refs[d], m)


def edge_patch(n_edges, e, corners, zr_ref, mcols, v_s, t_al, scratch):
    s_ref, q0_ref, q1_ref, di_ref = scratch
    side = edge_side(n_edges, e)
    lanes = edge_tile(side, zr_ref.shape[1])
    lane = lane_iota()
    mine = ((lane >= LANES - HALO) & (side == 1)) | ((lane < HALO) & (side == 0))
    zsrc = 16 * NEAR + ZMECH
    per = LANES // SPAN

    def strip(i):
        x = zr_ref[far_place(e, i // per, zr_ref.shape[1], mcols)]
        return pltpu.roll(x, LANES - SPAN * (i % per) - side * HALO, 1)

    def cell(j, kind):
        x = zr_ref[16 * j + 8 * kind : 16 * j + 8 * kind + 8, lanes] if j < NEAR else strip(2 * (j - NEAR) + kind)
        return jnp.where(mine, x, corners.cell(j, kind))

    first = FAR_ROW - 2
    codes = {}
    for j in range(first, HALO):
        codes[j] = cell(j, 1)
        (s,) = choose([v_s], codes[j])
        s_ref[at8(j - first), :] = s
        q0_ref[at8(j - first), :] = s * cell(j, 0)
    power = [
        jnp.where(mine, zr_ref[zsrc : zsrc + 8, lanes], corners.power(0)),
        jnp.where(mine, strip(2 * (HALO - NEAR)), corners.power(1)),
    ]
    top = sub_iota(LANES) == 0
    h = sink(LANES)

    def power_of(j):
        x = power[j // 8][j % 8 : j % 8 + 1, :]
        return jnp.where(top, jnp.broadcast_to(x, (8, LANES)), 0.0)

    for j in range(first + 1, HALO - 1):
        at = at8(j - first)
        di_ref[at, :], q1_ref[at, :] = first_sweep(s_ref, q0_ref, j - first, power_of(j), h)
    out = []
    for f in range(FAR):
        x = None
        for j in range(FAR_ROW + 3 * f, FAR_ROW + 3 * f + 3):
            ea = lookup(t_al, codes[j]) * second_sweep(s_ref, q1_ref, di_ref, j - first, power_of(j))
            x = ea if x is None else x + ea
        out.append(restrict_sides(x))
    return out


def k_outer(n_edges, n_col, rows, tab, zr_ref, *refs):
    sides = Sides(n_col, rows, rows // 6, refs[0], refs[n_edges - 1])
    corners = Sides(n_col, rows, rows // 6, refs[n_edges], refs[2 * n_edges - 1])
    rest = refs[2 * n_edges :]
    s_in, al_in, q0_in, q1_in, di_in, t_in, ea_in, strain_in, src_ref = rest[:9]
    mi_in, mod_in = rest[9:11]
    uu_in, pre_in = rest[11:14], rest[14:17]
    x_ref, keep_ref, u_ref = rest[17:20]
    s_ref, q0_ref, q1_ref, di_ref, al_ref, ea_ref, t_keep, pw_ref = rest[20:28]
    st_ref, mi_ref, mod_ref, sf_ref = rest[28:32]
    uu_refs, p_refs, d_refs = rest[32:35], rest[35:38], rest[38:41]
    own = rows - 1
    wide = zr_ref.shape[1]
    half = wide // 2
    width = wide + LANES
    t_s = jnp.sqrt(table_of(tab, 0))
    t_al = table_of(tab, 1)
    v_s = splats(t_s, NMAT)
    zmech = 16 * NEAR
    zsrc = zmech + ZMECH
    zfar = zsrc + 8
    for g in range(3):
        k = AHEAD - 1 - g
        for dst, src in ((s_ref, s_in), (al_ref, al_in), (q0_ref, q0_in)):
            dst[at8(k), :] = row8(src, FRONT + g)
    ea_ref[at8(AHEAD - 3), :] = row8(ea_in, FRONT + 2)
    for g in (1, 2):
        q1_ref[at8(AHEAD - 1 - g), :] = row8(q1_in, FRONT + g)
    di_ref[at8(AHEAD - 2), :] = row8(di_in, FRONT + 1)
    n_p = s_ref.shape[0] // 8
    near = jnp.concatenate([src_ref[0:8, :], sides.power(0)], axis=1)
    far = jnp.concatenate([zr_ref[zsrc : zsrc + 8, :], corners.power(0)], axis=1)
    spread_power(
        pw_ref,
        n_p,
        [(AHEAD - 1, near[0:1, :]), (AHEAD - 2, near[1:2, :]), (AHEAD, far)],
    )
    h = sink(width)

    for i in range(0, NEAR + 2 * STEP + 1, STEP):
        later = []
        for j in range(i, min(i + STEP, NEAR)):
            temp = jnp.concatenate([zr_ref[16 * j : 16 * j + 8, :], corners.cell(j, 0)], axis=1)
            code = jnp.concatenate([zr_ref[16 * j + 8 : 16 * j + 16, :], corners.cell(j, 1)], axis=1)
            s, al = choose([v_s], code)[0], lookup(t_al, code)
            later += [(s_ref, AHEAD + j, s), (q0_ref, AHEAD + j, s * temp), (al_ref, AHEAD + j, al)]
        for j in range(max(-1, i - STEP - 1), min(i - 1, NEAR - 1)):
            r = AHEAD + j
            inv, q1 = first_sweep(s_ref, q0_ref, r, power_row(pw_ref, n_p, r), h)
            later += [(di_ref, r, inv), (q1_ref, r, q1)]
        for j in range(max(-2, i - 2 * STEP - 2), min(i - STEP - 2, NEAR - 2)):
            r = AHEAD + j
            t2 = second_sweep(s_ref, q1_ref, di_ref, r, power_row(pw_ref, n_p, r))
            later += [(t_keep, r, t2), (ea_ref, r, row8(al_ref, r) * t2)]
        for ref, r, x in later:
            ref[at8(r), :] = x

    core = lax.axis_index(CORE)

    def other_half(x):
        return jnp.where(core == 0, x[:, half:wide], x[:, 0:half])

    def own_half(x):
        return jnp.where(core == 0, x[:, 0:half], x[:, half:wide])

    for g in range(2):
        t2 = row8(t_keep, AHEAD - 1 - g)
        keep_ref[8 * g : 8 * g + 8, :] = own_half(t2)
        x_ref[8 * g : 8 * g + 8, :] = other_half(t2)
    x_ref[16:24, :] = other_half(row8(t_in, FRONT + 2))

    count = mod_in.shape[0] // 8
    mrows = count - MHALO
    mwidth = mod_in.shape[1]
    mcols = mwidth - LANES
    n_m = count + MHALO
    for m in range(MHALO + 1 - FAR):
        i = AHEAD - 3 + 3 * m
        x = row8(ea_ref, i) + row8(ea_ref, i + 1) + row8(ea_ref, i + 2)
        st_ref[at8(MHALO - m), :] = restrict_columns(x)
    lane = lane_iota()
    has_left, has_right = sides.side > 0, sides.side < n_col - 1
    patches = [edge_patch(n_edges, e, corners, zr_ref, mcols, v_s, t_al, rest[41:45]) for e in range(n_edges)]
    for f in range(FAR):
        pieces = tiles(zr_ref[zfar : zfar + 8, mcols * f : mcols * (f + 1)])
        right, left = patches[0][f], patches[-1][f]
        pieces[0] = jnp.where((lane == 0) & has_left, left, pieces[0])
        pieces[-1] = jnp.where((lane == LANES - 1) & has_right, right, pieces[-1])
        beside = jnp.where((lane < MHALO) & has_right, right, jnp.where((lane >= LANES - MHALO) & has_left, left, 0.0))
        st_ref[at8(FAR - 1 - f), :] = jnp.concatenate(pieces + [beside], axis=1)
    for m in range(1, count):
        st_ref[at8(MHALO + m), :] = row8(strain_in, m)
    values = splats(table_of(tab, 2), NMAT)
    for i in range(MHALO):
        j = MHALO - 1 - i
        fields = []
        for f in range(4):
            body = zr_ref[zmech + ML * f : zmech + ML * f + 8, mcols * j : mcols * (j + 1)]
            body = jnp.where(sub_iota(mcols) < ML, body, 0.0)
            side = corners.field(j, f)
            fields.append(jnp.concatenate([body, side], axis=1))
        mod_ref[at8(i), :], root, mi_ref[at8(i), :] = moduli(values, fields[3])
        for f in range(3):
            uu_refs[f][at8(i), :] = root * fields[f]
    for ref, src in zip((mi_ref, mod_ref, *uu_refs), (mi_in, mod_in, *uu_in)):
        ref[8 * MHALO : 8 * n_m, :] = src[...]
    for i in range(n_m):
        sf_ref[at8(i), :] = row8(mod_ref, i) * row8(st_ref, i)
    sign = jnp.where(core == 0, 0.5, -0.5).astype(jnp.float32)
    for i in range(1, n_m - 1):
        load = row8(sf_ref, i)
        force = [
            0.5 * (next_sub(load) - prev_sub(load)),
            sign * (row8(sf_ref, i + 1) - row8(sf_ref, i - 1)),
            0.5 * (next_lane(load) - prev_lane(load)),
        ]
        inv = row8(mi_ref, i)
        inside = inv > 0.0
        if i <= MHALO:
            near = couple_sum([[row8(r, i - 1), row8(r, i), row8(r, i + 1)] for r in uu_refs])
            pre = [near[d] * (1.0 / STIFF_DIAG) - row8(uu_refs[d], i) for d in range(3)]
        else:
            pre = [row8(r, i - MHALO) for r in pre_in]
        inv = inv * (1.0 / STIFF_DIAG)
        for d in range(3):
            p_refs[d][at8(i), :] = jnp.where(inside, force[d] * inv + pre[d], 0.0)
    c_near = 2.0 * RHO1 / DELTA / STIFF_DIAG
    c_self = 1.0 + RHO1 * RHO0
    for i in range(2, n_m - 2):
        near = couple_sum([[row8(r, i - 1), row8(r, i), row8(r, i + 1)] for r in p_refs])
        inv = row8(mi_ref, i)
        for d in range(3):
            moved = row8(uu_refs[d], i) + c_self * row8(p_refs[d], i) + c_near * near[d]
            d_refs[d][at8(i), :] = moved * inv
    sub = sub_iota(mwidth)
    weight = jnp.where(sub < ML, (ML - sub).astype(jnp.float32) * (1.0 / (ML * (ML + 1) / 2.0)), 0.0)
    x_ref[24:32, :] = jnp.zeros((8, x_ref.shape[1]), jnp.float32)
    for g in range(mrows):
        i = MHALO + g
        u0, u2 = row8(d_refs[0], i), row8(d_refs[2], i)
        div = 0.5 * (next_sub(u0) - prev_sub(u0)) + 0.5 * (next_lane(u2) - prev_lane(u2))
        div = div + sign * (row8(d_refs[1], i + 1) - row8(d_refs[1], i - 1))
        stress = row8(mod_ref, i) * (div - 3.0 * row8(st_ref, i))
        die = jnp.sum(weight * stress, axis=0, keepdims=True)
        first, second = die[:, 0:LANES], die[:, LANES : 2 * LANES]
        keep_ref[16 + g : 17 + g, 0:LANES] = jnp.where(core == 0, first, second)
        x_ref[24 + g : 25 + g, 0:LANES] = jnp.where(core == 0, second, first)
        for d in range(3):
            u_ref[8 * (mrows * d + g) : 8 * (mrows * d + g) + 8, :] = row8(d_refs[d], i)[:, 0:mcols]


def k_out(rows, mrows, t_in, keep_ref, xr_ref, u_in, t_out, u_out, slow_ref, buf, die, wide_die, ubuf):
    half = slow_ref.shape[1]
    mcols = u_in.shape[1]
    core = lax.axis_index(CORE)

    def put(ref, at, x):
        count = ref.shape[0] * LANES // x.shape[1]
        for t, piece in enumerate(tiles(x)):
            ref[count * t + at : count * t + at + piece.shape[0], :] = piece

    def build(rev):
        lo = half if rev else 0
        for g in range(rows):
            i = rows - 1 - g if rev else g
            if g < 2:
                x = keep_ref[8 * g : 8 * g + 8, :]
            elif g < rows - 3:
                x = t_in[8 * (FRONT + g) : 8 * (FRONT + g) + 8, lo : lo + half]
            else:
                k = rows - 1 - g
                x = xr_ref[8 * k : 8 * k + 8, :]
            put(buf, 8 * i, x)
        for g in range(mrows):
            mine = 2 * mrows - 1 - g if rev else g
            theirs = g if rev else 2 * mrows - 1 - g
            die[mine : mine + 1, :] = keep_ref[16 + g : 17 + g, 0:LANES]
            die[theirs : theirs + 1, :] = xr_ref[24 + g : 25 + g, 0:LANES]
            for d in range(3):
                i = mrows - 1 - g if rev else g
                put(ubuf, 8 * (mrows * d + i), row8(u_in, mrows * d + g))

    @pl.when(core == 0)
    def _():
        build(False)

    @pl.when(core != 0)
    def _():
        build(True)

    for t in range(half // LANES):
        at = 8 * rows * t
        for l in range(DEPTH):
            t_out[l, :, tile_lanes(t)] = buf[pl.ds(at + l, rows, stride=8), :]
    for t in range(mcols // LANES):
        for d in range(3):
            for l in range(ML):
                u_out[d, l, :, tile_lanes(t)] = ubuf[pl.ds(8 * mrows * (3 * t + d) + l, mrows, stride=8), :]
    lane = lane_iota(2 * mrows)
    for t in range(half // LANES):
        x = gather_lanes(die[...], (lane + LANES * t) // 3)
        for b in range(3):
            wide_die[pl.ds(b, 2 * mrows, stride=3), :] = x
        slow = 1.0 + 0.2 * buf[pl.ds(8 * rows * t, rows, stride=8), :] + 0.5 * wide_die[...]
        slow_ref[:, tile_lanes(t)] = slow


def pairs(dims, sends):
    index = {}
    for r in range(dims[0]):
        for c in range(dims[1]):
            for a in range(dims[2]):
                index[(r, c, a)] = (r * dims[1] + c) * dims[2] + a
    out = []
    for source in index:
        target = sends(*source)
        if target in index:
            out.append((index[source], index[target]))
    return out


def per_device(temp, ids, power, mat, offset, heat_table, growth_table, modulus_table):
    axes = ("row", "col", "lay")
    dims = tuple(lax.axis_size(x) for x in axes)
    n_col = dims[1]
    _, rows, half = temp.shape
    _, _, mrows, mcols = offset.shape
    n_edges = 1 if n_col == 2 else 2
    n_t = half // LANES
    m_t = mcols // LANES

    def send(x, sends):
        return lax.ppermute(x, axes, pairs(dims, sends))

    def swap(r, c, a):
        return (r, c, 1 - a)

    def along(r, c, a):
        return (r + 1, c, 0) if a == 1 else (r - 1, c, 1)

    wide = 2 * half
    own = rows - 1
    kind = lax.broadcasted_iota(jnp.int32, (2, *temp.shape), 0)
    both = jnp.where(kind == 0, temp[None], power[None, None])
    tab = jnp.stack([heat_table, growth_table, modulus_table])
    tab = jnp.pad(tab, ((0, 0), (1, LANES - 1 - tab.shape[1])))
    n = 16 * HALO
    n_far = 8 * far_rows(rows)
    cells, one = call(k_rows, [(16 * rows * n_t, LANES), ((n + 16) * n_t + n_far, LANES)], [both, ids])
    got1 = send(one, swap)
    two, mg, strip = call(
        functools.partial(k_rest, n_edges),
        [
            ((16 * (rows - HALO) + rows - 16) * n_t + 32 * MHALO * m_t, LANES),
            (32 * mrows, mcols),
            (8 * n_edges, LANES),
        ],
        [both, cells, offset, mat],
        scratch=[(32 * mrows * m_t, LANES)],
    )
    strip = send(strip, swap)
    got2 = send(two, swap)
    n_c = 32 + n_far - 8 * (-4 * (mrows - MHALO) * MSPAN // LANES) + 8
    z, first_rows, *edges = call(
        functools.partial(k_edge, n_edges),
        [(far_place(n_edges, -1, wide, mcols)[0].stop, wide), (n + 16, wide)] + [(n_c, LANES), (32, LANES)] * n_edges,
        [tab, both, cells, got1, mg, strip],
        cost=EDGE_COST,
        scratch=[(8 * HALO, wide)] * 4,
    )
    leaving = [z, *edges]
    w, src, mw, z, *edges = call(
        functools.partial(k_chip, rows),
        [(16 * rows, wide), (rows, wide), (32 * (mrows + MHALO), mcols)] + [x.shape for x in leaving],
        [both, cells, got2, mg, first_rows] + leaving,
        aliases={5 + k: 3 + k for k in range(len(leaving))},
    )
    zr = send(z, along)
    if n_edges == 1:
        sides = [send(edges[0], lambda r, c, a: (r, 1 - c, a))]
        corners = [send(edges[1], lambda r, c, a: along(r, 1 - c, a))]
    else:
        sides = [send(edges[0], lambda r, c, a: (r, c + 1, a)), send(edges[2], lambda r, c, a: (r, c - 1, a))]
        corners = [
            send(edges[1], lambda r, c, a: along(r, c + 1, a)),
            send(edges[3], lambda r, c, a: along(r, c - 1, a)),
        ]
    width = wide + LANES
    mwidth = mcols + LANES
    n_w = 8 * (rows + FRONT + 4)
    inner = call(
        functools.partial(k_inner, n_edges, n_col, rows),
        [(n_w, width)] * 7 + [(8 * (mrows + MHALO), mwidth)],
        [tab, w, src] + sides,
        scratch=[(n_w * (width // LANES), LANES)],
    )
    t2 = inner[5]
    solid = call(
        functools.partial(k_mech, n_edges, n_col, rows), [(8 * (mrows + MHALO), mwidth)] * 8, [tab, mw] + sides
    )
    n_h = 8 * (AHEAD + HALO + 5)
    n_m = 8 * (mrows + 2 * MHALO)
    x, keep, u = call(
        functools.partial(k_outer, n_edges, n_col, rows),
        [(32, half), (24, half), (24 * mrows, mcols)],
        [tab, zr] + sides + corners + list(inner) + [src] + list(solid),
        scratch=[(n_h, width)] * 7
        + [(n_h * (width // LANES), LANES)]
        + [(n_m, mwidth)] * 13
        + [(8 * HALO, LANES)] * 4,
    )
    xr = send(x, swap)
    t_out, u_out, slow = call(
        functools.partial(k_out, rows, mrows),
        [temp.shape, offset.shape, power.shape],
        [t2, keep, xr, u],
        scratch=[
            (8 * rows * n_t, LANES),
            (2 * mrows, LANES),
            (rows, LANES),
            (24 * mrows * m_t, LANES),
        ],
    )
    return t_out, u_out, slow


def solution(mesh):
    placed = (
        P("grp", "row", ("col", "lay")),
        P("grp", "row", ("col", "lay")),
        P(("grp", "row"), ("col", "lay")),
        P("grp", ("row", "lay"), "col"),
        P(None, "grp", ("row", "lay"), "col"),
        P(),
        P(),
        P(),
    )
    return jax.shard_map(
        per_device,
        mesh=mesh,
        in_specs=placed,
        out_specs=(
            P("grp", "row", ("col", "lay")),
            P(None, "grp", ("row", "lay"), "col"),
            P(("grp", "row"), ("col", "lay")),
        ),
        check_vma=False,
    )
```

```python
import functools

import jax
import jax.numpy as jnp
from jax import lax
from jax.experimental import pallas as pl
from jax.experimental.pallas import tpu as pltpu
from jax.sharding import PartitionSpec as P

DEPTH = 8
ML = 6
LANES = 128
HALO = 11
MHALO = 3

STIFF_DIAG = 12.0
THETA = 1.0
DELTA = 0.75
SIGMA = THETA / DELTA
RHO0 = 1.0 / SIGMA
RHO1 = 1.0 / (2.0 * SIGMA - RHO0)

VMEM = pl.BlockSpec(memory_space=pltpu.VMEM)
FRONT = 9
AHEAD = 5
STEP = 3
SPAN = 11
MSPAN = 8
NMAT = 16
FAR = 2
EDGE_COST = 10**10
FAR_ROW = 9 - 3 * FAR
KEEP = 3
Z_TEMP, Z_CODE, Z_HEAT, Z_STRAIN, Z_SOLID, Z_POWER, Z_FAR = 0, 16, 40, 56, 64, 88, 96
CORE = "lay"
UNROLL_STRAIN = 3


def call(kernel, outs, args, scratch=(), specs=None, aliases=None, cost=0):
    return pl.pallas_call(
        kernel,
        out_shape=[jax.ShapeDtypeStruct(s, jnp.float32) for s in outs],
        in_specs=specs or [VMEM] * len(args),
        out_specs=[VMEM] * len(outs),
        input_output_aliases=aliases or {},
        cost_estimate=pl.CostEstimate(flops=cost, bytes_accessed=0, transcendentals=0) if cost else None,
        scratch_shapes=[pltpu.VMEM(s, jnp.float32) if isinstance(s, tuple) else s for s in scratch],
        compiler_params=pltpu.CompilerParams(vmem_limit_bytes=16 * 1024 * 1024),
    )(*args)


def lane_iota(rows=8):
    return lax.broadcasted_iota(jnp.int32, (rows, LANES), 1)


def sub_iota(width):
    return lax.broadcasted_iota(jnp.int32, (8, width), 0)


def tile_lanes(t):
    return slice(LANES * t, LANES * (t + 1))


def tiles(x):
    return [x[:, tile_lanes(t)] for t in range(x.shape[1] // LANES)]


def table_of(ref, k):
    return jnp.broadcast_to(ref[k : k + 1, :], (8, LANES))


def gather_lanes(table, index):
    return jnp.take_along_axis(table, index, axis=1, mode="promise_in_bounds")


def lookup(table, code):
    return jnp.concatenate([gather_lanes(table, c.astype(jnp.int32)) for c in tiles(code)], axis=1)


def splats(table, count):
    return [jnp.broadcast_to(table[:, m : m + 1], (8, LANES)) for m in range(count + 1)]


def choose(lists, code):
    out = [[] for _ in lists]
    for c in tiles(code):
        c = c.astype(jnp.int32)
        bits = [(c & (1 << k)) != 0 for k in range(5)]
        for n, values in enumerate(lists):
            level = values[:16]
            for k in range(4):
                level = [jnp.where(bits[k], b, a) for a, b in zip(level[::2], level[1::2])]
            out[n].append(jnp.where(bits[4], values[16], level[0]))
    return [jnp.concatenate(x, axis=1) for x in out]


def prev_lane(x):
    return pltpu.roll(x, 1, 1)


def next_lane(x):
    return pltpu.roll(x, x.shape[1] - 1, 1)


def prev_sub(x):
    return pltpu.roll(x, 1, 0)


def next_sub(x):
    return pltpu.roll(x, 7, 0)


def at8(i):
    return pl.ds(8 * i, 8) if isinstance(i, int) else pl.ds(pl.multiple_of(8 * i, 8), 8)


def row8(ref, i):
    return ref[at8(i), :]


def turned(core, last, g):
    return core * last + (1 - 2 * core) * g


def k_rows(in_ref, id_ref, a_ref, one_ref):
    core = lax.axis_index(CORE)
    other = 1 - core
    rows = in_ref.shape[2]
    n_t = in_ref.shape[3] // LANES
    n = 16 * HALO
    for t in range(n_t):
        at = 16 * rows * t
        for l in range(DEPTH):
            a_ref[pl.ds(at + l, rows, stride=16), :] = in_ref[0, l, :, tile_lanes(t)]
            a_ref[pl.ds(at + DEPTH + l, rows, stride=16), :] = (id_ref[l, :, tile_lanes(t)] + 1).astype(jnp.float32)
    for t in range(n_t):
        to = (n + 16) * t
        for g in range(HALO):
            i = 16 * (rows * t + turned(other, rows - 1, g))
            one_ref[to + 16 * g : to + 16 * g + 16, :] = a_ref[pl.ds(pl.multiple_of(i, 16), 16), :]
        for b in range(2):
            one_ref[to + n + 8 * b : to + n + 8 * b + 8, :] = power_rows(in_ref, other, b, t)
    for k, x in enumerate(far_strip(in_ref, a_ref, other, core * (n_t - 1), core)):
        to = (n + 16) * n_t + 8 * k
        one_ref[to : to + 8, :] = x


def k_rest(n_edges, in_ref, a_ref, u_ref, mat_ref, two_ref, mg_ref, m_ref):
    core = lax.axis_index(CORE)
    other = 1 - core
    rows = in_ref.shape[2]
    n_t = in_ref.shape[3] // LANES
    mrows = mat_ref.shape[1]
    mcols = mat_ref.shape[2]
    m_t = mcols // LANES
    m_ref[...] = jnp.zeros(m_ref.shape, jnp.float32)
    for t in range(m_t):
        at = 32 * mrows * t
        for l in range(ML):
            for f in range(3):
                m_ref[pl.ds(at + 8 * f + l, mrows, stride=32), :] = u_ref[f, l, :, tile_lanes(t)]
            m_ref[pl.ds(at + 24 + l, mrows, stride=32), :] = (mat_ref[l, :, tile_lanes(t)] + 1).astype(jnp.float32)
        for g in range(mrows):
            i = 32 * (mrows * t + turned(core, mrows - 1, g))
            mg_ref[32 * g : 32 * g + 32, tile_lanes(t)] = m_ref[pl.ds(pl.multiple_of(i, 32), 32), :]
    for e in range(n_edges):
        side = edge_side(n_edges, e)
        fields = []
        for g in range(MHALO):
            i = 32 * (mrows * side * (m_t - 1) + turned(core, mrows - 1, mrows - 1 - g))
            fields += [m_ref[pl.ds(pl.multiple_of(i + 8 * f, 8), 8), :] for f in range(4)]
        at = two_ref.shape[0] - 8 * (n_edges - e)
        (two_ref[at : at + 8, :],) = packed(side, fields, MSPAN, MHALO)
    rest = 16 * (rows - HALO)
    for t in range(n_t):
        to = (rest + rows - 16) * t
        for g in range(HALO, rows):
            i = 16 * (rows * t + turned(other, rows - 1, g))
            k = to + 16 * (g - HALO)
            two_ref[k : k + 16, :] = a_ref[pl.ds(pl.multiple_of(i, 16), 16), :]
        for b in range(2, rows // 8):
            two_ref[to + rest + 8 * (b - 2) : to + rest + 8 * (b - 1), :] = power_rows(in_ref, other, b, t)
    for t in range(m_t):
        for g in range(MHALO):
            i = 32 * (mrows * t + turned(core, mrows - 1, mrows - 1 - g))
            k = (rest + rows - 16) * n_t + 32 * (MHALO * t + g)
            two_ref[k : k + 32, :] = m_ref[pl.ds(pl.multiple_of(i, 32), 32), :]


def power_rows(in_ref, turn, b, t):
    rows = in_ref.shape[2]
    lanes = tile_lanes(t) if isinstance(t, int) else pl.ds(pl.multiple_of(LANES * t, LANES), LANES)
    x = in_ref[1, 0, at8(turned(turn, rows // 8 - 1, b)), lanes]
    return jnp.take_along_axis(x, turned(turn, 7, sub_iota(LANES)), axis=0, mode="promise_in_bounds")


def far_strip(in_ref, a_ref, turn, t, side):
    rows = in_ref.shape[2]
    blocks = []
    for g in range(HALO, rows - 1):
        i = 16 * (rows * t + turned(turn, rows - 1, g))
        blocks += [a_ref[pl.ds(pl.multiple_of(i + k, 8), 8), :] for k in (0, 8)]
    blocks += [power_rows(in_ref, turn, b, t) for b in range(2, rows // 8)]
    return packed(side, blocks, SPAN, HALO)


def edge_side(n_edges, e):
    return 1 - lax.axis_index("col") if n_edges == 1 else 1 - e


def edge_tile(side, width):
    if isinstance(side, int):
        return tile_lanes(side * (width // LANES - 1))
    return pl.ds(pl.multiple_of(side * (width - LANES), LANES), LANES)


def packed(side, blocks, span, keep):
    lane = lane_iota()
    per = LANES // span
    out = []
    for i in range(0, len(blocks), per):
        acc = jnp.zeros((8, LANES), jnp.float32)
        for k, x in enumerate(blocks[i : i + per]):
            acc = jnp.where(lane // span == k, pltpu.roll(x, span * k + side * keep, 1), acc)
        out.append(acc)
    return out


def far_rows(rows):
    return -(-(2 * (rows - 1 - HALO) + rows // 8 - 2) // (LANES // SPAN))


def k_edge(n_edges, tab, in_ref, a_ref, got_ref, mg_ref, z_ref, w_ref, *refs):
    core = lax.axis_index(CORE)
    wide = z_ref.shape[1]
    n_t = wide // LANES // 2
    rows = in_ref.shape[2]
    mcols = mg_ref.shape[1]
    n = 16 * HALO
    edge_refs, (s_ref, q0_ref, q1_ref, di_ref) = refs[:n_edges], refs[n_edges:]

    def build(first):
        for t in range(n_t):
            lanes = tile_lanes(t if first else n_t + t)
            for g in range(HALO):
                i = 16 * (rows * t + (g if first else rows - 1 - g))
                w_ref[16 * g : 16 * g + 16, lanes] = a_ref[i : i + 16, :]
            for b in range(2):
                w_ref[n + 8 * b : n + 8 * b + 8, lanes] = power_rows(in_ref, 0 if first else 1, b, t)
            lanes = tile_lanes(n_t + t if first else t)
            at = (n + 16) * t
            w_ref[0 : n + 16, lanes] = got_ref[at : at + n + 16, :]

    @pl.when(core == 0)
    def _():
        build(True)

    @pl.when(core != 0)
    def _():
        build(False)

    for g in range(2):
        z_ref[Z_TEMP + 8 * g : Z_TEMP + 8 * g + 8, :] = w_ref[16 * g : 16 * g + 8, :]
    for g in range(3):
        z_ref[Z_CODE + 8 * g : Z_CODE + 8 * g + 8, :] = w_ref[16 * g + 8 : 16 * g + 16, :]
    z_ref[Z_POWER : Z_POWER + 8, :] = w_ref[n : n + 8, :]
    z_ref[Z_FAR:, :] = jnp.zeros((z_ref.shape[0] - Z_FAR, wide), jnp.float32)
    for g in range(MHALO):
        for f in range(4):
            at = Z_SOLID + ML * f
            z_ref[at : at + ML, mcols * g : mcols * (g + 1)] = mg_ref[32 * g + 8 * f : 32 * g + 8 * f + ML, :]
    for e in range(n_edges):
        side = edge_side(n_edges, e)
        lanes, mlanes = edge_tile(side, wide), edge_tile(side, mcols)
        blocks = [w_ref[8 * i : 8 * i + 8, lanes] for i in range(2 * HALO)]
        blocks += [w_ref[n + 8 * b : n + 8 * b + 8, lanes] for b in range(2)]
        fields = [mg_ref[8 * i : 8 * i + 8, mlanes] for i in range(4 * MHALO)]
        near = packed(side, blocks, SPAN, HALO) + packed(side, fields, MSPAN, MHALO)
        strip = blocks[4 : 2 * HALO : 2] + blocks[7 : 2 * HALO : 2] + blocks[2 * HALO + 1 :]
        for k, x in enumerate(packed(side, strip, SPAN, HALO)):
            z_ref[far_place(e, k, wide, mcols)] = x
        for k, x in enumerate(near):
            edge_refs[e][8 * k : 8 * k + 8, :] = x
    t_s = jnp.sqrt(table_of(tab, 0))
    t_al = table_of(tab, 1)
    v_s = splats(t_s, NMAT)
    codes = {}
    for g in range(HALO):
        codes[g] = w_ref[16 * g + 8 : 16 * g + 16, :]
        x = lookup(t_s, codes[g]) if g % 2 else choose([v_s], codes[g])[0]
        s_ref[at8(g), :] = x
        q0_ref[at8(g), :] = x * w_ref[16 * g : 16 * g + 8, :]
    h = sink(wide)
    top = sub_iota(wide) == 0
    powers = {
        g: jnp.where(top, jnp.broadcast_to(w_ref[n + g : n + g + 1, :], (8, wide)), 0.0) for g in range(1, HALO - 1)
    }
    for g in range(1, HALO - 1):
        di_ref[at8(g), :], q1_ref[at8(g), :] = first_sweep(s_ref, q0_ref, g, powers[g], h, True)
    z_ref[Z_HEAT : Z_HEAT + 16, :] = q1_ref[8:24, :]

    def expansion(g):
        return lookup(t_al, codes[g]) * second_sweep(s_ref, q1_ref, di_ref, g, powers[g], True)

    z_ref[Z_STRAIN : Z_STRAIN + 8, :] = expansion(2)
    for f in range(FAR):
        g = FAR_ROW + 3 * f
        x = expansion(g) + expansion(g + 1) + expansion(g + 2)
        z_ref[Z_FAR : Z_FAR + 8, mcols * f : mcols * (f + 1)] = restrict_main(x)


def far_tiles():
    return -(-(2 * HALO - 4) // (LANES // SPAN))


def far_place(e, k, wide, mcols):
    q = FAR * mcols // LANES + far_tiles() * e + k
    at = Z_FAR + 8 * (q // (wide // LANES))
    return slice(at, at + 8), tile_lanes(q % (wide // LANES))


def k_beside(n_edges, rows, in_ref, a_ref, one_ref, got_ref, mg_ref, z_ref, *refs):
    near_refs, c_refs = refs[:n_edges], refs[n_edges : 2 * n_edges]
    core = lax.axis_index(CORE)
    n_t = in_ref.shape[3] // LANES
    mrows = mg_ref.shape[0] // 32
    n = 16 * HALO
    for e in range(n_edges):
        side = edge_side(n_edges, e)
        mlanes = edge_tile(side, mg_ref.shape[1])
        fields = [mg_ref[8 * i : 8 * i + 8, mlanes] for i in range(4 * MHALO, 4 * mrows)]
        far = [near_refs[e][8 * k : 8 * k + 8, :] for k in range(4)]
        for k, x in enumerate(far_strip(in_ref, a_ref, core, side * (n_t - 1), side)):
            at = (n + 16) * n_t + 8 * k
            far.append(jnp.where(core == side, x, one_ref[at : at + 8, :]))
        far += packed(side, fields, MSPAN, MHALO)
        at = got_ref.shape[0] - 8 * (n_edges - e)
        far.append(got_ref[at : at + 8, :])
        for k, x in enumerate(far):
            c_refs[e][8 * k : 8 * k + 8, :] = x


def k_chip(rows, in_ref, a_ref, got_ref, mg_ref, first_ref, w_ref, src_ref, mw_ref):
    core = lax.axis_index(CORE)
    n_t = w_ref.shape[1] // LANES // 2
    mrows = mg_ref.shape[0] // 32
    n = 16 * HALO
    rest = 16 * (rows - HALO)
    w_ref[0:n, :] = first_ref[0:n, :]
    src_ref[0:16, :] = first_ref[n : n + 16, :]

    def build(first):
        for t in range(n_t):
            lanes = tile_lanes(t if first else n_t + t)
            for g in range(HALO, rows):
                i = 16 * (rows * t + (g if first else rows - 1 - g))
                w_ref[16 * g : 16 * g + 16, lanes] = a_ref[i : i + 16, :]
            for b in range(2, rows // 8):
                src_ref[8 * b : 8 * b + 8, lanes] = power_rows(in_ref, 0 if first else 1, b, t)
            lanes = tile_lanes(n_t + t if first else t)
            at = (rest + rows - 16) * t
            w_ref[n : n + rest, lanes] = got_ref[at : at + rest, :]
            src_ref[16:rows, lanes] = got_ref[at + rest : at + rest + rows - 16, :]

    @pl.when(core == 0)
    def _():
        build(True)

    @pl.when(core != 0)
    def _():
        build(False)

    mw_ref[0 : 32 * mrows, :] = mg_ref[...]
    for t in range(mw_ref.shape[1] // LANES):
        at = (rest + rows - 16) * n_t + 32 * MHALO * t
        mw_ref[32 * mrows : 32 * (mrows + MHALO), tile_lanes(t)] = got_ref[at : at + 32 * MHALO, :]


class Sides:
    def __init__(self, n_col, rows, mrows, from_left, from_right):
        self.left = from_left
        self.right = from_right
        self.rows = rows
        self.mrows = mrows
        lane = lane_iota()
        col = lax.axis_index("col")
        self.masks = {
            w: ((lane < w) & (col < n_col - 1), (lane >= LANES - w) & (col > 0)) for w in (HALO, MHALO)
        }
        self.only = self.left is self.right
        self.side = col

    def take(self, v, k, span, width):
        right_mask, left_mask = self.masks[width]
        x = row8(self.right, v)
        if self.only:
            x = pltpu.roll(x, LANES - span * k - self.side * width, 1)
            return jnp.where(right_mask | left_mask, x, 0.0)
        r = pltpu.roll(x, (LANES - span * k) % LANES, 1)
        l = pltpu.roll(row8(self.left, v), LANES - span * k - width, 1)
        return jnp.where(right_mask, r, jnp.where(left_mask, l, 0.0))

    def block(self, first, i, span, width):
        per = LANES // span
        return self.take(first + i // per, i % per, span, width)

    def cell(self, g, kind):
        if g < HALO:
            return self.block(0, 2 * g + kind, SPAN, HALO)
        return self.block(4, 2 * (g - HALO) + kind, SPAN, HALO)

    def power(self, b):
        if b < 2:
            return self.block(0, 2 * HALO + b, SPAN, HALO)
        return self.block(4, 2 * (self.rows - 1 - HALO) + b - 2, SPAN, HALO)

    def field(self, m, f):
        if m < MHALO:
            return self.block(3, 4 * m + f, MSPAN, MHALO)
        first = 4 + far_rows(self.rows)
        if m < self.mrows:
            return self.block(first, 4 * (m - MHALO) + f, MSPAN, MHALO)
        first += -(-4 * (self.mrows - MHALO) * MSPAN // LANES)
        return self.block(first, 4 * (m - self.mrows) + f, MSPAN, MHALO)


def spread_power(ref, n, blocks):
    ref[...] = jnp.zeros(ref.shape, jnp.float32)
    count = ref.shape[0] // (n * 8)
    for first, x in blocks:
        for t, piece in enumerate(tiles(x)):
            ref[pl.ds(8 * (n * t + first), piece.shape[0], stride=8), :] = piece
    return count


def power_row(ref, n, i):
    count = ref.shape[0] // (n * 8)
    return jnp.concatenate([row8(ref, n * t + i) for t in range(count)], axis=1)


def conduct_sum(ref, i, closed=False):
    x = row8(ref, i)
    sub = sub_iota(x.shape[1])
    before, after = prev_lane(x), next_lane(x)
    if closed:
        lane = lax.broadcasted_iota(jnp.int32, x.shape, 1)
        before = jnp.where(lane > 0, before, 0.0)
        after = jnp.where(lane < x.shape[1] - 1, after, 0.0)
    total = row8(ref, i - 1) + row8(ref, i + 1) + before + after
    total = total + jnp.where(sub < DEPTH - 1, next_sub(x), 0.0)
    return total + jnp.where(sub > 0, prev_sub(x), 0.0)


def sink(width):
    return jnp.where(sub_iota(width) == DEPTH - 1, 2.0, 0.2).astype(jnp.float32)


def column_sums(x):
    width = x.shape[1]
    return x + pltpu.roll(x, width - 1, 1) + pltpu.roll(x, width - 2, 1)


def to_solid_layers(y):
    return jnp.where(sub_iota(y.shape[1]) < 3, y, next_sub(y)) * (1.0 / 9.0)


def gather_main(pieces):
    lane = lane_iota()
    out = []
    for j in range(len(pieces) // 3):
        got = None
        for t in range(3):
            g = gather_lanes(pieces[3 * j + t], (3 * lane) & (LANES - 1))
            got = g if got is None else jnp.where((3 * lane) >= LANES * t, g, got)
        out.append(got)
    return out


def gather_sides(piece):
    lane = lane_iota()
    first = LANES - MHALO
    index = jnp.where(lane < MHALO, 3 * lane, jnp.where(lane >= first, LANES - 9 + 3 * (lane - first), 64))
    return gather_lanes(piece, index)


def restrict_main(x):
    return to_solid_layers(jnp.concatenate(gather_main(tiles(column_sums(x))), axis=1))


def restrict_sides(x):
    return to_solid_layers(gather_sides(column_sums(x)))


def restrict_columns(x):
    pieces = tiles(column_sums(x))
    return to_solid_layers(jnp.concatenate(gather_main(pieces[:-1]) + [gather_sides(pieces[-1])], axis=1))


def first_sweep(s_ref, q0_ref, i, power, h, closed=False):
    s = row8(s_ref, i)
    inv = 1.0 / (h + s * conduct_sum(s_ref, i, closed))
    return inv, s * ((power + s * conduct_sum(q0_ref, i, closed)) * inv)


def second_sweep(s_ref, q1_ref, di_ref, i, power, closed=False):
    return (power + row8(s_ref, i) * conduct_sum(q1_ref, i, closed)) * row8(di_ref, i)


def k_inner(n_edges, n_col, rows, tab, w_ref, src_ref, *refs):
    sides = Sides(n_col, rows, rows // 6, refs[0], refs[n_edges - 1])
    s_ref, al_ref, q0_ref, q1_ref, di_ref, t_ref, ea_ref, strain_ref, pw_ref = refs[n_edges:]
    own = rows - 1
    width = src_ref.shape[1] + LANES
    t_s = jnp.sqrt(table_of(tab, 0))
    t_al = table_of(tab, 1)
    v_s = splats(t_s, NMAT)
    side_power = jnp.concatenate([sides.power(k) for k in range(rows // 8)], axis=0)
    n_p = s_ref.shape[0] // 8
    spread_power(pw_ref, n_p, [(FRONT, jnp.concatenate([src_ref[...], side_power], axis=1))])
    h = sink(width)

    for i in range(0, own + 2 * STEP + 2, STEP):
        later = []
        for g in range(i, min(i + STEP, own)):
            temp = jnp.concatenate([w_ref[16 * g : 16 * g + 8, :], sides.cell(g, 0)], axis=1)
            code = jnp.concatenate([w_ref[16 * g + 8 : 16 * g + 16, :], sides.cell(g, 1)], axis=1)
            s, al = choose([v_s], code)[0], lookup(t_al, code)
            later += [(s_ref, FRONT + g, s), (q0_ref, FRONT + g, s * temp), (al_ref, FRONT + g, al)]
        for g in range(max(1, i - STEP - 1), min(i - 1, own - 1)):
            r = FRONT + g
            inv, q1 = first_sweep(s_ref, q0_ref, r, power_row(pw_ref, n_p, r), h)
            later += [(di_ref, r, inv), (q1_ref, r, q1)]
        for g in range(max(2, i - 2 * STEP - 2), min(i - STEP - 2, own - 2)):
            r = FRONT + g
            t2 = second_sweep(s_ref, q1_ref, di_ref, r, power_row(pw_ref, n_p, r))
            later += [(t_ref, r, t2), (ea_ref, r, row8(al_ref, r) * t2)]
        for ref, r, x in later:
            ref[at8(r), :] = x

    def strain(m, carry):
        i = FRONT + 3 * m
        x = row8(ea_ref, i) + row8(ea_ref, i + 1) + row8(ea_ref, i + 2)
        strain_ref[at8(m), :] = restrict_columns(x)
        return carry

    lax.fori_loop(1, (own - 2) // 3, strain, 0, unroll=UNROLL_STRAIN)


def couple_sum(rows3):
    near = [[None] * 3 for _ in range(3)]
    for j in range(3):
        below, mid, above = rows3[j]
        near[0][j] = next_sub(mid) + prev_sub(mid)
        near[1][j] = above + below
        near[2][j] = next_lane(mid) + prev_lane(mid)
    out = []
    for i in range(3):
        j, k = [x for x in range(3) if x != i]
        main = near[i][i] + 0.5 * (near[j][i] + near[k][i])
        side = (near[i][j] + near[j][j]) + (near[i][k] + near[k][k])
        out.append(main + 0.25 * side)
    return out


def moduli(values, code):
    (mod,) = choose([values], code)
    inside = mod > 0.0
    root = jnp.sqrt(mod)
    return mod, root, jnp.where(inside, 1.0 / jnp.where(inside, root, 1.0), 0.0)


def k_mech(n_edges, n_col, rows, tab, mw_ref, *refs):
    sides = Sides(n_col, rows, rows // 6, refs[0], refs[n_edges - 1])
    mi_ref, mod_ref = refs[n_edges : n_edges + 2]
    uu_refs = refs[n_edges + 2 : n_edges + 5]
    pre_refs = refs[n_edges + 5 : n_edges + 8]
    values = splats(table_of(tab, 2), NMAT)
    count = mw_ref.shape[0] // 32
    for m in range(count):
        fields = []
        for f in range(4):
            side = sides.field(m, f)
            fields.append(jnp.concatenate([mw_ref[32 * m + 8 * f : 32 * m + 8 * f + 8, :], side], axis=1))
        mod_ref[at8(m), :], root, mi_ref[at8(m), :] = moduli(values, fields[3])
        for f in range(3):
            uu_refs[f][at8(m), :] = root * fields[f]
    for m in range(1, count - 1):
        near = couple_sum([[row8(r, m - 1), row8(r, m), row8(r, m + 1)] for r in uu_refs])
        for d in range(3):
            pre_refs[d][at8(m), :] = near[d] * (1.0 / STIFF_DIAG) - row8(uu_refs[d], m)


def edge_patch(n_edges, e, corners, zr_ref, mcols, v_s, t_al, scratch):
    s_ref, q0_ref, q1_ref, di_ref = scratch
    side = edge_side(n_edges, e)
    lanes = edge_tile(side, zr_ref.shape[1])
    lane = lane_iota()
    mine = ((lane >= LANES - HALO) & (side == 1)) | ((lane < HALO) & (side == 0))
    per = LANES // SPAN

    def strip(i):
        x = zr_ref[far_place(e, i // per, zr_ref.shape[1], mcols)]
        return pltpu.roll(x, LANES - SPAN * (i % per) - side * HALO, 1)

    def cell(j, kind):
        held = 2 + kind
        if j < held:
            at = (Z_TEMP, Z_CODE)[kind] + 8 * j
            x = zr_ref[at : at + 8, lanes]
        else:
            x = strip(kind * (HALO - 2) + j - held)
        return jnp.where(mine, x, corners.cell(j, kind))

    codes = {}
    for j in range(HALO):
        codes[j] = cell(j, 1)
        (s,) = choose([v_s], codes[j])
        s_ref[at8(j), :] = s
        q0_ref[at8(j), :] = s * cell(j, 0)
    power = [
        jnp.where(mine, zr_ref[Z_POWER : Z_POWER + 8, lanes], corners.power(0)),
        jnp.where(mine, strip(2 * HALO - 5), corners.power(1)),
    ]
    top = sub_iota(LANES) == 0
    h = sink(LANES)

    def power_of(j):
        x = power[j // 8][j % 8 : j % 8 + 1, :]
        return jnp.where(top, jnp.broadcast_to(x, (8, LANES)), 0.0)

    heat = {}
    for j in range(1, HALO - 1):
        di_ref[at8(j), :], heat[j] = first_sweep(s_ref, q0_ref, j, power_of(j), h)
        q1_ref[at8(j), :] = heat[j]

    def expansion(j):
        return lookup(t_al, codes[j]) * second_sweep(s_ref, q1_ref, di_ref, j, power_of(j))

    out = [heat[1], heat[2], expansion(2)]
    for f in range(FAR):
        j = FAR_ROW + 3 * f
        out.append(restrict_sides(expansion(j) + expansion(j + 1) + expansion(j + 2)))
    return out


def k_outer(n_edges, n_col, rows, tab, zr_ref, *refs):
    sides = Sides(n_col, rows, rows // 6, refs[0], refs[n_edges - 1])
    corners = Sides(n_col, rows, rows // 6, refs[n_edges], refs[2 * n_edges - 1])
    rest = refs[2 * n_edges :]
    s_in, al_in, q0_in, q1_in, di_in, t_in, ea_in, strain_in, src_ref = rest[:9]
    mi_in, mod_in = rest[9:11]
    uu_in, pre_in = rest[11:14], rest[14:17]
    x_ref, keep_ref, u_ref = rest[17:20]
    s_ref, q0_ref, q1_ref, di_ref, al_ref, ea_ref, t_keep, pw_ref = rest[20:28]
    st_ref, mi_ref, mod_ref, sf_ref = rest[28:32]
    uu_refs, p_refs, d_refs = rest[32:35], rest[35:38], rest[38:41]
    own = rows - 1
    wide = zr_ref.shape[1]
    half = wide // 2
    width = wide + LANES
    mcols = mod_in.shape[1] - LANES
    t_s = jnp.sqrt(table_of(tab, 0))
    t_al = table_of(tab, 1)
    v_s = splats(t_s, NMAT)
    for g in range(3):
        k = AHEAD - 1 - g
        for dst, src in ((s_ref, s_in), (al_ref, al_in), (q0_ref, q0_in)):
            dst[at8(k), :] = row8(src, FRONT + g)
    ea_ref[at8(AHEAD - 3), :] = row8(ea_in, FRONT + 2)
    for g in (1, 2):
        q1_ref[at8(AHEAD - 1 - g), :] = row8(q1_in, FRONT + g)
    di_ref[at8(AHEAD - 2), :] = row8(di_in, FRONT + 1)
    n_p = s_ref.shape[0] // 8
    near = jnp.concatenate([src_ref[0:8, :], sides.power(0)], axis=1)
    far = jnp.concatenate([zr_ref[Z_POWER : Z_POWER + 8, :], corners.power(0)], axis=1)
    spread_power(
        pw_ref,
        n_p,
        [(AHEAD - 1, near[0:1, :]), (AHEAD - 2, near[1:2, :]), (AHEAD, far)],
    )
    h = sink(width)

    lane = lane_iota()
    has_left, has_right = sides.side > 0, sides.side < n_col - 1
    patches = [edge_patch(n_edges, e, corners, zr_ref, mcols, v_s, t_al, rest[41:45]) for e in range(n_edges)]

    def mend(x, k, near, reach):
        pieces = tiles(x)
        right, left = patches[0][k], patches[-1][k]
        pieces[0] = jnp.where((lane < near) & has_left, left, pieces[0])
        pieces[-1] = jnp.where((lane >= LANES - near) & has_right, right, pieces[-1])
        beside = jnp.where((lane < reach) & has_right, right, jnp.where((lane >= LANES - reach) & has_left, left, 0.0))
        return jnp.concatenate(pieces + [beside], axis=1)

    for j in range(KEEP):
        code = jnp.concatenate([zr_ref[Z_CODE + 8 * j : Z_CODE + 8 * j + 8, :], corners.cell(j, 1)], axis=1)
        s = choose([v_s], code)[0]
        s_ref[at8(AHEAD + j), :] = s
        if j < 2:
            temp = jnp.concatenate([zr_ref[Z_TEMP + 8 * j : Z_TEMP + 8 * j + 8, :], corners.cell(j, 0)], axis=1)
            q0_ref[at8(AHEAD + j), :] = s * temp
            al_ref[at8(AHEAD + j), :] = lookup(t_al, code)
            at = Z_HEAT + 8 * j
            q1_ref[at8(AHEAD + 1 + j), :] = mend(zr_ref[at : at + 8, :], j, KEEP, HALO)
    for r in (AHEAD - 1, AHEAD):
        di_ref[at8(r), :], q1_ref[at8(r), :] = first_sweep(s_ref, q0_ref, r, power_row(pw_ref, n_p, r), h)
    r = AHEAD + 1
    di_ref[at8(r), :] = 1.0 / (h + row8(s_ref, r) * conduct_sum(s_ref, r))
    for r in range(AHEAD - 2, AHEAD + 2):
        t2 = second_sweep(s_ref, q1_ref, di_ref, r, power_row(pw_ref, n_p, r))
        t_keep[at8(r), :] = t2
        ea_ref[at8(r), :] = row8(al_ref, r) * t2
    ea_ref[at8(AHEAD + 2), :] = mend(zr_ref[Z_STRAIN : Z_STRAIN + 8, :], 2, KEEP, HALO)

    core = lax.axis_index(CORE)

    def other_half(x):
        return jnp.where(core == 0, x[:, half:wide], x[:, 0:half])

    def own_half(x):
        return jnp.where(core == 0, x[:, 0:half], x[:, half:wide])

    for g in range(2):
        t2 = row8(t_keep, AHEAD - 1 - g)
        keep_ref[8 * g : 8 * g + 8, :] = own_half(t2)
        x_ref[8 * g : 8 * g + 8, :] = other_half(t2)
    x_ref[16:24, :] = other_half(row8(t_in, FRONT + 2))

    count = mod_in.shape[0] // 8
    mrows = count - MHALO
    mwidth = mod_in.shape[1]
    n_m = count + MHALO
    for m in range(MHALO + 1 - FAR):
        i = AHEAD - 3 + 3 * m
        x = row8(ea_ref, i) + row8(ea_ref, i + 1) + row8(ea_ref, i + 2)
        st_ref[at8(MHALO - m), :] = restrict_columns(x)
    for f in range(FAR):
        x = zr_ref[Z_FAR : Z_FAR + 8, mcols * f : mcols * (f + 1)]
        st_ref[at8(FAR - 1 - f), :] = mend(x, 3 + f, 1, MHALO)
    for m in range(1, count):
        st_ref[at8(MHALO + m), :] = row8(strain_in, m)
    values = splats(table_of(tab, 2), NMAT)
    for i in range(MHALO):
        j = MHALO - 1 - i
        fields = []
        for f in range(4):
            body = zr_ref[Z_SOLID + ML * f : Z_SOLID + ML * f + 8, mcols * j : mcols * (j + 1)]
            body = jnp.where(sub_iota(mcols) < ML, body, 0.0)
            side = corners.field(j, f)
            fields.append(jnp.concatenate([body, side], axis=1))
        mod_ref[at8(i), :], root, mi_ref[at8(i), :] = moduli(values, fields[3])
        for f in range(3):
            uu_refs[f][at8(i), :] = root * fields[f]
    for ref, src in zip((mi_ref, mod_ref, *uu_refs), (mi_in, mod_in, *uu_in)):
        ref[8 * MHALO : 8 * n_m, :] = src[...]
    for i in range(n_m):
        sf_ref[at8(i), :] = row8(mod_ref, i) * row8(st_ref, i)
    sign = jnp.where(core == 0, 0.5, -0.5).astype(jnp.float32)
    for i in range(1, n_m - 1):
        load = row8(sf_ref, i)
        force = [
            0.5 * (next_sub(load) - prev_sub(load)),
            sign * (row8(sf_ref, i + 1) - row8(sf_ref, i - 1)),
            0.5 * (next_lane(load) - prev_lane(load)),
        ]
        inv = row8(mi_ref, i)
        inside = inv > 0.0
        if i <= MHALO:
            near = couple_sum([[row8(r, i - 1), row8(r, i), row8(r, i + 1)] for r in uu_refs])
            pre = [near[d] * (1.0 / STIFF_DIAG) - row8(uu_refs[d], i) for d in range(3)]
        else:
            pre = [row8(r, i - MHALO) for r in pre_in]
        inv = inv * (1.0 / STIFF_DIAG)
        for d in range(3):
            p_refs[d][at8(i), :] = jnp.where(inside, force[d] * inv + pre[d], 0.0)
    c_near = 2.0 * RHO1 / DELTA / STIFF_DIAG
    c_self = 1.0 + RHO1 * RHO0
    for i in range(2, n_m - 2):
        near = couple_sum([[row8(r, i - 1), row8(r, i), row8(r, i + 1)] for r in p_refs])
        inv = row8(mi_ref, i)
        for d in range(3):
            moved = row8(uu_refs[d], i) + c_self * row8(p_refs[d], i) + c_near * near[d]
            d_refs[d][at8(i), :] = moved * inv
    sub = sub_iota(mwidth)
    weight = jnp.where(sub < ML, (ML - sub).astype(jnp.float32) * (1.0 / (ML * (ML + 1) / 2.0)), 0.0)
    x_ref[24:32, :] = jnp.zeros((8, x_ref.shape[1]), jnp.float32)
    for g in range(mrows):
        i = MHALO + g
        u0, u2 = row8(d_refs[0], i), row8(d_refs[2], i)
        div = 0.5 * (next_sub(u0) - prev_sub(u0)) + 0.5 * (next_lane(u2) - prev_lane(u2))
        div = div + sign * (row8(d_refs[1], i + 1) - row8(d_refs[1], i - 1))
        stress = row8(mod_ref, i) * (div - 3.0 * row8(st_ref, i))
        die = jnp.sum(weight * stress, axis=0, keepdims=True)
        first, second = die[:, 0:LANES], die[:, LANES : 2 * LANES]
        keep_ref[16 + g : 17 + g, 0:LANES] = jnp.where(core == 0, first, second)
        x_ref[24 + g : 25 + g, 0:LANES] = jnp.where(core == 0, second, first)
        for d in range(3):
            u_ref[8 * (mrows * d + g) : 8 * (mrows * d + g) + 8, :] = row8(d_refs[d], i)[:, 0:mcols]


def k_out(rows, mrows, t_in, keep_ref, xr_ref, u_in, t_out, u_out, slow_ref, buf, die, wide_die, ubuf):
    half = slow_ref.shape[1]
    mcols = u_in.shape[1]
    core = lax.axis_index(CORE)

    def put(ref, at, x):
        count = ref.shape[0] * LANES // x.shape[1]
        for t, piece in enumerate(tiles(x)):
            ref[count * t + at : count * t + at + piece.shape[0], :] = piece

    def build(rev):
        lo = half if rev else 0
        for g in range(rows):
            i = rows - 1 - g if rev else g
            if g < 2:
                x = keep_ref[8 * g : 8 * g + 8, :]
            elif g < rows - 3:
                x = t_in[8 * (FRONT + g) : 8 * (FRONT + g) + 8, lo : lo + half]
            else:
                k = rows - 1 - g
                x = xr_ref[8 * k : 8 * k + 8, :]
            put(buf, 8 * i, x)
        for g in range(mrows):
            mine = 2 * mrows - 1 - g if rev else g
            theirs = g if rev else 2 * mrows - 1 - g
            die[mine : mine + 1, :] = keep_ref[16 + g : 17 + g, 0:LANES]
            die[theirs : theirs + 1, :] = xr_ref[24 + g : 25 + g, 0:LANES]
            for d in range(3):
                i = mrows - 1 - g if rev else g
                put(ubuf, 8 * (mrows * d + i), row8(u_in, mrows * d + g))

    @pl.when(core == 0)
    def _():
        build(False)

    @pl.when(core != 0)
    def _():
        build(True)

    for t in range(half // LANES):
        at = 8 * rows * t
        for l in range(DEPTH):
            t_out[l, :, tile_lanes(t)] = buf[pl.ds(at + l, rows, stride=8), :]
    for t in range(mcols // LANES):
        for d in range(3):
            for l in range(ML):
                u_out[d, l, :, tile_lanes(t)] = ubuf[pl.ds(8 * mrows * (3 * t + d) + l, mrows, stride=8), :]
    lane = lane_iota(2 * mrows)
    for t in range(half // LANES):
        x = gather_lanes(die[...], (lane + LANES * t) // 3)
        for b in range(3):
            wide_die[pl.ds(b, 2 * mrows, stride=3), :] = x
        slow = 1.0 + 0.2 * buf[pl.ds(8 * rows * t, rows, stride=8), :] + 0.5 * wide_die[...]
        slow_ref[:, tile_lanes(t)] = slow


def pairs(dims, sends):
    index = {}
    for r in range(dims[0]):
        for c in range(dims[1]):
            for a in range(dims[2]):
                index[(r, c, a)] = (r * dims[1] + c) * dims[2] + a
    out = []
    for source in index:
        target = sends(*source)
        if target in index:
            out.append((index[source], index[target]))
    return out


def per_device(temp, ids, power, mat, offset, heat_table, growth_table, modulus_table):
    axes = ("row", "col", "lay")
    dims = tuple(lax.axis_size(x) for x in axes)
    n_col = dims[1]
    _, rows, half = temp.shape
    _, _, mrows, mcols = offset.shape
    n_edges = 1 if n_col == 2 else 2
    n_t = half // LANES
    m_t = mcols // LANES

    def send(x, sends):
        return lax.ppermute(x, axes, pairs(dims, sends))

    def swap(r, c, a):
        return (r, c, 1 - a)

    def along(r, c, a):
        return (r + 1, c, 0) if a == 1 else (r - 1, c, 1)

    wide = 2 * half
    own = rows - 1
    kind = lax.broadcasted_iota(jnp.int32, (2, *temp.shape), 0)
    both = jnp.where(kind == 0, temp[None], power[None, None])
    tab = jnp.stack([heat_table, growth_table, modulus_table])
    tab = jnp.pad(tab, ((0, 0), (1, LANES - 1 - tab.shape[1])))
    n = 16 * HALO
    n_far = 8 * far_rows(rows)
    cells, one = call(k_rows, [(16 * rows * n_t, LANES), ((n + 16) * n_t + n_far, LANES)], [both, ids])
    got1 = send(one, swap)
    two, mg = call(
        functools.partial(k_rest, n_edges),
        [
            ((16 * (rows - HALO) + rows - 16) * n_t + 32 * MHALO * m_t + 8 * n_edges, LANES),
            (32 * mrows, mcols),
        ],
        [both, cells, offset, mat],
        scratch=[(32 * mrows * m_t, LANES)],
    )
    got2 = send(two, swap)
    n_c = 32 + n_far - 8 * (-4 * (mrows - MHALO) * MSPAN // LANES) + 8
    z, first_rows, *edges = call(
        functools.partial(k_edge, n_edges),
        [(far_place(n_edges, -1, wide, mcols)[0].stop, wide), (n + 16, wide)] + [(32, LANES)] * n_edges,
        [tab, both, cells, got1, mg],
        cost=EDGE_COST,
        scratch=[(8 * HALO, wide)] * 4,
    )
    leaving = [z, *edges]
    leaving = call(
        functools.partial(k_beside, n_edges, rows),
        [(n_c, LANES)] * n_edges + [x.shape for x in leaving],
        [both, cells, got1, got2, mg] + leaving,
        aliases={5 + k: n_edges + k for k in range(len(leaving))},
    )
    beside, z, near = leaving[:n_edges], leaving[n_edges], leaving[n_edges + 1 :]
    zr = send(z, along)
    if n_edges == 1:
        sides = [send(beside[0], lambda r, c, a: (r, 1 - c, a))]
        corners = [send(near[0], lambda r, c, a: along(r, 1 - c, a))]
    else:
        sides = [send(beside[0], lambda r, c, a: (r, c + 1, a)), send(beside[1], lambda r, c, a: (r, c - 1, a))]
        corners = [
            send(near[0], lambda r, c, a: along(r, c + 1, a)),
            send(near[1], lambda r, c, a: along(r, c - 1, a)),
        ]
    w, src, mw = call(
        functools.partial(k_chip, rows),
        [(16 * rows, wide), (rows, wide), (32 * (mrows + MHALO), mcols)],
        [both, cells, got2, mg, first_rows],
    )
    width = wide + LANES
    mwidth = mcols + LANES
    n_w = 8 * (rows + FRONT + 4)
    inner = call(
        functools.partial(k_inner, n_edges, n_col, rows),
        [(n_w, width)] * 7 + [(8 * (mrows + MHALO), mwidth)],
        [tab, w, src] + sides,
        scratch=[(n_w * (width // LANES), LANES)],
    )
    t2 = inner[5]
    solid = call(
        functools.partial(k_mech, n_edges, n_col, rows), [(8 * (mrows + MHALO), mwidth)] * 8, [tab, mw] + sides
    )
    n_h = 8 * (AHEAD + HALO + 5)
    n_m = 8 * (mrows + 2 * MHALO)
    x, keep, u = call(
        functools.partial(k_outer, n_edges, n_col, rows),
        [(32, half), (24, half), (24 * mrows, mcols)],
        [tab, zr] + sides + corners + list(inner) + [src] + list(solid),
        scratch=[(n_h, width)] * 7
        + [(n_h * (width // LANES), LANES)]
        + [(n_m, mwidth)] * 13
        + [(8 * HALO, LANES)] * 4,
    )
    xr = send(x, swap)
    t_out, u_out, slow = call(
        functools.partial(k_out, rows, mrows),
        [temp.shape, offset.shape, power.shape],
        [t2, keep, xr, u],
        scratch=[
            (8 * rows * n_t, LANES),
            (2 * mrows, LANES),
            (rows, LANES),
            (24 * mrows * m_t, LANES),
        ],
    )
    return t_out, u_out, slow


def solution(mesh):
    placed = (
        P("grp", "row", ("col", "lay")),
        P("grp", "row", ("col", "lay")),
        P(("grp", "row"), ("col", "lay")),
        P("grp", ("row", "lay"), "col"),
        P(None, "grp", ("row", "lay"), "col"),
        P(),
        P(),
        P(),
    )
    return jax.shard_map(
        per_device,
        mesh=mesh,
        in_specs=placed,
        out_specs=(
            P("grp", "row", ("col", "lay")),
            P(None, "grp", ("row", "lay"), "col"),
            P(("grp", "row"), ("col", "lay")),
        ),
        check_vma=False,
    )
```

```python
import functools

import jax
import jax.numpy as jnp
from jax import lax
from jax.experimental import pallas as pl
from jax.experimental.pallas import tpu as pltpu
from jax.sharding import PartitionSpec as P

DEPTH = 8
ML = 6
LANES = 128
HALO = 11
MHALO = 3

STIFF_DIAG = 12.0
THETA = 1.0
DELTA = 0.75
SIGMA = THETA / DELTA
RHO0 = 1.0 / SIGMA
RHO1 = 1.0 / (2.0 * SIGMA - RHO0)

VMEM = pl.BlockSpec(memory_space=pltpu.VMEM)
FRONT = 9
AHEAD = 5
STEP = 3
SPAN = 11
MSPAN = 8
NMAT = 16
FAR = 2
EDGE_COST = 10**10
FAR_ROW = 9 - 3 * FAR
KEEP = 3
Z_TEMP, Z_CODE, Z_HEAT, Z_STRAIN, Z_SUM, Z_SOLID, Z_POWER, Z_FAR = 0, 16, 40, 56, 64, 80, 104, 112
CORE = "lay"
UNROLL_STRAIN = 3


def call(kernel, outs, args, scratch=(), specs=None, aliases=None, cost=0):
    return pl.pallas_call(
        kernel,
        out_shape=[jax.ShapeDtypeStruct(s, jnp.float32) for s in outs],
        in_specs=specs or [VMEM] * len(args),
        out_specs=[VMEM] * len(outs),
        input_output_aliases=aliases or {},
        cost_estimate=pl.CostEstimate(flops=cost, bytes_accessed=0, transcendentals=0) if cost else None,
        scratch_shapes=[pltpu.VMEM(s, jnp.float32) if isinstance(s, tuple) else s for s in scratch],
        compiler_params=pltpu.CompilerParams(vmem_limit_bytes=16 * 1024 * 1024),
    )(*args)


def lane_iota(rows=8):
    return lax.broadcasted_iota(jnp.int32, (rows, LANES), 1)


def sub_iota(width):
    return lax.broadcasted_iota(jnp.int32, (8, width), 0)


def tile_lanes(t):
    return slice(LANES * t, LANES * (t + 1))


def tiles(x):
    return [x[:, tile_lanes(t)] for t in range(x.shape[1] // LANES)]


def table_of(ref, k):
    return jnp.broadcast_to(ref[k : k + 1, :], (8, LANES))


def gather_lanes(table, index):
    return jnp.take_along_axis(table, index, axis=1, mode="promise_in_bounds")


def lookup(table, code):
    return jnp.concatenate([gather_lanes(table, c.astype(jnp.int32)) for c in tiles(code)], axis=1)


def k_tables(tab, out_ref):
    for k, table in enumerate((jnp.sqrt(table_of(tab, 0)), table_of(tab, 2))):
        for m in range(NMAT + 1):
            at = 8 * ((NMAT + 1) * k + m)
            out_ref[at : at + 8, :] = jnp.broadcast_to(table[:, m : m + 1], (8, LANES))
    out_ref[16 * (NMAT + 1) : 16 * (NMAT + 1) + 8, :] = table_of(tab, 1)


def splats(tab, k):
    return [row8(tab, (NMAT + 1) * k + m) for m in range(NMAT + 1)]


def expansion_table(tab):
    return row8(tab, 2 * (NMAT + 1))


def choose(lists, code):
    out = [[] for _ in lists]
    for c in tiles(code):
        c = c.astype(jnp.int32)
        bits = [(c & (1 << k)) != 0 for k in range(5)]
        for n, values in enumerate(lists):
            level = values[:16]
            for k in range(4):
                level = [jnp.where(bits[k], b, a) for a, b in zip(level[::2], level[1::2])]
            out[n].append(jnp.where(bits[4], values[16], level[0]))
    return [jnp.concatenate(x, axis=1) for x in out]


def prev_lane(x):
    return pltpu.roll(x, 1, 1)


def next_lane(x):
    return pltpu.roll(x, x.shape[1] - 1, 1)


def prev_sub(x):
    return pltpu.roll(x, 1, 0)


def next_sub(x):
    return pltpu.roll(x, 7, 0)


def at8(i):
    return pl.ds(8 * i, 8) if isinstance(i, int) else pl.ds(pl.multiple_of(8 * i, 8), 8)


def row8(ref, i):
    return ref[at8(i), :]


def turned(core, last, g):
    return core * last + (1 - 2 * core) * g


def k_rows(in_ref, id_ref, a_ref, one_ref):
    core = lax.axis_index(CORE)
    other = 1 - core
    rows = in_ref.shape[2]
    n_t = in_ref.shape[3] // LANES
    n = 16 * HALO
    for t in range(n_t):
        at = 16 * rows * t
        for l in range(DEPTH):
            a_ref[pl.ds(at + l, rows, stride=16), :] = in_ref[0, l, :, tile_lanes(t)]
            a_ref[pl.ds(at + DEPTH + l, rows, stride=16), :] = (id_ref[l, :, tile_lanes(t)] + 1).astype(jnp.float32)
    for t in range(n_t):
        to = (n + 16) * t
        for g in range(HALO):
            i = 16 * (rows * t + turned(other, rows - 1, g))
            one_ref[to + 16 * g : to + 16 * g + 16, :] = a_ref[pl.ds(pl.multiple_of(i, 16), 16), :]
        for b in range(2):
            one_ref[to + n + 8 * b : to + n + 8 * b + 8, :] = power_rows(in_ref, other, b, t)
    for k, x in enumerate(far_strip(in_ref, a_ref, other, core * (n_t - 1), core)):
        to = (n + 16) * n_t + 8 * k
        one_ref[to : to + 8, :] = x


def k_rest(n_edges, in_ref, a_ref, u_ref, mat_ref, two_ref, mg_ref, m_ref):
    core = lax.axis_index(CORE)
    other = 1 - core
    rows = in_ref.shape[2]
    n_t = in_ref.shape[3] // LANES
    mrows = mat_ref.shape[1]
    mcols = mat_ref.shape[2]
    m_t = mcols // LANES
    m_ref[...] = jnp.zeros(m_ref.shape, jnp.float32)
    for t in range(m_t):
        at = 32 * mrows * t
        for l in range(ML):
            for f in range(3):
                m_ref[pl.ds(at + 8 * f + l, mrows, stride=32), :] = u_ref[f, l, :, tile_lanes(t)]
            m_ref[pl.ds(at + 24 + l, mrows, stride=32), :] = (mat_ref[l, :, tile_lanes(t)] + 1).astype(jnp.float32)
        for g in range(mrows):
            i = 32 * (mrows * t + turned(core, mrows - 1, g))
            mg_ref[32 * g : 32 * g + 32, tile_lanes(t)] = m_ref[pl.ds(pl.multiple_of(i, 32), 32), :]
    for e in range(n_edges):
        side = edge_side(n_edges, e)
        fields = []
        for g in range(MHALO):
            i = 32 * (mrows * side * (m_t - 1) + turned(core, mrows - 1, mrows - 1 - g))
            fields += [m_ref[pl.ds(pl.multiple_of(i + 8 * f, 8), 8), :] for f in range(4)]
        at = two_ref.shape[0] - 8 * (n_edges - e)
        (two_ref[at : at + 8, :],) = packed(side, fields, MSPAN, MHALO)
    rest = 16 * (rows - 1 - HALO)
    for t in range(n_t):
        to = (rest + rows - 16) * t
        for g in range(HALO, rows - 1):
            i = 16 * (rows * t + turned(other, rows - 1, g))
            k = to + 16 * (g - HALO)
            two_ref[k : k + 16, :] = a_ref[pl.ds(pl.multiple_of(i, 16), 16), :]
        for b in range(2, rows // 8):
            two_ref[to + rest + 8 * (b - 2) : to + rest + 8 * (b - 1), :] = power_rows(in_ref, other, b, t)
    for t in range(m_t):
        for g in range(MHALO):
            i = 32 * (mrows * t + turned(core, mrows - 1, mrows - 1 - g))
            k = (rest + rows - 16) * n_t + 32 * (MHALO * t + g)
            two_ref[k : k + 32, :] = m_ref[pl.ds(pl.multiple_of(i, 32), 32), :]


def power_rows(in_ref, turn, b, t):
    rows = in_ref.shape[2]
    lanes = tile_lanes(t) if isinstance(t, int) else pl.ds(pl.multiple_of(LANES * t, LANES), LANES)
    x = in_ref[1, 0, at8(turned(turn, rows // 8 - 1, b)), lanes]
    return jnp.take_along_axis(x, turned(turn, 7, sub_iota(LANES)), axis=0, mode="promise_in_bounds")


def far_strip(in_ref, a_ref, turn, t, side):
    rows = in_ref.shape[2]
    blocks = []
    for g in range(HALO, rows - 1):
        i = 16 * (rows * t + turned(turn, rows - 1, g))
        blocks += [a_ref[pl.ds(pl.multiple_of(i + k, 8), 8), :] for k in (0, 8)]
    blocks += [power_rows(in_ref, turn, b, t) for b in range(2, rows // 8)]
    return packed(side, blocks, SPAN, HALO)


def edge_side(n_edges, e):
    return 1 - lax.axis_index("col") if n_edges == 1 else 1 - e


def edge_tile(side, width):
    if isinstance(side, int):
        return tile_lanes(side * (width // LANES - 1))
    return pl.ds(pl.multiple_of(side * (width - LANES), LANES), LANES)


def packed(side, blocks, span, keep):
    lane = lane_iota()
    per = LANES // span
    out = []
    for i in range(0, len(blocks), per):
        acc = jnp.zeros((8, LANES), jnp.float32)
        for k, x in enumerate(blocks[i : i + per]):
            acc = jnp.where(lane // span == k, pltpu.roll(x, span * k + side * keep, 1), acc)
        out.append(acc)
    return out


def far_rows(rows):
    return -(-(2 * (rows - 1 - HALO) + rows // 8 - 2) // (LANES // SPAN))


def k_half(n_edges, tab, in_ref, a_ref, s_ref, q0_ref, al_ref, far_ref):
    core = lax.axis_index(CORE)
    rows = in_ref.shape[2]
    n_t = in_ref.shape[3] // LANES
    v_s = splats(tab, 0)
    t_al = expansion_table(tab)
    for t in range(n_t):
        for g in range(HALO):
            i = 16 * (rows * t + turned(core, rows - 1, g))
            code = a_ref[pl.ds(pl.multiple_of(i + 8, 8), 8), :]
            (x,) = choose([v_s], code)
            s_ref[at8(g), tile_lanes(t)] = x
            q0_ref[at8(g), tile_lanes(t)] = x * a_ref[pl.ds(pl.multiple_of(i, 16), 8), :]
            if 2 <= g < 9:
                al_ref[at8(g), tile_lanes(t)] = lookup(t_al, code)
    for e in range(n_edges):
        side = edge_side(n_edges, e)
        for k, x in enumerate(far_strip(in_ref, a_ref, core, side * (n_t - 1), side)):
            at = 8 * (far_rows(rows) * e + k)
            far_ref[at : at + 8, :] = x


def k_edge(n_edges, tab, in_ref, a_ref, got_ref, mg_ref, s_own, q0_own, al_own, z_ref, w_ref, *refs):
    core = lax.axis_index(CORE)
    wide = z_ref.shape[1]
    half = wide // 2
    n_t = half // LANES
    rows = in_ref.shape[2]
    mcols = mg_ref.shape[1]
    n = 16 * HALO
    edge_refs, (s_ref, q0_ref, al_ref, q1_ref, di_ref) = refs[:n_edges], refs[n_edges:]
    v_s = splats(tab, 0)
    t_al = expansion_table(tab)

    def build(first):
        for t in range(n_t):
            lanes = tile_lanes(t if first else n_t + t)
            for g in range(HALO):
                i = 16 * (rows * t + (g if first else rows - 1 - g))
                w_ref[16 * g : 16 * g + 16, lanes] = a_ref[i : i + 16, :]
            for b in range(2):
                w_ref[n + 8 * b : n + 8 * b + 8, lanes] = power_rows(in_ref, 0 if first else 1, b, t)
            lanes = tile_lanes(n_t + t if first else t)
            at = (n + 16) * t
            w_ref[0 : n + 16, lanes] = got_ref[at : at + n + 16, :]
            for g in range(HALO):
                code = got_ref[at + 16 * g + 8 : at + 16 * g + 16, :]
                (x,) = choose([v_s], code)
                s_ref[at8(g), lanes] = x
                q0_ref[at8(g), lanes] = x * got_ref[at + 16 * g : at + 16 * g + 8, :]
                if 2 <= g < 9:
                    al_ref[at8(g), lanes] = lookup(t_al, code)
        lanes = slice(0, half) if first else slice(half, wide)
        for dst, src in ((s_ref, s_own), (q0_ref, q0_own), (al_ref, al_own)):
            dst[:, lanes] = src[...]

    @pl.when(core == 0)
    def _():
        build(True)

    @pl.when(core != 0)
    def _():
        build(False)

    for g in range(2):
        z_ref[Z_TEMP + 8 * g : Z_TEMP + 8 * g + 8, :] = w_ref[16 * g : 16 * g + 8, :]
    for g in range(3):
        z_ref[Z_CODE + 8 * g : Z_CODE + 8 * g + 8, :] = w_ref[16 * g + 8 : 16 * g + 16, :]
    z_ref[Z_POWER : Z_POWER + 8, :] = w_ref[n : n + 8, :]
    z_ref[Z_FAR:, :] = jnp.zeros((z_ref.shape[0] - Z_FAR, wide), jnp.float32)
    for g in range(MHALO):
        for f in range(4):
            at = Z_SOLID + ML * f
            z_ref[at : at + ML, mcols * g : mcols * (g + 1)] = mg_ref[32 * g + 8 * f : 32 * g + 8 * f + ML, :]
    for e in range(n_edges):
        side = edge_side(n_edges, e)
        lanes, mlanes = edge_tile(side, wide), edge_tile(side, mcols)
        blocks = [w_ref[8 * i : 8 * i + 8, lanes] for i in range(2 * HALO)]
        blocks += [w_ref[n + 8 * b : n + 8 * b + 8, lanes] for b in range(2)]
        fields = [mg_ref[8 * i : 8 * i + 8, mlanes] for i in range(4 * MHALO)]
        near = packed(side, blocks, SPAN, HALO) + packed(side, fields, MSPAN, MHALO)
        strip = blocks[4 : 2 * HALO : 2] + blocks[7 : 2 * HALO : 2] + blocks[2 * HALO + 1 :]
        for k, x in enumerate(packed(side, strip, SPAN, HALO)):
            z_ref[far_place(e, k, wide)] = x
        for k, x in enumerate(near):
            edge_refs[e][8 * k : 8 * k + 8, :] = x
    h = sink(wide)
    top = sub_iota(wide) == 0
    powers = {
        g: jnp.where(top, jnp.broadcast_to(w_ref[n + g : n + g + 1, :], (8, wide)), 0.0) for g in range(1, HALO - 1)
    }
    for g in range(1, HALO - 1):
        di_ref[at8(g), :], q1_ref[at8(g), :] = first_sweep(s_ref, q0_ref, g, powers[g], h, True)
    z_ref[Z_HEAT : Z_HEAT + 16, :] = q1_ref[8:24, :]

    def expansion(g):
        return row8(al_ref, g) * second_sweep(s_ref, q1_ref, di_ref, g, powers[g], True)

    z_ref[Z_STRAIN : Z_STRAIN + 8, :] = expansion(2)
    for f in range(FAR):
        g = FAR_ROW + 3 * f
        x = expansion(g) + expansion(g + 1) + expansion(g + 2)
        z_ref[Z_SUM + 8 * f : Z_SUM + 8 * f + 8, :] = x


def far_tiles():
    return -(-(2 * HALO - 4) // (LANES // SPAN))


def far_place(e, k, wide):
    q = far_tiles() * e + k
    at = Z_FAR + 8 * (q // (wide // LANES))
    return slice(at, at + 8), tile_lanes(q % (wide // LANES))


def k_beside(n_edges, rows, n_t, far_ref, one_ref, got_ref, mg_ref, z_ref, *refs):
    near_refs, c_refs = refs[:n_edges], refs[n_edges : 2 * n_edges]
    core = lax.axis_index(CORE)
    mrows = mg_ref.shape[0] // 32
    n = 16 * HALO
    for e in range(n_edges):
        side = edge_side(n_edges, e)
        mlanes = edge_tile(side, mg_ref.shape[1])
        fields = [mg_ref[8 * i : 8 * i + 8, mlanes] for i in range(4 * MHALO, 4 * mrows)]
        far = [near_refs[e][8 * k : 8 * k + 8, :] for k in range(4)]
        for k in range(far_rows(rows)):
            at = (n + 16) * n_t + 8 * k
            x = row8(far_ref, far_rows(rows) * e + k)
            far.append(jnp.where(core == side, x, one_ref[at : at + 8, :]))
        far += packed(side, fields, MSPAN, MHALO)
        at = got_ref.shape[0] - 8 * (n_edges - e)
        far.append(got_ref[at : at + 8, :])
        for k, x in enumerate(far):
            c_refs[e][8 * k : 8 * k + 8, :] = x


def k_chip(rows, in_ref, a_ref, got_ref, mg_ref, first_ref, w_ref, src_ref, mw_ref):
    core = lax.axis_index(CORE)
    n_t = w_ref.shape[1] // LANES // 2
    mrows = mg_ref.shape[0] // 32
    n = 16 * HALO
    rest = 16 * (rows - 1 - HALO)
    w_ref[0:n, :] = first_ref[0:n, :]
    src_ref[0:16, :] = first_ref[n : n + 16, :]

    def build(first):
        for t in range(n_t):
            lanes = tile_lanes(t if first else n_t + t)
            for g in range(HALO, rows - 1):
                i = 16 * (rows * t + (g if first else rows - 1 - g))
                w_ref[16 * g : 16 * g + 16, lanes] = a_ref[i : i + 16, :]
            for b in range(2, rows // 8):
                src_ref[8 * b : 8 * b + 8, lanes] = power_rows(in_ref, 0 if first else 1, b, t)
            lanes = tile_lanes(n_t + t if first else t)
            at = (rest + rows - 16) * t
            w_ref[n : n + rest, lanes] = got_ref[at : at + rest, :]
            src_ref[16:rows, lanes] = got_ref[at + rest : at + rest + rows - 16, :]

    @pl.when(core == 0)
    def _():
        build(True)

    @pl.when(core != 0)
    def _():
        build(False)

    mw_ref[0 : 32 * mrows, :] = mg_ref[...]
    for t in range(mw_ref.shape[1] // LANES):
        at = (rest + rows - 16) * n_t + 32 * MHALO * t
        mw_ref[32 * mrows : 32 * (mrows + MHALO), tile_lanes(t)] = got_ref[at : at + 32 * MHALO, :]


class Sides:
    def __init__(self, n_col, rows, mrows, from_left, from_right):
        self.left = from_left
        self.right = from_right
        self.rows = rows
        self.mrows = mrows
        lane = lane_iota()
        col = lax.axis_index("col")
        self.masks = {
            w: ((lane < w) & (col < n_col - 1), (lane >= LANES - w) & (col > 0)) for w in (HALO, MHALO)
        }
        self.only = self.left is self.right
        self.side = col

    def take(self, v, k, span, width):
        right_mask, left_mask = self.masks[width]
        x = row8(self.right, v)
        if self.only:
            x = pltpu.roll(x, LANES - span * k - self.side * width, 1)
            return jnp.where(right_mask | left_mask, x, 0.0)
        r = pltpu.roll(x, (LANES - span * k) % LANES, 1)
        l = pltpu.roll(row8(self.left, v), LANES - span * k - width, 1)
        return jnp.where(right_mask, r, jnp.where(left_mask, l, 0.0))

    def block(self, first, i, span, width):
        per = LANES // span
        return self.take(first + i // per, i % per, span, width)

    def cell(self, g, kind):
        if g < HALO:
            return self.block(0, 2 * g + kind, SPAN, HALO)
        return self.block(4, 2 * (g - HALO) + kind, SPAN, HALO)

    def power(self, b):
        if b < 2:
            return self.block(0, 2 * HALO + b, SPAN, HALO)
        return self.block(4, 2 * (self.rows - 1 - HALO) + b - 2, SPAN, HALO)

    def field(self, m, f):
        if m < MHALO:
            return self.block(3, 4 * m + f, MSPAN, MHALO)
        first = 4 + far_rows(self.rows)
        if m < self.mrows:
            return self.block(first, 4 * (m - MHALO) + f, MSPAN, MHALO)
        first += -(-4 * (self.mrows - MHALO) * MSPAN // LANES)
        return self.block(first, 4 * (m - self.mrows) + f, MSPAN, MHALO)


def spread_power(ref, n, blocks):
    ref[...] = jnp.zeros(ref.shape, jnp.float32)
    count = ref.shape[0] // (n * 8)
    for first, x in blocks:
        for t, piece in enumerate(tiles(x)):
            ref[pl.ds(8 * (n * t + first), piece.shape[0], stride=8), :] = piece
    return count


def power_row(ref, n, i):
    count = ref.shape[0] // (n * 8)
    return jnp.concatenate([row8(ref, n * t + i) for t in range(count)], axis=1)


def conduct_sum(ref, i, closed=False):
    x = row8(ref, i)
    sub = sub_iota(x.shape[1])
    before, after = prev_lane(x), next_lane(x)
    if closed:
        lane = lax.broadcasted_iota(jnp.int32, x.shape, 1)
        before = jnp.where(lane > 0, before, 0.0)
        after = jnp.where(lane < x.shape[1] - 1, after, 0.0)
    total = row8(ref, i - 1) + row8(ref, i + 1) + before + after
    total = total + jnp.where(sub < DEPTH - 1, next_sub(x), 0.0)
    return total + jnp.where(sub > 0, prev_sub(x), 0.0)


def sink(width):
    return jnp.where(sub_iota(width) == DEPTH - 1, 2.0, 0.2).astype(jnp.float32)


def to_solid_layers(y):
    return jnp.where(sub_iota(y.shape[1]) < 3, y, next_sub(y)) * (1.0 / 9.0)


def gather_main(pieces):
    lane = 3 * lane_iota()
    out = []
    for j in range(len(pieces) // 3):
        total = None
        for k in range(3):
            got = None
            for t in range(3):
                g = gather_lanes(pieces[3 * j + t], (lane + k) & (LANES - 1))
                got = g if got is None else jnp.where(lane + k >= LANES * t, g, got)
            total = got if total is None else total + got
        out.append(total)
    return out


def gather_sides(piece):
    lane = lane_iota()
    first = LANES - MHALO
    inside = (lane < MHALO) | (lane >= first)
    index = jnp.where(lane < MHALO, 3 * lane, jnp.where(lane >= first, LANES - 9 + 3 * (lane - first), 0))
    total = gather_lanes(piece, index) + gather_lanes(piece, index + 1) + gather_lanes(piece, index + 2)
    return jnp.where(inside, total, 0.0)


def restrict_columns(x):
    pieces = tiles(x)
    return to_solid_layers(jnp.concatenate(gather_main(pieces[:-1]) + [gather_sides(pieces[-1])], axis=1))


def first_sweep(s_ref, q0_ref, i, power, h, closed=False):
    s = row8(s_ref, i)
    inv = 1.0 / (h + s * conduct_sum(s_ref, i, closed))
    return inv, s * ((power + s * conduct_sum(q0_ref, i, closed)) * inv)


def second_sweep(s_ref, q1_ref, di_ref, i, power, closed=False):
    return (power + row8(s_ref, i) * conduct_sum(q1_ref, i, closed)) * row8(di_ref, i)


def k_inner(n_edges, n_col, rows, tab, w_ref, src_ref, *refs):
    sides = Sides(n_col, rows, rows // 6, refs[0], refs[n_edges - 1])
    s_ref, al_ref, q0_ref, q1_ref, di_ref, t_ref, ea_ref, strain_ref, pw_ref = refs[n_edges:]
    own = rows - 1
    width = src_ref.shape[1] + LANES
    t_al = expansion_table(tab)
    v_s = splats(tab, 0)
    side_power = jnp.concatenate([sides.power(k) for k in range(rows // 8)], axis=0)
    n_p = s_ref.shape[0] // 8
    spread_power(pw_ref, n_p, [(FRONT, jnp.concatenate([src_ref[...], side_power], axis=1))])
    h = sink(width)

    for i in range(0, own + 2 * STEP + 2, STEP):
        later = []
        for g in range(i, min(i + STEP, own)):
            temp = jnp.concatenate([w_ref[16 * g : 16 * g + 8, :], sides.cell(g, 0)], axis=1)
            code = jnp.concatenate([w_ref[16 * g + 8 : 16 * g + 16, :], sides.cell(g, 1)], axis=1)
            s, al = choose([v_s], code)[0], lookup(t_al, code)
            later += [(s_ref, FRONT + g, s), (q0_ref, FRONT + g, s * temp), (al_ref, FRONT + g, al)]
        for g in range(max(1, i - STEP - 1), min(i - 1, own - 1)):
            r = FRONT + g
            inv, q1 = first_sweep(s_ref, q0_ref, r, power_row(pw_ref, n_p, r), h)
            later += [(di_ref, r, inv), (q1_ref, r, q1)]
        for g in range(max(2, i - 2 * STEP - 2), min(i - STEP - 2, own - 2)):
            r = FRONT + g
            t2 = second_sweep(s_ref, q1_ref, di_ref, r, power_row(pw_ref, n_p, r))
            later += [(t_ref, r, t2), (ea_ref, r, row8(al_ref, r) * t2)]
        for ref, r, x in later:
            ref[at8(r), :] = x

    def strain(m, carry):
        i = FRONT + 3 * m
        x = row8(ea_ref, i) + row8(ea_ref, i + 1) + row8(ea_ref, i + 2)
        strain_ref[at8(m), :] = restrict_columns(x)
        return carry

    lax.fori_loop(1, (own - 2) // 3, strain, 0, unroll=UNROLL_STRAIN)


def couple_sum(rows3):
    near = [[None] * 3 for _ in range(3)]
    for j in range(3):
        below, mid, above = rows3[j]
        near[0][j] = next_sub(mid) + prev_sub(mid)
        near[1][j] = above + below
        near[2][j] = next_lane(mid) + prev_lane(mid)
    out = []
    for i in range(3):
        j, k = [x for x in range(3) if x != i]
        main = near[i][i] + 0.5 * (near[j][i] + near[k][i])
        side = (near[i][j] + near[j][j]) + (near[i][k] + near[k][k])
        out.append(main + 0.25 * side)
    return out


def moduli(values, code):
    (mod,) = choose([values], code)
    inside = mod > 0.0
    root = jnp.sqrt(mod)
    return mod, root, jnp.where(inside, 1.0 / jnp.where(inside, root, 1.0), 0.0)


def k_mech(n_edges, n_col, rows, tab, mw_ref, *refs):
    sides = Sides(n_col, rows, rows // 6, refs[0], refs[n_edges - 1])
    mi_ref, mod_ref = refs[n_edges : n_edges + 2]
    uu_refs = refs[n_edges + 2 : n_edges + 5]
    pre_refs = refs[n_edges + 5 : n_edges + 8]
    values = splats(tab, 1)
    count = mw_ref.shape[0] // 32
    for m in range(count):
        fields = []
        for f in range(4):
            side = sides.field(m, f)
            fields.append(jnp.concatenate([mw_ref[32 * m + 8 * f : 32 * m + 8 * f + 8, :], side], axis=1))
        mod_ref[at8(m), :], root, mi_ref[at8(m), :] = moduli(values, fields[3])
        for f in range(3):
            uu_refs[f][at8(m), :] = root * fields[f]
    for m in range(1, count - 1):
        near = couple_sum([[row8(r, m - 1), row8(r, m), row8(r, m + 1)] for r in uu_refs])
        for d in range(3):
            pre_refs[d][at8(m), :] = near[d] * (1.0 / STIFF_DIAG) - row8(uu_refs[d], m)


def edge_patch(n_edges, e, corners, zr_ref, v_s, t_al, scratch):
    s_ref, q0_ref, q1_ref, di_ref = scratch
    side = edge_side(n_edges, e)
    lanes = edge_tile(side, zr_ref.shape[1])
    lane = lane_iota()
    mine = ((lane >= LANES - HALO) & (side == 1)) | ((lane < HALO) & (side == 0))
    per = LANES // SPAN

    def strip(i):
        x = zr_ref[far_place(e, i // per, zr_ref.shape[1])]
        return pltpu.roll(x, LANES - SPAN * (i % per) - side * HALO, 1)

    def cell(j, kind):
        held = 2 + kind
        if j < held:
            at = (Z_TEMP, Z_CODE)[kind] + 8 * j
            x = zr_ref[at : at + 8, lanes]
        else:
            x = strip(kind * (HALO - 2) + j - held)
        return jnp.where(mine, x, corners.cell(j, kind))

    codes = {}
    for j in range(HALO):
        codes[j] = cell(j, 1)
        (s,) = choose([v_s], codes[j])
        s_ref[at8(j), :] = s
        q0_ref[at8(j), :] = s * cell(j, 0)
    power = [
        jnp.where(mine, zr_ref[Z_POWER : Z_POWER + 8, lanes], corners.power(0)),
        jnp.where(mine, strip(2 * HALO - 5), corners.power(1)),
    ]
    top = sub_iota(LANES) == 0
    h = sink(LANES)

    def power_of(j):
        x = power[j // 8][j % 8 : j % 8 + 1, :]
        return jnp.where(top, jnp.broadcast_to(x, (8, LANES)), 0.0)

    heat = {}
    for j in range(1, HALO - 1):
        di_ref[at8(j), :], heat[j] = first_sweep(s_ref, q0_ref, j, power_of(j), h)
        q1_ref[at8(j), :] = heat[j]

    def expansion(j):
        return lookup(t_al, codes[j]) * second_sweep(s_ref, q1_ref, di_ref, j, power_of(j))

    out = [heat[1], heat[2], expansion(2)]
    for f in range(FAR):
        j = FAR_ROW + 3 * f
        out.append(expansion(j) + expansion(j + 1) + expansion(j + 2))
    return out


def k_outer(n_edges, n_col, rows, tab, zr_ref, *refs):
    sides = Sides(n_col, rows, rows // 6, refs[0], refs[n_edges - 1])
    corners = Sides(n_col, rows, rows // 6, refs[n_edges], refs[2 * n_edges - 1])
    rest = refs[2 * n_edges :]
    s_in, al_in, q0_in, q1_in, di_in, t_in, ea_in, strain_in, src_ref = rest[:9]
    mi_in, mod_in = rest[9:11]
    uu_in, pre_in = rest[11:14], rest[14:17]
    x_ref, keep_ref, u_ref = rest[17:20]
    s_ref, q0_ref, q1_ref, di_ref, al_ref, ea_ref, t_keep, pw_ref = rest[20:28]
    st_ref, mi_ref, mod_ref, sf_ref = rest[28:32]
    uu_refs, p_refs, d_refs = rest[32:35], rest[35:38], rest[38:41]
    own = rows - 1
    wide = zr_ref.shape[1]
    half = wide // 2
    width = wide + LANES
    mcols = mod_in.shape[1] - LANES
    t_al = expansion_table(tab)
    v_s = splats(tab, 0)
    for g in range(3):
        k = AHEAD - 1 - g
        for dst, src in ((s_ref, s_in), (al_ref, al_in), (q0_ref, q0_in)):
            dst[at8(k), :] = row8(src, FRONT + g)
    ea_ref[at8(AHEAD - 3), :] = row8(ea_in, FRONT + 2)
    for g in (1, 2):
        q1_ref[at8(AHEAD - 1 - g), :] = row8(q1_in, FRONT + g)
    di_ref[at8(AHEAD - 2), :] = row8(di_in, FRONT + 1)
    n_p = s_ref.shape[0] // 8
    near = jnp.concatenate([src_ref[0:8, :], sides.power(0)], axis=1)
    far = jnp.concatenate([zr_ref[Z_POWER : Z_POWER + 8, :], corners.power(0)], axis=1)
    spread_power(
        pw_ref,
        n_p,
        [(AHEAD - 1, near[0:1, :]), (AHEAD - 2, near[1:2, :]), (AHEAD, far)],
    )
    h = sink(width)

    lane = lane_iota()
    has_left, has_right = sides.side > 0, sides.side < n_col - 1
    patches = [edge_patch(n_edges, e, corners, zr_ref, v_s, t_al, rest[41:45]) for e in range(n_edges)]

    def mend(x, k, near, reach):
        pieces = tiles(x)
        right, left = patches[0][k], patches[-1][k]
        pieces[0] = jnp.where((lane < near) & has_left, left, pieces[0])
        pieces[-1] = jnp.where((lane >= LANES - near) & has_right, right, pieces[-1])
        beside = jnp.where((lane < reach) & has_right, right, jnp.where((lane >= LANES - reach) & has_left, left, 0.0))
        return jnp.concatenate(pieces + [beside], axis=1)

    for j in range(KEEP):
        code = jnp.concatenate([zr_ref[Z_CODE + 8 * j : Z_CODE + 8 * j + 8, :], corners.cell(j, 1)], axis=1)
        s = choose([v_s], code)[0]
        s_ref[at8(AHEAD + j), :] = s
        if j < 2:
            temp = jnp.concatenate([zr_ref[Z_TEMP + 8 * j : Z_TEMP + 8 * j + 8, :], corners.cell(j, 0)], axis=1)
            q0_ref[at8(AHEAD + j), :] = s * temp
            al_ref[at8(AHEAD + j), :] = lookup(t_al, code)
            at = Z_HEAT + 8 * j
            q1_ref[at8(AHEAD + 1 + j), :] = mend(zr_ref[at : at + 8, :], j, KEEP, HALO)
    for r in (AHEAD - 1, AHEAD):
        di_ref[at8(r), :], q1_ref[at8(r), :] = first_sweep(s_ref, q0_ref, r, power_row(pw_ref, n_p, r), h)
    r = AHEAD + 1
    di_ref[at8(r), :] = 1.0 / (h + row8(s_ref, r) * conduct_sum(s_ref, r))
    for r in range(AHEAD - 2, AHEAD + 2):
        t2 = second_sweep(s_ref, q1_ref, di_ref, r, power_row(pw_ref, n_p, r))
        t_keep[at8(r), :] = t2
        ea_ref[at8(r), :] = row8(al_ref, r) * t2
    ea_ref[at8(AHEAD + 2), :] = mend(zr_ref[Z_STRAIN : Z_STRAIN + 8, :], 2, KEEP, HALO)

    core = lax.axis_index(CORE)

    def other_half(x):
        return jnp.where(core == 0, x[:, half:wide], x[:, 0:half])

    def own_half(x):
        return jnp.where(core == 0, x[:, 0:half], x[:, half:wide])

    for g in range(2):
        t2 = row8(t_keep, AHEAD - 1 - g)
        keep_ref[8 * g : 8 * g + 8, :] = own_half(t2)
        x_ref[8 * g : 8 * g + 8, :] = other_half(t2)
    x_ref[16:24, :] = other_half(row8(t_in, FRONT + 2))

    count = mod_in.shape[0] // 8
    mrows = count - MHALO
    mwidth = mod_in.shape[1]
    n_m = count + MHALO
    for m in range(MHALO + 1 - FAR):
        i = AHEAD - 3 + 3 * m
        x = row8(ea_ref, i) + row8(ea_ref, i + 1) + row8(ea_ref, i + 2)
        st_ref[at8(MHALO - m), :] = restrict_columns(x)
    for f in range(FAR):
        at = Z_SUM + 8 * f
        st_ref[at8(FAR - 1 - f), :] = restrict_columns(mend(zr_ref[at : at + 8, :], 3 + f, KEEP, HALO))
    for m in range(1, count):
        st_ref[at8(MHALO + m), :] = row8(strain_in, m)
    values = splats(tab, 1)
    for i in range(MHALO):
        j = MHALO - 1 - i
        fields = []
        for f in range(4):
            body = zr_ref[Z_SOLID + ML * f : Z_SOLID + ML * f + 8, mcols * j : mcols * (j + 1)]
            body = jnp.where(sub_iota(mcols) < ML, body, 0.0)
            side = corners.field(j, f)
            fields.append(jnp.concatenate([body, side], axis=1))
        mod_ref[at8(i), :], root, mi_ref[at8(i), :] = moduli(values, fields[3])
        for f in range(3):
            uu_refs[f][at8(i), :] = root * fields[f]
    for ref, src in zip((mi_ref, mod_ref, *uu_refs), (mi_in, mod_in, *uu_in)):
        ref[8 * MHALO : 8 * n_m, :] = src[...]
    for i in range(n_m):
        sf_ref[at8(i), :] = row8(mod_ref, i) * row8(st_ref, i)
    sign = jnp.where(core == 0, 0.5, -0.5).astype(jnp.float32)
    for i in range(1, n_m - 1):
        load = row8(sf_ref, i)
        force = [
            0.5 * (next_sub(load) - prev_sub(load)),
            sign * (row8(sf_ref, i + 1) - row8(sf_ref, i - 1)),
            0.5 * (next_lane(load) - prev_lane(load)),
        ]
        inv = row8(mi_ref, i)
        inside = inv > 0.0
        if i <= MHALO:
            near = couple_sum([[row8(r, i - 1), row8(r, i), row8(r, i + 1)] for r in uu_refs])
            pre = [near[d] * (1.0 / STIFF_DIAG) - row8(uu_refs[d], i) for d in range(3)]
        else:
            pre = [row8(r, i - MHALO) for r in pre_in]
        inv = inv * (1.0 / STIFF_DIAG)
        for d in range(3):
            p_refs[d][at8(i), :] = jnp.where(inside, force[d] * inv + pre[d], 0.0)
    c_near = 2.0 * RHO1 / DELTA / STIFF_DIAG
    c_self = 1.0 + RHO1 * RHO0
    for i in range(2, n_m - 2):
        near = couple_sum([[row8(r, i - 1), row8(r, i), row8(r, i + 1)] for r in p_refs])
        inv = row8(mi_ref, i)
        for d in range(3):
            moved = row8(uu_refs[d], i) + c_self * row8(p_refs[d], i) + c_near * near[d]
            d_refs[d][at8(i), :] = moved * inv
    sub = sub_iota(mwidth)
    weight = jnp.where(sub < ML, (ML - sub).astype(jnp.float32) * (1.0 / (ML * (ML + 1) / 2.0)), 0.0)
    x_ref[24:32, :] = jnp.zeros((8, x_ref.shape[1]), jnp.float32)
    for g in range(mrows):
        i = MHALO + g
        u0, u2 = row8(d_refs[0], i), row8(d_refs[2], i)
        div = 0.5 * (next_sub(u0) - prev_sub(u0)) + 0.5 * (next_lane(u2) - prev_lane(u2))
        div = div + sign * (row8(d_refs[1], i + 1) - row8(d_refs[1], i - 1))
        stress = row8(mod_ref, i) * (div - 3.0 * row8(st_ref, i))
        die = jnp.sum(weight * stress, axis=0, keepdims=True)
        first, second = die[:, 0:LANES], die[:, LANES : 2 * LANES]
        keep_ref[16 + g : 17 + g, 0:LANES] = jnp.where(core == 0, first, second)
        x_ref[24 + g : 25 + g, 0:LANES] = jnp.where(core == 0, second, first)
        for d in range(3):
            u_ref[8 * (mrows * d + g) : 8 * (mrows * d + g) + 8, :] = row8(d_refs[d], i)[:, 0:mcols]


def k_out(rows, mrows, t_in, keep_ref, xr_ref, u_in, t_out, u_out, slow_ref, buf, die, wide_die, ubuf):
    half = slow_ref.shape[1]
    mcols = u_in.shape[1]
    core = lax.axis_index(CORE)

    def put(ref, at, x):
        count = ref.shape[0] * LANES // x.shape[1]
        for t, piece in enumerate(tiles(x)):
            ref[count * t + at : count * t + at + piece.shape[0], :] = piece

    def build(rev):
        lo = half if rev else 0
        for g in range(rows):
            i = rows - 1 - g if rev else g
            if g < 2:
                x = keep_ref[8 * g : 8 * g + 8, :]
            elif g < rows - 3:
                x = t_in[8 * (FRONT + g) : 8 * (FRONT + g) + 8, lo : lo + half]
            else:
                k = rows - 1 - g
                x = xr_ref[8 * k : 8 * k + 8, :]
            put(buf, 8 * i, x)
        for g in range(mrows):
            mine = 2 * mrows - 1 - g if rev else g
            theirs = g if rev else 2 * mrows - 1 - g
            die[mine : mine + 1, :] = keep_ref[16 + g : 17 + g, 0:LANES]
            die[theirs : theirs + 1, :] = xr_ref[24 + g : 25 + g, 0:LANES]
            for d in range(3):
                i = mrows - 1 - g if rev else g
                put(ubuf, 8 * (mrows * d + i), row8(u_in, mrows * d + g))

    @pl.when(core == 0)
    def _():
        build(False)

    @pl.when(core != 0)
    def _():
        build(True)

    for t in range(half // LANES):
        at = 8 * rows * t
        for l in range(DEPTH):
            t_out[l, :, tile_lanes(t)] = buf[pl.ds(at + l, rows, stride=8), :]
    for t in range(mcols // LANES):
        for d in range(3):
            for l in range(ML):
                u_out[d, l, :, tile_lanes(t)] = ubuf[pl.ds(8 * mrows * (3 * t + d) + l, mrows, stride=8), :]
    lane = lane_iota(2 * mrows)
    for t in range(half // LANES):
        x = gather_lanes(die[...], (lane + LANES * t) // 3)
        for b in range(3):
            wide_die[pl.ds(b, 2 * mrows, stride=3), :] = x
        slow = 1.0 + 0.2 * buf[pl.ds(8 * rows * t, rows, stride=8), :] + 0.5 * wide_die[...]
        slow_ref[:, tile_lanes(t)] = slow


def pairs(dims, sends):
    index = {}
    for r in range(dims[0]):
        for c in range(dims[1]):
            for a in range(dims[2]):
                index[(r, c, a)] = (r * dims[1] + c) * dims[2] + a
    out = []
    for source in index:
        target = sends(*source)
        if target in index:
            out.append((index[source], index[target]))
    return out


def per_device(temp, ids, power, mat, offset, heat_table, growth_table, modulus_table):
    axes = ("row", "col", "lay")
    dims = tuple(lax.axis_size(x) for x in axes)
    n_col = dims[1]
    _, rows, half = temp.shape
    _, _, mrows, mcols = offset.shape
    n_edges = 1 if n_col == 2 else 2
    n_t = half // LANES
    m_t = mcols // LANES

    def send(x, sends):
        return lax.ppermute(x, axes, pairs(dims, sends))

    def swap(r, c, a):
        return (r, c, 1 - a)

    def along(r, c, a):
        return (r + 1, c, 0) if a == 1 else (r - 1, c, 1)

    wide = 2 * half
    own = rows - 1
    kind = lax.broadcasted_iota(jnp.int32, (2, *temp.shape), 0)
    both = jnp.where(kind == 0, temp[None], power[None, None])
    tab = jnp.stack([heat_table, growth_table, modulus_table])
    tab = jnp.pad(tab, ((0, 0), (1, LANES - 1 - tab.shape[1])))
    (tab,) = call(k_tables, [(16 * (NMAT + 1) + 8, LANES)], [tab])
    n = 16 * HALO
    n_far = 8 * far_rows(rows)
    cells, one = call(k_rows, [(16 * rows * n_t, LANES), ((n + 16) * n_t + n_far, LANES)], [both, ids])
    got1 = send(one, swap)
    two, mg = call(
        functools.partial(k_rest, n_edges),
        [
            ((16 * (rows - 1 - HALO) + rows - 16) * n_t + 32 * MHALO * m_t + 8 * n_edges, LANES),
            (32 * mrows, mcols),
        ],
        [both, cells, offset, mat],
        scratch=[(32 * mrows * m_t, LANES)],
    )
    got2 = send(two, swap)
    *own_part, far = call(
        functools.partial(k_half, n_edges),
        [(8 * HALO, half)] * 3 + [(n_far * n_edges, LANES)],
        [tab, both, cells],
    )
    n_c = 32 + n_far - 8 * (-4 * (mrows - MHALO) * MSPAN // LANES) + 8
    z, first_rows, *edges = call(
        functools.partial(k_edge, n_edges),
        [(far_place(n_edges, -1, wide)[0].stop, wide), (n + 16, wide)] + [(32, LANES)] * n_edges,
        [tab, both, cells, got1, mg, *own_part],
        cost=EDGE_COST,
        scratch=[(8 * HALO, wide)] * 5,
    )
    leaving = [z, *edges]
    leaving = call(
        functools.partial(k_beside, n_edges, rows, n_t),
        [(n_c, LANES)] * n_edges + [x.shape for x in leaving],
        [far, got1, got2, mg] + leaving,
        aliases={4 + k: n_edges + k for k in range(len(leaving))},
    )
    beside, z, near = leaving[:n_edges], leaving[n_edges], leaving[n_edges + 1 :]
    zr = send(z, along)
    if n_edges == 1:
        sides = [send(beside[0], lambda r, c, a: (r, 1 - c, a))]
        corners = [send(near[0], lambda r, c, a: along(r, 1 - c, a))]
    else:
        sides = [send(beside[0], lambda r, c, a: (r, c + 1, a)), send(beside[1], lambda r, c, a: (r, c - 1, a))]
        corners = [
            send(near[0], lambda r, c, a: along(r, c + 1, a)),
            send(near[1], lambda r, c, a: along(r, c - 1, a)),
        ]
    w, src, mw = call(
        functools.partial(k_chip, rows),
        [(16 * own, wide), (rows, wide), (32 * (mrows + MHALO), mcols)],
        [both, cells, got2, mg, first_rows],
    )
    width = wide + LANES
    mwidth = mcols + LANES
    n_w = 8 * (rows + FRONT + 4)
    inner = call(
        functools.partial(k_inner, n_edges, n_col, rows),
        [(n_w, width)] * 7 + [(8 * (mrows + MHALO), mwidth)],
        [tab, w, src] + sides,
        scratch=[(n_w * (width // LANES), LANES)],
    )
    t2 = inner[5]
    solid = call(
        functools.partial(k_mech, n_edges, n_col, rows), [(8 * (mrows + MHALO), mwidth)] * 8, [tab, mw] + sides
    )
    n_h = 8 * (AHEAD + HALO + 5)
    n_m = 8 * (mrows + 2 * MHALO)
    x, keep, u = call(
        functools.partial(k_outer, n_edges, n_col, rows),
        [(32, half), (24, half), (24 * mrows, mcols)],
        [tab, zr] + sides + corners + list(inner) + [src] + list(solid),
        scratch=[(n_h, width)] * 7
        + [(n_h * (width // LANES), LANES)]
        + [(n_m, mwidth)] * 13
        + [(8 * HALO, LANES)] * 4,
    )
    xr = send(x, swap)
    t_out, u_out, slow = call(
        functools.partial(k_out, rows, mrows),
        [temp.shape, offset.shape, power.shape],
        [t2, keep, xr, u],
        scratch=[
            (8 * rows * n_t, LANES),
            (2 * mrows, LANES),
            (rows, LANES),
            (24 * mrows * m_t, LANES),
        ],
    )
    return t_out, u_out, slow


def solution(mesh):
    placed = (
        P("grp", "row", ("col", "lay")),
        P("grp", "row", ("col", "lay")),
        P(("grp", "row"), ("col", "lay")),
        P("grp", ("row", "lay"), "col"),
        P(None, "grp", ("row", "lay"), "col"),
        P(),
        P(),
        P(),
    )
    return jax.shard_map(
        per_device,
        mesh=mesh,
        in_specs=placed,
        out_specs=(
            P("grp", "row", ("col", "lay")),
            P(None, "grp", ("row", "lay"), "col"),
            P(("grp", "row"), ("col", "lay")),
        ),
        check_vma=False,
    )
```

```python
import functools

import jax
import jax.numpy as jnp
from jax import lax
from jax.experimental import pallas as pl
from jax.experimental.pallas import tpu as pltpu
from jax.sharding import PartitionSpec as P

DEPTH = 8
ML = 6
LANES = 128
HALO = 11
MHALO = 3

STIFF_DIAG = 12.0
THETA = 1.0
DELTA = 0.75
SIGMA = THETA / DELTA
RHO0 = 1.0 / SIGMA
RHO1 = 1.0 / (2.0 * SIGMA - RHO0)

VMEM = pl.BlockSpec(memory_space=pltpu.VMEM)
FRONT = 9
AHEAD = 5
STEP = 3
SPAN = 11
MSPAN = 8
NMAT = 16
FAR = 2
EDGE_COST = 10**10
FAR_ROW = 9 - 3 * FAR
KEEP = 3
Z_TEMP, Z_CODE, Z_HEAT, Z_STRAIN, Z_SUM, Z_SOLID, Z_POWER, Z_FAR = 0, 16, 40, 56, 64, 80, 104, 112
CORE = "lay"
UNROLL_STRAIN = 3


def call(kernel, outs, args, scratch=(), specs=None, aliases=None, cost=0):
    return pl.pallas_call(
        kernel,
        out_shape=[jax.ShapeDtypeStruct(s, jnp.float32) for s in outs],
        in_specs=specs or [VMEM] * len(args),
        out_specs=[VMEM] * len(outs),
        input_output_aliases=aliases or {},
        cost_estimate=pl.CostEstimate(flops=cost, bytes_accessed=0, transcendentals=0) if cost else None,
        scratch_shapes=[pltpu.VMEM(s, jnp.float32) if isinstance(s, tuple) else s for s in scratch],
        compiler_params=pltpu.CompilerParams(vmem_limit_bytes=16 * 1024 * 1024),
    )(*args)


def lane_iota(rows=8):
    return lax.broadcasted_iota(jnp.int32, (rows, LANES), 1)


def sub_iota(width):
    return lax.broadcasted_iota(jnp.int32, (8, width), 0)


def tile_lanes(t):
    return slice(LANES * t, LANES * (t + 1))


def tiles(x):
    return [x[:, tile_lanes(t)] for t in range(x.shape[1] // LANES)]


def table_of(ref, k):
    return jnp.broadcast_to(ref[k : k + 1, :], (8, LANES))


def gather_lanes(table, index):
    return jnp.take_along_axis(table, index, axis=1, mode="promise_in_bounds")


def lookup(table, code):
    return jnp.concatenate([gather_lanes(table, c.astype(jnp.int32)) for c in tiles(code)], axis=1)


def k_tables(tab, out_ref):
    for k, table in enumerate((jnp.sqrt(table_of(tab, 0)), table_of(tab, 2))):
        for m in range(NMAT + 1):
            at = 8 * ((NMAT + 1) * k + m)
            out_ref[at : at + 8, :] = jnp.broadcast_to(table[:, m : m + 1], (8, LANES))
    out_ref[16 * (NMAT + 1) : 16 * (NMAT + 1) + 8, :] = table_of(tab, 1)


def splats(tab, k):
    return [row8(tab, (NMAT + 1) * k + m) for m in range(NMAT + 1)]


def expansion_table(tab):
    return row8(tab, 2 * (NMAT + 1))


def choose(lists, code):
    out = [[] for _ in lists]
    for c in tiles(code):
        c = c.astype(jnp.int32)
        bits = [(c & (1 << k)) != 0 for k in range(5)]
        for n, values in enumerate(lists):
            level = values[:16]
            for k in range(4):
                level = [jnp.where(bits[k], b, a) for a, b in zip(level[::2], level[1::2])]
            out[n].append(jnp.where(bits[4], values[16], level[0]))
    return [jnp.concatenate(x, axis=1) for x in out]


def prev_lane(x):
    return pltpu.roll(x, 1, 1)


def next_lane(x):
    return pltpu.roll(x, x.shape[1] - 1, 1)


def prev_sub(x):
    return pltpu.roll(x, 1, 0)


def next_sub(x):
    return pltpu.roll(x, 7, 0)


def at8(i):
    return pl.ds(8 * i, 8) if isinstance(i, int) else pl.ds(pl.multiple_of(8 * i, 8), 8)


def row8(ref, i):
    return ref[at8(i), :]


def turned(core, last, g):
    return core * last + (1 - 2 * core) * g


def k_rows(in_ref, id_ref, a_ref, one_ref):
    other = 1 - lax.axis_index(CORE)
    rows = in_ref.shape[2]
    n_t = in_ref.shape[3] // LANES
    n = 16 * HALO
    for t in range(n_t):
        at = 16 * rows * t
        for l in range(DEPTH):
            a_ref[pl.ds(at + l, rows, stride=16), :] = in_ref[0, l, :, tile_lanes(t)]
            a_ref[pl.ds(at + DEPTH + l, rows, stride=16), :] = (id_ref[l, :, tile_lanes(t)] + 1).astype(jnp.float32)
    for t in range(n_t):
        to = (n + 16) * t
        for g in range(HALO):
            i = 16 * (rows * t + turned(other, rows - 1, g))
            one_ref[to + 16 * g : to + 16 * g + 16, :] = a_ref[pl.ds(pl.multiple_of(i, 16), 16), :]
        for b in range(2):
            one_ref[to + n + 8 * b : to + n + 8 * b + 8, :] = power_rows(in_ref, other, b, t)


def k_rest(n_edges, in_ref, a_ref, u_ref, mat_ref, two_ref, mg_ref, m_ref):
    core = lax.axis_index(CORE)
    other = 1 - core
    rows = in_ref.shape[2]
    n_t = in_ref.shape[3] // LANES
    mrows = mat_ref.shape[1]
    mcols = mat_ref.shape[2]
    m_t = mcols // LANES
    m_ref[...] = jnp.zeros(m_ref.shape, jnp.float32)
    for t in range(m_t):
        at = 32 * mrows * t
        for l in range(ML):
            for f in range(3):
                m_ref[pl.ds(at + 8 * f + l, mrows, stride=32), :] = u_ref[f, l, :, tile_lanes(t)]
            m_ref[pl.ds(at + 24 + l, mrows, stride=32), :] = (mat_ref[l, :, tile_lanes(t)] + 1).astype(jnp.float32)
        for g in range(mrows):
            i = 32 * (mrows * t + turned(core, mrows - 1, g))
            mg_ref[32 * g : 32 * g + 32, tile_lanes(t)] = m_ref[pl.ds(pl.multiple_of(i, 32), 32), :]
    for e in range(n_edges):
        side = edge_side(n_edges, e)
        fields = []
        for g in range(MHALO):
            i = 32 * (mrows * side * (m_t - 1) + turned(core, mrows - 1, mrows - 1 - g))
            fields += [m_ref[pl.ds(pl.multiple_of(i + 8 * f, 8), 8), :] for f in range(4)]
        at = two_ref.shape[0] - 8 * (n_edges - e)
        (two_ref[at : at + 8, :],) = packed(side, fields, MSPAN, MHALO)
    for k, x in enumerate(far_strip(in_ref, a_ref, other, core * (n_t - 1), core)):
        at = two_ref.shape[0] - 8 * (n_edges + far_rows(rows) - k)
        two_ref[at : at + 8, :] = x
    rest = 16 * (rows - 1 - HALO)
    for t in range(n_t):
        to = (rest + rows - 16) * t
        for g in range(HALO, rows - 1):
            i = 16 * (rows * t + turned(other, rows - 1, g))
            k = to + 16 * (g - HALO)
            two_ref[k : k + 16, :] = a_ref[pl.ds(pl.multiple_of(i, 16), 16), :]
        for b in range(2, rows // 8):
            two_ref[to + rest + 8 * (b - 2) : to + rest + 8 * (b - 1), :] = power_rows(in_ref, other, b, t)
    for t in range(m_t):
        for g in range(MHALO):
            i = 32 * (mrows * t + turned(core, mrows - 1, mrows - 1 - g))
            k = (rest + rows - 16) * n_t + 32 * (MHALO * t + g)
            two_ref[k : k + 32, :] = m_ref[pl.ds(pl.multiple_of(i, 32), 32), :]


def power_rows(in_ref, turn, b, t):
    rows = in_ref.shape[2]
    lanes = tile_lanes(t) if isinstance(t, int) else pl.ds(pl.multiple_of(LANES * t, LANES), LANES)
    x = in_ref[1, 0, at8(turned(turn, rows // 8 - 1, b)), lanes]
    return jnp.take_along_axis(x, turned(turn, 7, sub_iota(LANES)), axis=0, mode="promise_in_bounds")


def far_strip(in_ref, a_ref, turn, t, side):
    rows = in_ref.shape[2]
    blocks = []
    for g in range(HALO, rows - 1):
        i = 16 * (rows * t + turned(turn, rows - 1, g))
        blocks += [a_ref[pl.ds(pl.multiple_of(i + k, 8), 8), :] for k in (0, 8)]
    blocks += [power_rows(in_ref, turn, b, t) for b in range(2, rows // 8)]
    return packed(side, blocks, SPAN, HALO)


def edge_side(n_edges, e):
    return 1 - lax.axis_index("col") if n_edges == 1 else 1 - e


def edge_tile(side, width):
    if isinstance(side, int):
        return tile_lanes(side * (width // LANES - 1))
    return pl.ds(pl.multiple_of(side * (width - LANES), LANES), LANES)


def packed(side, blocks, span, keep):
    lane = lane_iota()
    per = LANES // span
    out = []
    for i in range(0, len(blocks), per):
        acc = jnp.zeros((8, LANES), jnp.float32)
        for k, x in enumerate(blocks[i : i + per]):
            acc = jnp.where(lane // span == k, pltpu.roll(x, span * k + side * keep, 1), acc)
        out.append(acc)
    return out


def far_rows(rows):
    return -(-(2 * (rows - 1 - HALO) + rows // 8 - 2) // (LANES // SPAN))


def k_half(n_edges, tab, in_ref, a_ref, s_ref, q0_ref, al_ref, far_ref):
    core = lax.axis_index(CORE)
    rows = in_ref.shape[2]
    n_t = in_ref.shape[3] // LANES
    v_s = splats(tab, 0)
    t_al = expansion_table(tab)
    for t in range(n_t):
        for g in range(HALO):
            i = 16 * (rows * t + turned(core, rows - 1, g))
            code = a_ref[pl.ds(pl.multiple_of(i + 8, 8), 8), :]
            (x,) = choose([v_s], code)
            s_ref[at8(g), tile_lanes(t)] = x
            q0_ref[at8(g), tile_lanes(t)] = x * a_ref[pl.ds(pl.multiple_of(i, 16), 8), :]
            if 2 <= g < 9:
                al_ref[at8(g), tile_lanes(t)] = lookup(t_al, code)
    for e in range(n_edges):
        side = edge_side(n_edges, e)
        for k, x in enumerate(far_strip(in_ref, a_ref, core, side * (n_t - 1), side)):
            at = 8 * (far_rows(rows) * e + k)
            far_ref[at : at + 8, :] = x


def k_edge(n_edges, tab, in_ref, a_ref, got_ref, mg_ref, s_own, q0_own, al_own, z_ref, w_ref, *refs):
    core = lax.axis_index(CORE)
    wide = z_ref.shape[1]
    half = wide // 2
    n_t = half // LANES
    rows = in_ref.shape[2]
    mcols = mg_ref.shape[1]
    n = 16 * HALO
    edge_refs, (s_ref, q0_ref, al_ref, q1_ref, di_ref) = refs[:n_edges], refs[n_edges:]
    v_s = splats(tab, 0)
    t_al = expansion_table(tab)

    def build(first):
        for t in range(n_t):
            lanes = tile_lanes(t if first else n_t + t)
            for g in range(HALO):
                i = 16 * (rows * t + (g if first else rows - 1 - g))
                w_ref[16 * g : 16 * g + 16, lanes] = a_ref[i : i + 16, :]
            for b in range(2):
                w_ref[n + 8 * b : n + 8 * b + 8, lanes] = power_rows(in_ref, 0 if first else 1, b, t)
            lanes = tile_lanes(n_t + t if first else t)
            at = (n + 16) * t
            w_ref[0 : n + 16, lanes] = got_ref[at : at + n + 16, :]
            for g in range(HALO):
                code = got_ref[at + 16 * g + 8 : at + 16 * g + 16, :]
                (x,) = choose([v_s], code)
                s_ref[at8(g), lanes] = x
                q0_ref[at8(g), lanes] = x * got_ref[at + 16 * g : at + 16 * g + 8, :]
                if 2 <= g < 9:
                    al_ref[at8(g), lanes] = lookup(t_al, code)
        lanes = slice(0, half) if first else slice(half, wide)
        for dst, src in ((s_ref, s_own), (q0_ref, q0_own), (al_ref, al_own)):
            dst[:, lanes] = src[...]

    @pl.when(core == 0)
    def _():
        build(True)

    @pl.when(core != 0)
    def _():
        build(False)

    for g in range(2):
        z_ref[Z_TEMP + 8 * g : Z_TEMP + 8 * g + 8, :] = w_ref[16 * g : 16 * g + 8, :]
    for g in range(3):
        z_ref[Z_CODE + 8 * g : Z_CODE + 8 * g + 8, :] = w_ref[16 * g + 8 : 16 * g + 16, :]
    z_ref[Z_POWER : Z_POWER + 8, :] = w_ref[n : n + 8, :]
    z_ref[Z_FAR:, :] = jnp.zeros((z_ref.shape[0] - Z_FAR, wide), jnp.float32)
    for g in range(MHALO):
        for f in range(4):
            at = Z_SOLID + ML * f
            z_ref[at : at + ML, mcols * g : mcols * (g + 1)] = mg_ref[32 * g + 8 * f : 32 * g + 8 * f + ML, :]
    for e in range(n_edges):
        side = edge_side(n_edges, e)
        lanes, mlanes = edge_tile(side, wide), edge_tile(side, mcols)
        blocks = [w_ref[8 * i : 8 * i + 8, lanes] for i in range(2 * HALO)]
        blocks += [w_ref[n + 8 * b : n + 8 * b + 8, lanes] for b in range(2)]
        fields = [mg_ref[8 * i : 8 * i + 8, mlanes] for i in range(4 * MHALO)]
        near = packed(side, blocks, SPAN, HALO) + packed(side, fields, MSPAN, MHALO)
        strip = blocks[4 : 2 * HALO : 2] + blocks[7 : 2 * HALO : 2] + blocks[2 * HALO + 1 :]
        for k, x in enumerate(packed(side, strip, SPAN, HALO)):
            z_ref[far_place(e, k, wide)] = x
        for k, x in enumerate(near):
            edge_refs[e][8 * k : 8 * k + 8, :] = x
    h = sink(wide)
    top = sub_iota(wide) == 0
    powers = {
        g: jnp.where(top, jnp.broadcast_to(w_ref[n + g : n + g + 1, :], (8, wide)), 0.0) for g in range(1, HALO - 1)
    }
    for g in range(1, HALO - 1):
        di_ref[at8(g), :], q1_ref[at8(g), :] = first_sweep(s_ref, q0_ref, g, powers[g], h, True)
    z_ref[Z_HEAT : Z_HEAT + 16, :] = q1_ref[8:24, :]

    def expansion(g):
        return row8(al_ref, g) * second_sweep(s_ref, q1_ref, di_ref, g, powers[g], True)

    z_ref[Z_STRAIN : Z_STRAIN + 8, :] = expansion(2)
    for f in range(FAR):
        g = FAR_ROW + 3 * f
        x = expansion(g) + expansion(g + 1) + expansion(g + 2)
        z_ref[Z_SUM + 8 * f : Z_SUM + 8 * f + 8, :] = x


def far_tiles():
    return -(-(2 * HALO - 4) // (LANES // SPAN))


def far_place(e, k, wide):
    q = far_tiles() * e + k
    at = Z_FAR + 8 * (q // (wide // LANES))
    return slice(at, at + 8), tile_lanes(q % (wide // LANES))


def k_beside(n_edges, rows, far_ref, got_ref, mg_ref, z_ref, *refs):
    near_refs, c_refs = refs[:n_edges], refs[n_edges : 2 * n_edges]
    core = lax.axis_index(CORE)
    mrows = mg_ref.shape[0] // 32
    for e in range(n_edges):
        side = edge_side(n_edges, e)
        mlanes = edge_tile(side, mg_ref.shape[1])
        fields = [mg_ref[8 * i : 8 * i + 8, mlanes] for i in range(4 * MHALO, 4 * mrows)]
        far = [near_refs[e][8 * k : 8 * k + 8, :] for k in range(4)]
        for k in range(far_rows(rows)):
            at = got_ref.shape[0] - 8 * (n_edges + far_rows(rows) - k)
            x = row8(far_ref, far_rows(rows) * e + k)
            far.append(jnp.where(core == side, x, got_ref[at : at + 8, :]))
        far += packed(side, fields, MSPAN, MHALO)
        at = got_ref.shape[0] - 8 * (n_edges - e)
        far.append(got_ref[at : at + 8, :])
        for k, x in enumerate(far):
            c_refs[e][8 * k : 8 * k + 8, :] = x


def k_chip(rows, in_ref, a_ref, got_ref, mg_ref, first_ref, w_ref, src_ref, mw_ref):
    core = lax.axis_index(CORE)
    n_t = w_ref.shape[1] // LANES // 2
    mrows = mg_ref.shape[0] // 32
    n = 16 * HALO
    rest = 16 * (rows - 1 - HALO)
    w_ref[0:n, :] = first_ref[0:n, :]
    src_ref[0:16, :] = first_ref[n : n + 16, :]

    def build(first):
        for t in range(n_t):
            lanes = tile_lanes(t if first else n_t + t)
            for g in range(HALO, rows - 1):
                i = 16 * (rows * t + (g if first else rows - 1 - g))
                w_ref[16 * g : 16 * g + 16, lanes] = a_ref[i : i + 16, :]
            for b in range(2, rows // 8):
                src_ref[8 * b : 8 * b + 8, lanes] = power_rows(in_ref, 0 if first else 1, b, t)
            lanes = tile_lanes(n_t + t if first else t)
            at = (rest + rows - 16) * t
            w_ref[n : n + rest, lanes] = got_ref[at : at + rest, :]
            src_ref[16:rows, lanes] = got_ref[at + rest : at + rest + rows - 16, :]

    @pl.when(core == 0)
    def _():
        build(True)

    @pl.when(core != 0)
    def _():
        build(False)

    mw_ref[0 : 32 * mrows, :] = mg_ref[...]
    for t in range(mw_ref.shape[1] // LANES):
        at = (rest + rows - 16) * n_t + 32 * MHALO * t
        mw_ref[32 * mrows : 32 * (mrows + MHALO), tile_lanes(t)] = got_ref[at : at + 32 * MHALO, :]


class Sides:
    def __init__(self, n_col, rows, mrows, from_left, from_right):
        self.left = from_left
        self.right = from_right
        self.rows = rows
        self.mrows = mrows
        lane = lane_iota()
        col = lax.axis_index("col")
        self.masks = {
            w: ((lane < w) & (col < n_col - 1), (lane >= LANES - w) & (col > 0)) for w in (HALO, MHALO)
        }
        self.only = self.left is self.right
        self.side = col

    def take(self, v, k, span, width):
        right_mask, left_mask = self.masks[width]
        x = row8(self.right, v)
        if self.only:
            x = pltpu.roll(x, LANES - span * k - self.side * width, 1)
            return jnp.where(right_mask | left_mask, x, 0.0)
        r = pltpu.roll(x, (LANES - span * k) % LANES, 1)
        l = pltpu.roll(row8(self.left, v), LANES - span * k - width, 1)
        return jnp.where(right_mask, r, jnp.where(left_mask, l, 0.0))

    def block(self, first, i, span, width):
        per = LANES // span
        return self.take(first + i // per, i % per, span, width)

    def cell(self, g, kind):
        if g < HALO:
            return self.block(0, 2 * g + kind, SPAN, HALO)
        return self.block(4, 2 * (g - HALO) + kind, SPAN, HALO)

    def power(self, b):
        if b < 2:
            return self.block(0, 2 * HALO + b, SPAN, HALO)
        return self.block(4, 2 * (self.rows - 1 - HALO) + b - 2, SPAN, HALO)

    def field(self, m, f):
        if m < MHALO:
            return self.block(3, 4 * m + f, MSPAN, MHALO)
        first = 4 + far_rows(self.rows)
        if m < self.mrows:
            return self.block(first, 4 * (m - MHALO) + f, MSPAN, MHALO)
        first += -(-4 * (self.mrows - MHALO) * MSPAN // LANES)
        return self.block(first, 4 * (m - self.mrows) + f, MSPAN, MHALO)


def spread_power(ref, n, blocks):
    ref[...] = jnp.zeros(ref.shape, jnp.float32)
    count = ref.shape[0] // (n * 8)
    for first, x in blocks:
        for t, piece in enumerate(tiles(x)):
            ref[pl.ds(8 * (n * t + first), piece.shape[0], stride=8), :] = piece
    return count


def power_row(ref, n, i):
    count = ref.shape[0] // (n * 8)
    return jnp.concatenate([row8(ref, n * t + i) for t in range(count)], axis=1)


def conduct_sum(ref, i, closed=False):
    x = row8(ref, i)
    sub = sub_iota(x.shape[1])
    before, after = prev_lane(x), next_lane(x)
    if closed:
        lane = lax.broadcasted_iota(jnp.int32, x.shape, 1)
        before = jnp.where(lane > 0, before, 0.0)
        after = jnp.where(lane < x.shape[1] - 1, after, 0.0)
    total = row8(ref, i - 1) + row8(ref, i + 1) + before + after
    total = total + jnp.where(sub < DEPTH - 1, next_sub(x), 0.0)
    return total + jnp.where(sub > 0, prev_sub(x), 0.0)


def sink(width):
    return jnp.where(sub_iota(width) == DEPTH - 1, 2.0, 0.2).astype(jnp.float32)


def to_solid_layers(y):
    return jnp.where(sub_iota(y.shape[1]) < 3, y, next_sub(y)) * (1.0 / 9.0)


def gather_main(pieces):
    lane = 3 * lane_iota()
    out = []
    for j in range(len(pieces) // 3):
        total = None
        for k in range(3):
            got = None
            for t in range(3):
                g = gather_lanes(pieces[3 * j + t], (lane + k) & (LANES - 1))
                got = g if got is None else jnp.where(lane + k >= LANES * t, g, got)
            total = got if total is None else total + got
        out.append(total)
    return out


def gather_sides(piece):
    lane = lane_iota()
    first = LANES - MHALO
    inside = (lane < MHALO) | (lane >= first)
    index = jnp.where(lane < MHALO, 3 * lane, jnp.where(lane >= first, LANES - 9 + 3 * (lane - first), 0))
    total = gather_lanes(piece, index) + gather_lanes(piece, index + 1) + gather_lanes(piece, index + 2)
    return jnp.where(inside, total, 0.0)


def restrict_columns(x):
    pieces = tiles(x)
    return to_solid_layers(jnp.concatenate(gather_main(pieces[:-1]) + [gather_sides(pieces[-1])], axis=1))


def first_sweep(s_ref, q0_ref, i, power, h, closed=False):
    s = row8(s_ref, i)
    inv = 1.0 / (h + s * conduct_sum(s_ref, i, closed))
    return inv, s * ((power + s * conduct_sum(q0_ref, i, closed)) * inv)


def second_sweep(s_ref, q1_ref, di_ref, i, power, closed=False):
    return (power + row8(s_ref, i) * conduct_sum(q1_ref, i, closed)) * row8(di_ref, i)


def k_inner(n_edges, n_col, rows, tab, w_ref, src_ref, *refs):
    sides = Sides(n_col, rows, rows // 6, refs[0], refs[n_edges - 1])
    s_ref, al_ref, q0_ref, q1_ref, di_ref, t_ref, ea_ref, strain_ref, pw_ref = refs[n_edges:]
    own = rows - 1
    width = src_ref.shape[1] + LANES
    t_al = expansion_table(tab)
    v_s = splats(tab, 0)
    side_power = jnp.concatenate([sides.power(k) for k in range(rows // 8)], axis=0)
    n_p = s_ref.shape[0] // 8
    spread_power(pw_ref, n_p, [(FRONT, jnp.concatenate([src_ref[...], side_power], axis=1))])
    h = sink(width)

    for i in range(0, own + 2 * STEP + 2, STEP):
        later = []
        for g in range(i, min(i + STEP, own)):
            temp = jnp.concatenate([w_ref[16 * g : 16 * g + 8, :], sides.cell(g, 0)], axis=1)
            code = jnp.concatenate([w_ref[16 * g + 8 : 16 * g + 16, :], sides.cell(g, 1)], axis=1)
            s, al = choose([v_s], code)[0], lookup(t_al, code)
            later += [(s_ref, FRONT + g, s), (q0_ref, FRONT + g, s * temp), (al_ref, FRONT + g, al)]
        for g in range(max(1, i - STEP - 1), min(i - 1, own - 1)):
            r = FRONT + g
            inv, q1 = first_sweep(s_ref, q0_ref, r, power_row(pw_ref, n_p, r), h)
            later += [(di_ref, r, inv), (q1_ref, r, q1)]
        for g in range(max(2, i - 2 * STEP - 2), min(i - STEP - 2, own - 2)):
            r = FRONT + g
            t2 = second_sweep(s_ref, q1_ref, di_ref, r, power_row(pw_ref, n_p, r))
            later += [(t_ref, r, t2), (ea_ref, r, row8(al_ref, r) * t2)]
        for ref, r, x in later:
            ref[at8(r), :] = x

    def strain(m, carry):
        i = FRONT + 3 * m
        x = row8(ea_ref, i) + row8(ea_ref, i + 1) + row8(ea_ref, i + 2)
        strain_ref[at8(m), :] = restrict_columns(x)
        return carry

    lax.fori_loop(1, (own - 2) // 3, strain, 0, unroll=UNROLL_STRAIN)


def couple_sum(rows3):
    near = [[None] * 3 for _ in range(3)]
    for j in range(3):
        below, mid, above = rows3[j]
        near[0][j] = next_sub(mid) + prev_sub(mid)
        near[1][j] = above + below
        near[2][j] = next_lane(mid) + prev_lane(mid)
    out = []
    for i in range(3):
        j, k = [x for x in range(3) if x != i]
        main = near[i][i] + 0.5 * (near[j][i] + near[k][i])
        side = (near[i][j] + near[j][j]) + (near[i][k] + near[k][k])
        out.append(main + 0.25 * side)
    return out


def moduli(values, code):
    (mod,) = choose([values], code)
    inside = mod > 0.0
    root = jnp.sqrt(mod)
    return mod, root, jnp.where(inside, 1.0 / jnp.where(inside, root, 1.0), 0.0)


def k_mech(n_edges, n_col, rows, tab, mw_ref, *refs):
    sides = Sides(n_col, rows, rows // 6, refs[0], refs[n_edges - 1])
    mi_ref, mod_ref = refs[n_edges : n_edges + 2]
    uu_refs = refs[n_edges + 2 : n_edges + 5]
    pre_refs = refs[n_edges + 5 : n_edges + 8]
    values = splats(tab, 1)
    count = mw_ref.shape[0] // 32
    for m in range(count):
        fields = []
        for f in range(4):
            side = sides.field(m, f)
            fields.append(jnp.concatenate([mw_ref[32 * m + 8 * f : 32 * m + 8 * f + 8, :], side], axis=1))
        mod_ref[at8(m), :], root, mi_ref[at8(m), :] = moduli(values, fields[3])
        for f in range(3):
            uu_refs[f][at8(m), :] = root * fields[f]
    for m in range(1, count - 1):
        near = couple_sum([[row8(r, m - 1), row8(r, m), row8(r, m + 1)] for r in uu_refs])
        for d in range(3):
            pre_refs[d][at8(m), :] = near[d] * (1.0 / STIFF_DIAG) - row8(uu_refs[d], m)


def edge_patch(n_edges, e, corners, zr_ref, v_s, t_al, scratch):
    s_ref, q0_ref, q1_ref, di_ref = scratch
    side = edge_side(n_edges, e)
    lanes = edge_tile(side, zr_ref.shape[1])
    lane = lane_iota()
    mine = ((lane >= LANES - HALO) & (side == 1)) | ((lane < HALO) & (side == 0))
    per = LANES // SPAN

    def strip(i):
        x = zr_ref[far_place(e, i // per, zr_ref.shape[1])]
        return pltpu.roll(x, LANES - SPAN * (i % per) - side * HALO, 1)

    def cell(j, kind):
        held = 2 + kind
        if j < held:
            at = (Z_TEMP, Z_CODE)[kind] + 8 * j
            x = zr_ref[at : at + 8, lanes]
        else:
            x = strip(kind * (HALO - 2) + j - held)
        return jnp.where(mine, x, corners.cell(j, kind))

    codes = {}
    for j in range(HALO):
        codes[j] = cell(j, 1)
        (s,) = choose([v_s], codes[j])
        s_ref[at8(j), :] = s
        q0_ref[at8(j), :] = s * cell(j, 0)
    power = [
        jnp.where(mine, zr_ref[Z_POWER : Z_POWER + 8, lanes], corners.power(0)),
        jnp.where(mine, strip(2 * HALO - 5), corners.power(1)),
    ]
    top = sub_iota(LANES) == 0
    h = sink(LANES)

    def power_of(j):
        x = power[j // 8][j % 8 : j % 8 + 1, :]
        return jnp.where(top, jnp.broadcast_to(x, (8, LANES)), 0.0)

    heat = {}
    for j in range(1, HALO - 1):
        di_ref[at8(j), :], heat[j] = first_sweep(s_ref, q0_ref, j, power_of(j), h)
        q1_ref[at8(j), :] = heat[j]

    def expansion(j):
        return lookup(t_al, codes[j]) * second_sweep(s_ref, q1_ref, di_ref, j, power_of(j))

    out = [heat[1], heat[2], expansion(2)]
    for f in range(FAR):
        j = FAR_ROW + 3 * f
        out.append(expansion(j) + expansion(j + 1) + expansion(j + 2))
    return out


def k_outer(n_edges, n_col, rows, tab, zr_ref, *refs):
    sides = Sides(n_col, rows, rows // 6, refs[0], refs[n_edges - 1])
    corners = Sides(n_col, rows, rows // 6, refs[n_edges], refs[2 * n_edges - 1])
    rest = refs[2 * n_edges :]
    s_in, al_in, q0_in, q1_in, di_in, t_in, ea_in, strain_in, src_ref = rest[:9]
    mi_in, mod_in = rest[9:11]
    uu_in, pre_in = rest[11:14], rest[14:17]
    x_ref, keep_ref, u_ref = rest[17:20]
    s_ref, q0_ref, q1_ref, di_ref, al_ref, ea_ref, t_keep, pw_ref = rest[20:28]
    st_ref, mi_ref, mod_ref, sf_ref = rest[28:32]
    uu_refs, p_refs, d_refs = rest[32:35], rest[35:38], rest[38:41]
    own = rows - 1
    wide = zr_ref.shape[1]
    half = wide // 2
    width = wide + LANES
    mcols = mod_in.shape[1] - LANES
    t_al = expansion_table(tab)
    v_s = splats(tab, 0)
    for g in range(3):
        k = AHEAD - 1 - g
        for dst, src in ((s_ref, s_in), (al_ref, al_in), (q0_ref, q0_in)):
            dst[at8(k), :] = row8(src, FRONT + g)
    ea_ref[at8(AHEAD - 3), :] = row8(ea_in, FRONT + 2)
    for g in (1, 2):
        q1_ref[at8(AHEAD - 1 - g), :] = row8(q1_in, FRONT + g)
    di_ref[at8(AHEAD - 2), :] = row8(di_in, FRONT + 1)
    n_p = s_ref.shape[0] // 8
    near = jnp.concatenate([src_ref[0:8, :], sides.power(0)], axis=1)
    far = jnp.concatenate([zr_ref[Z_POWER : Z_POWER + 8, :], corners.power(0)], axis=1)
    spread_power(
        pw_ref,
        n_p,
        [(AHEAD - 1, near[0:1, :]), (AHEAD - 2, near[1:2, :]), (AHEAD, far)],
    )
    h = sink(width)

    lane = lane_iota()
    has_left, has_right = sides.side > 0, sides.side < n_col - 1
    patches = [edge_patch(n_edges, e, corners, zr_ref, v_s, t_al, rest[41:45]) for e in range(n_edges)]

    def mend(x, k, near, reach):
        pieces = tiles(x)
        right, left = patches[0][k], patches[-1][k]
        pieces[0] = jnp.where((lane < near) & has_left, left, pieces[0])
        pieces[-1] = jnp.where((lane >= LANES - near) & has_right, right, pieces[-1])
        beside = jnp.where((lane < reach) & has_right, right, jnp.where((lane >= LANES - reach) & has_left, left, 0.0))
        return jnp.concatenate(pieces + [beside], axis=1)

    for j in range(KEEP):
        code = jnp.concatenate([zr_ref[Z_CODE + 8 * j : Z_CODE + 8 * j + 8, :], corners.cell(j, 1)], axis=1)
        s = choose([v_s], code)[0]
        s_ref[at8(AHEAD + j), :] = s
        if j < 2:
            temp = jnp.concatenate([zr_ref[Z_TEMP + 8 * j : Z_TEMP + 8 * j + 8, :], corners.cell(j, 0)], axis=1)
            q0_ref[at8(AHEAD + j), :] = s * temp
            al_ref[at8(AHEAD + j), :] = lookup(t_al, code)
            at = Z_HEAT + 8 * j
            q1_ref[at8(AHEAD + 1 + j), :] = mend(zr_ref[at : at + 8, :], j, KEEP, HALO)
    for r in (AHEAD - 1, AHEAD):
        di_ref[at8(r), :], q1_ref[at8(r), :] = first_sweep(s_ref, q0_ref, r, power_row(pw_ref, n_p, r), h)
    r = AHEAD + 1
    di_ref[at8(r), :] = 1.0 / (h + row8(s_ref, r) * conduct_sum(s_ref, r))
    for r in range(AHEAD - 2, AHEAD + 2):
        t2 = second_sweep(s_ref, q1_ref, di_ref, r, power_row(pw_ref, n_p, r))
        t_keep[at8(r), :] = t2
        ea_ref[at8(r), :] = row8(al_ref, r) * t2
    ea_ref[at8(AHEAD + 2), :] = mend(zr_ref[Z_STRAIN : Z_STRAIN + 8, :], 2, KEEP, HALO)

    core = lax.axis_index(CORE)

    def other_half(x):
        return jnp.where(core == 0, x[:, half:wide], x[:, 0:half])

    def own_half(x):
        return jnp.where(core == 0, x[:, 0:half], x[:, half:wide])

    for g in range(2):
        t2 = row8(t_keep, AHEAD - 1 - g)
        keep_ref[8 * g : 8 * g + 8, :] = own_half(t2)
        x_ref[8 * g : 8 * g + 8, :] = other_half(t2)
    x_ref[16:24, :] = other_half(row8(t_in, FRONT + 2))

    count = mod_in.shape[0] // 8
    mrows = count - MHALO
    mwidth = mod_in.shape[1]
    n_m = count + MHALO
    for m in range(MHALO + 1 - FAR):
        i = AHEAD - 3 + 3 * m
        x = row8(ea_ref, i) + row8(ea_ref, i + 1) + row8(ea_ref, i + 2)
        st_ref[at8(MHALO - m), :] = restrict_columns(x)
    for f in range(FAR):
        at = Z_SUM + 8 * f
        st_ref[at8(FAR - 1 - f), :] = restrict_columns(mend(zr_ref[at : at + 8, :], 3 + f, KEEP, HALO))
    for m in range(1, count):
        st_ref[at8(MHALO + m), :] = row8(strain_in, m)
    values = splats(tab, 1)
    for i in range(MHALO):
        j = MHALO - 1 - i
        fields = []
        for f in range(4):
            body = zr_ref[Z_SOLID + ML * f : Z_SOLID + ML * f + 8, mcols * j : mcols * (j + 1)]
            body = jnp.where(sub_iota(mcols) < ML, body, 0.0)
            side = corners.field(j, f)
            fields.append(jnp.concatenate([body, side], axis=1))
        mod_ref[at8(i), :], root, mi_ref[at8(i), :] = moduli(values, fields[3])
        for f in range(3):
            uu_refs[f][at8(i), :] = root * fields[f]
    for ref, src in zip((mi_ref, mod_ref, *uu_refs), (mi_in, mod_in, *uu_in)):
        ref[8 * MHALO : 8 * n_m, :] = src[...]
    for i in range(n_m):
        sf_ref[at8(i), :] = row8(mod_ref, i) * row8(st_ref, i)
    sign = jnp.where(core == 0, 0.5, -0.5).astype(jnp.float32)
    for i in range(1, n_m - 1):
        load = row8(sf_ref, i)
        force = [
            0.5 * (next_sub(load) - prev_sub(load)),
            sign * (row8(sf_ref, i + 1) - row8(sf_ref, i - 1)),
            0.5 * (next_lane(load) - prev_lane(load)),
        ]
        inv = row8(mi_ref, i)
        inside = inv > 0.0
        if i <= MHALO:
            near = couple_sum([[row8(r, i - 1), row8(r, i), row8(r, i + 1)] for r in uu_refs])
            pre = [near[d] * (1.0 / STIFF_DIAG) - row8(uu_refs[d], i) for d in range(3)]
        else:
            pre = [row8(r, i - MHALO) for r in pre_in]
        inv = inv * (1.0 / STIFF_DIAG)
        for d in range(3):
            p_refs[d][at8(i), :] = jnp.where(inside, force[d] * inv + pre[d], 0.0)
    c_near = 2.0 * RHO1 / DELTA / STIFF_DIAG
    c_self = 1.0 + RHO1 * RHO0
    for i in range(2, n_m - 2):
        near = couple_sum([[row8(r, i - 1), row8(r, i), row8(r, i + 1)] for r in p_refs])
        inv = row8(mi_ref, i)
        for d in range(3):
            moved = row8(uu_refs[d], i) + c_self * row8(p_refs[d], i) + c_near * near[d]
            d_refs[d][at8(i), :] = moved * inv
    sub = sub_iota(mwidth)
    weight = jnp.where(sub < ML, (ML - sub).astype(jnp.float32) * (1.0 / (ML * (ML + 1) / 2.0)), 0.0)
    x_ref[24:32, :] = jnp.zeros((8, x_ref.shape[1]), jnp.float32)
    for g in range(mrows):
        i = MHALO + g
        u0, u2 = row8(d_refs[0], i), row8(d_refs[2], i)
        div = 0.5 * (next_sub(u0) - prev_sub(u0)) + 0.5 * (next_lane(u2) - prev_lane(u2))
        div = div + sign * (row8(d_refs[1], i + 1) - row8(d_refs[1], i - 1))
        stress = row8(mod_ref, i) * (div - 3.0 * row8(st_ref, i))
        die = jnp.sum(weight * stress, axis=0, keepdims=True)
        first, second = die[:, 0:LANES], die[:, LANES : 2 * LANES]
        keep_ref[16 + g : 17 + g, 0:LANES] = jnp.where(core == 0, first, second)
        x_ref[24 + g : 25 + g, 0:LANES] = jnp.where(core == 0, second, first)
        for d in range(3):
            u_ref[8 * (mrows * d + g) : 8 * (mrows * d + g) + 8, :] = row8(d_refs[d], i)[:, 0:mcols]


def k_out(rows, mrows, t_in, keep_ref, xr_ref, u_in, t_out, u_out, slow_ref, buf, die, wide_die, ubuf):
    half = slow_ref.shape[1]
    mcols = u_in.shape[1]
    core = lax.axis_index(CORE)

    def put(ref, at, x):
        count = ref.shape[0] * LANES // x.shape[1]
        for t, piece in enumerate(tiles(x)):
            ref[count * t + at : count * t + at + piece.shape[0], :] = piece

    def build(rev):
        lo = half if rev else 0
        for g in range(rows):
            i = rows - 1 - g if rev else g
            if g < 2:
                x = keep_ref[8 * g : 8 * g + 8, :]
            elif g < rows - 3:
                x = t_in[8 * (FRONT + g) : 8 * (FRONT + g) + 8, lo : lo + half]
            else:
                k = rows - 1 - g
                x = xr_ref[8 * k : 8 * k + 8, :]
            put(buf, 8 * i, x)
        for g in range(mrows):
            mine = 2 * mrows - 1 - g if rev else g
            theirs = g if rev else 2 * mrows - 1 - g
            die[mine : mine + 1, :] = keep_ref[16 + g : 17 + g, 0:LANES]
            die[theirs : theirs + 1, :] = xr_ref[24 + g : 25 + g, 0:LANES]
            for d in range(3):
                i = mrows - 1 - g if rev else g
                put(ubuf, 8 * (mrows * d + i), row8(u_in, mrows * d + g))

    @pl.when(core == 0)
    def _():
        build(False)

    @pl.when(core != 0)
    def _():
        build(True)

    for t in range(half // LANES):
        at = 8 * rows * t
        for l in range(DEPTH):
            t_out[l, :, tile_lanes(t)] = buf[pl.ds(at + l, rows, stride=8), :]
    for t in range(mcols // LANES):
        for d in range(3):
            for l in range(ML):
                u_out[d, l, :, tile_lanes(t)] = ubuf[pl.ds(8 * mrows * (3 * t + d) + l, mrows, stride=8), :]
    lane = lane_iota(2 * mrows)
    for t in range(half // LANES):
        x = gather_lanes(die[...], (lane + LANES * t) // 3)
        for b in range(3):
            wide_die[pl.ds(b, 2 * mrows, stride=3), :] = x
        slow = 1.0 + 0.2 * buf[pl.ds(8 * rows * t, rows, stride=8), :] + 0.5 * wide_die[...]
        slow_ref[:, tile_lanes(t)] = slow


def pairs(dims, sends):
    index = {}
    for r in range(dims[0]):
        for c in range(dims[1]):
            for a in range(dims[2]):
                index[(r, c, a)] = (r * dims[1] + c) * dims[2] + a
    out = []
    for source in index:
        target = sends(*source)
        if target in index:
            out.append((index[source], index[target]))
    return out


def per_device(temp, ids, power, mat, offset, heat_table, growth_table, modulus_table):
    axes = ("row", "col", "lay")
    dims = tuple(lax.axis_size(x) for x in axes)
    n_col = dims[1]
    _, rows, half = temp.shape
    _, _, mrows, mcols = offset.shape
    n_edges = 1 if n_col == 2 else 2
    n_t = half // LANES
    m_t = mcols // LANES

    def send(x, sends):
        return lax.ppermute(x, axes, pairs(dims, sends))

    def swap(r, c, a):
        return (r, c, 1 - a)

    def along(r, c, a):
        return (r + 1, c, 0) if a == 1 else (r - 1, c, 1)

    wide = 2 * half
    own = rows - 1
    kind = lax.broadcasted_iota(jnp.int32, (2, *temp.shape), 0)
    both = jnp.where(kind == 0, temp[None], power[None, None])
    tab = jnp.stack([heat_table, growth_table, modulus_table])
    tab = jnp.pad(tab, ((0, 0), (1, LANES - 1 - tab.shape[1])))
    (tab,) = call(k_tables, [(16 * (NMAT + 1) + 8, LANES)], [tab])
    n = 16 * HALO
    n_far = 8 * far_rows(rows)
    cells, one = call(k_rows, [(16 * rows * n_t, LANES), ((n + 16) * n_t, LANES)], [both, ids])
    got1 = send(one, swap)
    two, mg = call(
        functools.partial(k_rest, n_edges),
        [
            ((16 * (rows - 1 - HALO) + rows - 16) * n_t + 32 * MHALO * m_t + n_far + 8 * n_edges, LANES),
            (32 * mrows, mcols),
        ],
        [both, cells, offset, mat],
        scratch=[(32 * mrows * m_t, LANES)],
    )
    got2 = send(two, swap)
    *own_part, far = call(
        functools.partial(k_half, n_edges),
        [(8 * HALO, half)] * 3 + [(n_far * n_edges, LANES)],
        [tab, both, cells],
    )
    n_c = 32 + n_far - 8 * (-4 * (mrows - MHALO) * MSPAN // LANES) + 8
    z, first_rows, *edges = call(
        functools.partial(k_edge, n_edges),
        [(far_place(n_edges, -1, wide)[0].stop, wide), (n + 16, wide)] + [(32, LANES)] * n_edges,
        [tab, both, cells, got1, mg, *own_part],
        cost=EDGE_COST,
        scratch=[(8 * HALO, wide)] * 5,
    )
    leaving = [z, *edges]
    leaving = call(
        functools.partial(k_beside, n_edges, rows),
        [(n_c, LANES)] * n_edges + [x.shape for x in leaving],
        [far, got2, mg] + leaving,
        aliases={3 + k: n_edges + k for k in range(len(leaving))},
    )
    beside, z, near = leaving[:n_edges], leaving[n_edges], leaving[n_edges + 1 :]
    zr = send(z, along)
    if n_edges == 1:
        sides = [send(beside[0], lambda r, c, a: (r, 1 - c, a))]
        corners = [send(near[0], lambda r, c, a: along(r, 1 - c, a))]
    else:
        sides = [send(beside[0], lambda r, c, a: (r, c + 1, a)), send(beside[1], lambda r, c, a: (r, c - 1, a))]
        corners = [
            send(near[0], lambda r, c, a: along(r, c + 1, a)),
            send(near[1], lambda r, c, a: along(r, c - 1, a)),
        ]
    w, src, mw = call(
        functools.partial(k_chip, rows),
        [(16 * own, wide), (rows, wide), (32 * (mrows + MHALO), mcols)],
        [both, cells, got2, mg, first_rows],
    )
    width = wide + LANES
    mwidth = mcols + LANES
    n_w = 8 * (rows + FRONT + 4)
    inner = call(
        functools.partial(k_inner, n_edges, n_col, rows),
        [(n_w, width)] * 7 + [(8 * (mrows + MHALO), mwidth)],
        [tab, w, src] + sides,
        scratch=[(n_w * (width // LANES), LANES)],
    )
    t2 = inner[5]
    solid = call(
        functools.partial(k_mech, n_edges, n_col, rows), [(8 * (mrows + MHALO), mwidth)] * 8, [tab, mw] + sides
    )
    n_h = 8 * (AHEAD + HALO + 5)
    n_m = 8 * (mrows + 2 * MHALO)
    x, keep, u = call(
        functools.partial(k_outer, n_edges, n_col, rows),
        [(32, half), (24, half), (24 * mrows, mcols)],
        [tab, zr] + sides + corners + list(inner) + [src] + list(solid),
        scratch=[(n_h, width)] * 7
        + [(n_h * (width // LANES), LANES)]
        + [(n_m, mwidth)] * 13
        + [(8 * HALO, LANES)] * 4,
    )
    xr = send(x, swap)
    t_out, u_out, slow = call(
        functools.partial(k_out, rows, mrows),
        [temp.shape, offset.shape, power.shape],
        [t2, keep, xr, u],
        scratch=[
            (8 * rows * n_t, LANES),
            (2 * mrows, LANES),
            (rows, LANES),
            (24 * mrows * m_t, LANES),
        ],
    )
    return t_out, u_out, slow


def solution(mesh):
    placed = (
        P("grp", "row", ("col", "lay")),
        P("grp", "row", ("col", "lay")),
        P(("grp", "row"), ("col", "lay")),
        P("grp", ("row", "lay"), "col"),
        P(None, "grp", ("row", "lay"), "col"),
        P(),
        P(),
        P(),
    )
    return jax.shard_map(
        per_device,
        mesh=mesh,
        in_specs=placed,
        out_specs=(
            P("grp", "row", ("col", "lay")),
            P(None, "grp", ("row", "lay"), "col"),
            P(("grp", "row"), ("col", "lay")),
        ),
        check_vma=False,
    )
```

```python
import functools

import jax
import jax.numpy as jnp
from jax import lax
from jax.experimental import pallas as pl
from jax.experimental.pallas import tpu as pltpu
from jax.sharding import PartitionSpec as P

DEPTH = 8
ML = 6
LANES = 128
HALO = 11
MHALO = 3

STIFF_DIAG = 12.0
THETA = 1.0
DELTA = 0.75
SIGMA = THETA / DELTA
RHO0 = 1.0 / SIGMA
RHO1 = 1.0 / (2.0 * SIGMA - RHO0)

VMEM = pl.BlockSpec(memory_space=pltpu.VMEM)
FRONT = 9
AHEAD = 5
STEP = 3
HBM = pl.BlockSpec(memory_space=pltpu.HBM)
SPAN = 11
MSPAN = 8
NMAT = 16
FAR = 2
EDGE_COST = 10**10
FAR_ROW = 9 - 3 * FAR
KEEP = 3
Z_TEMP, Z_CODE, Z_HEAT, Z_STRAIN, Z_SUM, Z_SOLID, Z_POWER, Z_FAR = 0, 16, 40, 56, 64, 80, 104, 112
CORE = "lay"
UNROLL_STRAIN = 3


def call(kernel, outs, args, scratch=(), specs=None, out_specs=None, aliases=None, cost=0):
    return pl.pallas_call(
        kernel,
        out_shape=[jax.ShapeDtypeStruct(s, jnp.float32) for s in outs],
        in_specs=specs or [VMEM] * len(args),
        out_specs=out_specs or [VMEM] * len(outs),
        input_output_aliases=aliases or {},
        cost_estimate=pl.CostEstimate(flops=cost, bytes_accessed=0, transcendentals=0) if cost else None,
        scratch_shapes=[pltpu.VMEM(s, jnp.float32) if isinstance(s, tuple) else s for s in scratch],
        compiler_params=pltpu.CompilerParams(vmem_limit_bytes=16 * 1024 * 1024),
    )(*args)


def lane_iota(rows=8):
    return lax.broadcasted_iota(jnp.int32, (rows, LANES), 1)


def sub_iota(width):
    return lax.broadcasted_iota(jnp.int32, (8, width), 0)


def tile_lanes(t):
    return slice(LANES * t, LANES * (t + 1))


def tiles(x):
    return [x[:, tile_lanes(t)] for t in range(x.shape[1] // LANES)]


def table_of(ref, k):
    return jnp.broadcast_to(ref[k : k + 1, :], (8, LANES))


def gather_lanes(table, index):
    return jnp.take_along_axis(table, index, axis=1, mode="promise_in_bounds")


def lookup(table, code):
    return jnp.concatenate([gather_lanes(table, c.astype(jnp.int32)) for c in tiles(code)], axis=1)


def k_tables(tab, out_ref):
    for k, table in enumerate((jnp.sqrt(table_of(tab, 0)), table_of(tab, 2))):
        for m in range(NMAT + 1):
            at = 8 * ((NMAT + 1) * k + m)
            out_ref[at : at + 8, :] = jnp.broadcast_to(table[:, m : m + 1], (8, LANES))
    out_ref[16 * (NMAT + 1) : 16 * (NMAT + 1) + 8, :] = table_of(tab, 1)


def splats(tab, k):
    return [row8(tab, (NMAT + 1) * k + m) for m in range(NMAT + 1)]


def expansion_table(tab):
    return row8(tab, 2 * (NMAT + 1))


def choose(lists, code):
    out = [[] for _ in lists]
    for c in tiles(code):
        c = c.astype(jnp.int32)
        bits = [(c & (1 << k)) != 0 for k in range(5)]
        for n, values in enumerate(lists):
            level = values[:16]
            for k in range(4):
                level = [jnp.where(bits[k], b, a) for a, b in zip(level[::2], level[1::2])]
            out[n].append(jnp.where(bits[4], values[16], level[0]))
    return [jnp.concatenate(x, axis=1) for x in out]


def prev_lane(x):
    return pltpu.roll(x, 1, 1)


def next_lane(x):
    return pltpu.roll(x, x.shape[1] - 1, 1)


def prev_sub(x):
    return pltpu.roll(x, 1, 0)


def next_sub(x):
    return pltpu.roll(x, 7, 0)


def at8(i):
    return pl.ds(8 * i, 8) if isinstance(i, int) else pl.ds(pl.multiple_of(8 * i, 8), 8)


def row8(ref, i):
    return ref[at8(i), :]


def turned(core, last, g):
    return core * last + (1 - 2 * core) * g


def k_rows(in_ref, id_ref, a_ref, one_ref):
    other = 1 - lax.axis_index(CORE)
    rows = in_ref.shape[2]
    n_t = in_ref.shape[3] // LANES
    n = 16 * HALO
    for t in range(n_t):
        at = 16 * rows * t
        for l in range(DEPTH):
            a_ref[pl.ds(at + l, rows, stride=16), :] = in_ref[0, l, :, tile_lanes(t)]
            a_ref[pl.ds(at + DEPTH + l, rows, stride=16), :] = (id_ref[l, :, tile_lanes(t)] + 1).astype(jnp.float32)
    for t in range(n_t):
        to = (n + 16) * t
        for g in range(HALO):
            i = 16 * (rows * t + turned(other, rows - 1, g))
            one_ref[to + 16 * g : to + 16 * g + 16, :] = a_ref[pl.ds(pl.multiple_of(i, 16), 16), :]
        for b in range(2):
            one_ref[to + n + 8 * b : to + n + 8 * b + 8, :] = power_rows(in_ref, other, b, t)


def k_rest(n_edges, in_ref, a_ref, u_ref, mat_ref, two_ref, mg_ref, m_ref):
    core = lax.axis_index(CORE)
    other = 1 - core
    rows = in_ref.shape[2]
    n_t = in_ref.shape[3] // LANES
    mrows = mat_ref.shape[1]
    mcols = mat_ref.shape[2]
    m_t = mcols // LANES
    m_ref[...] = jnp.zeros(m_ref.shape, jnp.float32)
    for t in range(m_t):
        at = 32 * mrows * t
        for l in range(ML):
            for f in range(3):
                m_ref[pl.ds(at + 8 * f + l, mrows, stride=32), :] = u_ref[f, l, :, tile_lanes(t)]
            m_ref[pl.ds(at + 24 + l, mrows, stride=32), :] = (mat_ref[l, :, tile_lanes(t)] + 1).astype(jnp.float32)
        for g in range(mrows):
            i = 32 * (mrows * t + turned(core, mrows - 1, g))
            mg_ref[32 * g : 32 * g + 32, tile_lanes(t)] = m_ref[pl.ds(pl.multiple_of(i, 32), 32), :]
    for e in range(n_edges):
        side = edge_side(n_edges, e)
        fields = []
        for g in range(MHALO):
            i = 32 * (mrows * side * (m_t - 1) + turned(core, mrows - 1, mrows - 1 - g))
            fields += [m_ref[pl.ds(pl.multiple_of(i + 8 * f, 8), 8), :] for f in range(4)]
        at = two_ref.shape[0] - 8 * (n_edges - e)
        (two_ref[at : at + 8, :],) = packed(side, fields, MSPAN, MHALO)
    for k, x in enumerate(far_strip(in_ref, a_ref, other, core * (n_t - 1), core)):
        at = two_ref.shape[0] - 8 * (n_edges + far_rows(rows) - k)
        two_ref[at : at + 8, :] = x
    rest = 16 * (rows - 1 - HALO)
    for t in range(n_t):
        to = (rest + rows - 16) * t
        for g in range(HALO, rows - 1):
            i = 16 * (rows * t + turned(other, rows - 1, g))
            k = to + 16 * (g - HALO)
            two_ref[k : k + 16, :] = a_ref[pl.ds(pl.multiple_of(i, 16), 16), :]
        for b in range(2, rows // 8):
            two_ref[to + rest + 8 * (b - 2) : to + rest + 8 * (b - 1), :] = power_rows(in_ref, other, b, t)
    for t in range(m_t):
        for g in range(MHALO):
            i = 32 * (mrows * t + turned(core, mrows - 1, mrows - 1 - g))
            k = (rest + rows - 16) * n_t + 4 * ML * (MHALO * t + g)
            x = m_ref[pl.ds(pl.multiple_of(i, 32), 32), :]
            for f in range(4):
                two_ref[k + ML * f : k + ML * (f + 1), :] = x[8 * f : 8 * f + ML, :]


def power_rows(in_ref, turn, b, t):
    rows = in_ref.shape[2]
    lanes = tile_lanes(t) if isinstance(t, int) else pl.ds(pl.multiple_of(LANES * t, LANES), LANES)
    x = in_ref[1, 0, at8(turned(turn, rows // 8 - 1, b)), lanes]
    return jnp.take_along_axis(x, turned(turn, 7, sub_iota(LANES)), axis=0, mode="promise_in_bounds")


def far_strip(in_ref, a_ref, turn, t, side):
    rows = in_ref.shape[2]
    blocks = []
    for g in range(HALO, rows - 1):
        i = 16 * (rows * t + turned(turn, rows - 1, g))
        blocks += [a_ref[pl.ds(pl.multiple_of(i + k, 8), 8), :] for k in (0, 8)]
    blocks += [power_rows(in_ref, turn, b, t) for b in range(2, rows // 8)]
    return packed(side, blocks, SPAN, HALO)


def edge_side(n_edges, e):
    return 1 - lax.axis_index("col") if n_edges == 1 else 1 - e


def edge_tile(side, width):
    if isinstance(side, int):
        return tile_lanes(side * (width // LANES - 1))
    return pl.ds(pl.multiple_of(side * (width - LANES), LANES), LANES)


def packed(side, blocks, span, keep):
    lane = lane_iota()
    per = LANES // span
    out = []
    for i in range(0, len(blocks), per):
        acc = jnp.zeros((8, LANES), jnp.float32)
        for k, x in enumerate(blocks[i : i + per]):
            acc = jnp.where(lane // span == k, pltpu.roll(x, span * k + side * keep, 1), acc)
        out.append(acc)
    return out


def far_rows(rows):
    return -(-(2 * (rows - 1 - HALO) + rows // 8 - 2) // (LANES // SPAN))


def k_half(n_edges, tab, in_ref, a_ref, s_ref, q0_ref, al_ref, far_ref):
    core = lax.axis_index(CORE)
    rows = in_ref.shape[2]
    n_t = in_ref.shape[3] // LANES
    v_s = splats(tab, 0)
    t_al = expansion_table(tab)
    for t in range(n_t):
        for g in range(HALO):
            i = 16 * (rows * t + turned(core, rows - 1, g))
            code = a_ref[pl.ds(pl.multiple_of(i + 8, 8), 8), :]
            (x,) = choose([v_s], code)
            s_ref[at8(g), tile_lanes(t)] = x
            q0_ref[at8(g), tile_lanes(t)] = x * a_ref[pl.ds(pl.multiple_of(i, 16), 8), :]
            if 2 <= g < 9:
                al_ref[at8(g), tile_lanes(t)] = lookup(t_al, code)
    for e in range(n_edges):
        side = edge_side(n_edges, e)
        for k, x in enumerate(far_strip(in_ref, a_ref, core, side * (n_t - 1), side)):
            at = 8 * (far_rows(rows) * e + k)
            far_ref[at : at + 8, :] = x


def k_edge(n_edges, tab, in_ref, a_ref, got_ref, mg_ref, s_own, q0_own, al_own, z_ref, w_ref, *refs):
    core = lax.axis_index(CORE)
    wide = z_ref.shape[1]
    half = wide // 2
    n_t = half // LANES
    rows = in_ref.shape[2]
    mcols = mg_ref.shape[1]
    n = 16 * HALO
    edge_refs, (s_ref, q0_ref, al_ref, q1_ref, di_ref) = refs[:n_edges], refs[n_edges:]
    v_s = splats(tab, 0)
    t_al = expansion_table(tab)

    def build(first):
        for t in range(n_t):
            lanes = tile_lanes(t if first else n_t + t)
            for g in range(HALO):
                i = 16 * (rows * t + (g if first else rows - 1 - g))
                w_ref[16 * g : 16 * g + 16, lanes] = a_ref[i : i + 16, :]
            for b in range(2):
                w_ref[n + 8 * b : n + 8 * b + 8, lanes] = power_rows(in_ref, 0 if first else 1, b, t)
            lanes = tile_lanes(n_t + t if first else t)
            at = (n + 16) * t
            w_ref[0 : n + 16, lanes] = got_ref[at : at + n + 16, :]
            for g in range(HALO):
                code = got_ref[at + 16 * g + 8 : at + 16 * g + 16, :]
                (x,) = choose([v_s], code)
                s_ref[at8(g), lanes] = x
                q0_ref[at8(g), lanes] = x * got_ref[at + 16 * g : at + 16 * g + 8, :]
                if 2 <= g < 9:
                    al_ref[at8(g), lanes] = lookup(t_al, code)
        lanes = slice(0, half) if first else slice(half, wide)
        for dst, src in ((s_ref, s_own), (q0_ref, q0_own), (al_ref, al_own)):
            dst[:, lanes] = src[...]

    @pl.when(core == 0)
    def _():
        build(True)

    @pl.when(core != 0)
    def _():
        build(False)

    for g in range(2):
        z_ref[Z_TEMP + 8 * g : Z_TEMP + 8 * g + 8, :] = w_ref[16 * g : 16 * g + 8, :]
    for g in range(3):
        z_ref[Z_CODE + 8 * g : Z_CODE + 8 * g + 8, :] = w_ref[16 * g + 8 : 16 * g + 16, :]
    z_ref[Z_POWER : Z_POWER + 8, :] = w_ref[n : n + 8, :]
    z_ref[Z_FAR:, :] = jnp.zeros((z_ref.shape[0] - Z_FAR, wide), jnp.float32)
    for g in range(MHALO):
        for f in range(4):
            at = Z_SOLID + ML * f
            z_ref[at : at + ML, mcols * g : mcols * (g + 1)] = mg_ref[32 * g + 8 * f : 32 * g + 8 * f + ML, :]
    for e in range(n_edges):
        side = edge_side(n_edges, e)
        lanes, mlanes = edge_tile(side, wide), edge_tile(side, mcols)
        blocks = [w_ref[8 * i : 8 * i + 8, lanes] for i in range(2 * HALO)]
        blocks += [w_ref[n + 8 * b : n + 8 * b + 8, lanes] for b in range(2)]
        fields = [mg_ref[8 * i : 8 * i + 8, mlanes] for i in range(4 * MHALO)]
        near = packed(side, blocks, SPAN, HALO) + packed(side, fields, MSPAN, MHALO)
        strip = blocks[4 : 2 * HALO : 2] + blocks[7 : 2 * HALO : 2] + blocks[2 * HALO + 1 :]
        for k, x in enumerate(packed(side, strip, SPAN, HALO)):
            z_ref[far_place(e, k, wide)] = x
        for k, x in enumerate(near):
            edge_refs[e][8 * k : 8 * k + 8, :] = x
    h = sink(wide)
    top = sub_iota(wide) == 0
    powers = {
        g: jnp.where(top, jnp.broadcast_to(w_ref[n + g : n + g + 1, :], (8, wide)), 0.0) for g in range(1, HALO - 1)
    }
    for g in range(1, HALO - 1):
        di_ref[at8(g), :], q1_ref[at8(g), :] = first_sweep(s_ref, q0_ref, g, powers[g], h, True)
    z_ref[Z_HEAT : Z_HEAT + 16, :] = q1_ref[8:24, :]

    def expansion(g):
        return row8(al_ref, g) * second_sweep(s_ref, q1_ref, di_ref, g, powers[g], True)

    z_ref[Z_STRAIN : Z_STRAIN + 8, :] = expansion(2)
    for f in range(FAR):
        g = FAR_ROW + 3 * f
        x = expansion(g) + expansion(g + 1) + expansion(g + 2)
        z_ref[Z_SUM + 8 * f : Z_SUM + 8 * f + 8, :] = x


def far_tiles():
    return -(-(2 * HALO - 4) // (LANES // SPAN))


def far_place(e, k, wide):
    q = far_tiles() * e + k
    at = Z_FAR + 8 * (q // (wide // LANES))
    return slice(at, at + 8), tile_lanes(q % (wide // LANES))


def k_beside(n_edges, rows, far_ref, got_ref, mg_ref, z_ref, *refs):
    near_refs, c_refs = refs[:n_edges], refs[n_edges : 2 * n_edges]
    core = lax.axis_index(CORE)
    mrows = mg_ref.shape[0] // 32
    for e in range(n_edges):
        side = edge_side(n_edges, e)
        mlanes = edge_tile(side, mg_ref.shape[1])
        fields = [mg_ref[8 * i : 8 * i + 8, mlanes] for i in range(4 * MHALO, 4 * mrows)]
        far = [near_refs[e][8 * k : 8 * k + 8, :] for k in range(4)]
        for k in range(far_rows(rows)):
            at = got_ref.shape[0] - 8 * (n_edges + far_rows(rows) - k)
            x = row8(far_ref, far_rows(rows) * e + k)
            far.append(jnp.where(core == side, x, got_ref[at : at + 8, :]))
        far += packed(side, fields, MSPAN, MHALO)
        at = got_ref.shape[0] - 8 * (n_edges - e)
        far.append(got_ref[at : at + 8, :])
        for k, x in enumerate(far):
            c_refs[e][8 * k : 8 * k + 8, :] = x


def k_chip(rows, in_ref, a_ref, got_ref, mg_ref, first_ref, w_ref, src_ref, mw_ref):
    core = lax.axis_index(CORE)
    n_t = w_ref.shape[1] // LANES // 2
    mrows = mg_ref.shape[0] // 32
    n = 16 * HALO
    rest = 16 * (rows - 1 - HALO)
    w_ref[0:n, :] = first_ref[0:n, :]
    src_ref[0:16, :] = first_ref[n : n + 16, :]

    def build(first):
        for t in range(n_t):
            lanes = tile_lanes(t if first else n_t + t)
            for g in range(HALO, rows - 1):
                i = 16 * (rows * t + (g if first else rows - 1 - g))
                w_ref[16 * g : 16 * g + 16, lanes] = a_ref[i : i + 16, :]
            for b in range(2, rows // 8):
                src_ref[8 * b : 8 * b + 8, lanes] = power_rows(in_ref, 0 if first else 1, b, t)
            lanes = tile_lanes(n_t + t if first else t)
            at = (rest + rows - 16) * t
            w_ref[n : n + rest, lanes] = got_ref[at : at + rest, :]
            src_ref[16:rows, lanes] = got_ref[at + rest : at + rest + rows - 16, :]

    @pl.when(core == 0)
    def _():
        build(True)

    @pl.when(core != 0)
    def _():
        build(False)

    mw_ref[0 : 32 * mrows, :] = mg_ref[...]
    for t in range(mw_ref.shape[1] // LANES):
        for k in range(4 * MHALO):
            at = (rest + rows - 16) * n_t + ML * (4 * MHALO * t + k)
            to = 32 * mrows + 8 * k
            x = jnp.where(sub_iota(LANES) < ML, got_ref[at : at + 8, :], 0.0)
            mw_ref[to : to + 8, tile_lanes(t)] = x


class Sides:
    def __init__(self, n_col, rows, mrows, from_left, from_right):
        self.left = from_left
        self.right = from_right
        self.rows = rows
        self.mrows = mrows
        lane = lane_iota()
        col = lax.axis_index("col")
        self.masks = {
            w: ((lane < w) & (col < n_col - 1), (lane >= LANES - w) & (col > 0)) for w in (HALO, MHALO)
        }
        self.only = self.left is self.right
        self.side = col

    def take(self, v, k, span, width):
        right_mask, left_mask = self.masks[width]
        x = row8(self.right, v)
        if self.only:
            x = pltpu.roll(x, LANES - span * k - self.side * width, 1)
            return jnp.where(right_mask | left_mask, x, 0.0)
        r = pltpu.roll(x, (LANES - span * k) % LANES, 1)
        l = pltpu.roll(row8(self.left, v), LANES - span * k - width, 1)
        return jnp.where(right_mask, r, jnp.where(left_mask, l, 0.0))

    def block(self, first, i, span, width):
        per = LANES // span
        return self.take(first + i // per, i % per, span, width)

    def cell(self, g, kind):
        if g < HALO:
            return self.block(0, 2 * g + kind, SPAN, HALO)
        return self.block(4, 2 * (g - HALO) + kind, SPAN, HALO)

    def power(self, b):
        if b < 2:
            return self.block(0, 2 * HALO + b, SPAN, HALO)
        return self.block(4, 2 * (self.rows - 1 - HALO) + b - 2, SPAN, HALO)

    def field(self, m, f):
        if m < MHALO:
            return self.block(3, 4 * m + f, MSPAN, MHALO)
        first = 4 + far_rows(self.rows)
        if m < self.mrows:
            return self.block(first, 4 * (m - MHALO) + f, MSPAN, MHALO)
        first += -(-4 * (self.mrows - MHALO) * MSPAN // LANES)
        return self.block(first, 4 * (m - self.mrows) + f, MSPAN, MHALO)


def spread_power(ref, n, blocks):
    ref[...] = jnp.zeros(ref.shape, jnp.float32)
    count = ref.shape[0] // (n * 8)
    for first, x in blocks:
        for t, piece in enumerate(tiles(x)):
            ref[pl.ds(8 * (n * t + first), piece.shape[0], stride=8), :] = piece
    return count


def power_row(ref, n, i):
    count = ref.shape[0] // (n * 8)
    return jnp.concatenate([row8(ref, n * t + i) for t in range(count)], axis=1)


def conduct_sum(ref, i, closed=False):
    x = row8(ref, i)
    sub = sub_iota(x.shape[1])
    before, after = prev_lane(x), next_lane(x)
    if closed:
        lane = lax.broadcasted_iota(jnp.int32, x.shape, 1)
        before = jnp.where(lane > 0, before, 0.0)
        after = jnp.where(lane < x.shape[1] - 1, after, 0.0)
    total = row8(ref, i - 1) + row8(ref, i + 1) + before + after
    total = total + jnp.where(sub < DEPTH - 1, next_sub(x), 0.0)
    return total + jnp.where(sub > 0, prev_sub(x), 0.0)


def sink(width):
    return jnp.where(sub_iota(width) == DEPTH - 1, 2.0, 0.2).astype(jnp.float32)


def to_solid_layers(y):
    return jnp.where(sub_iota(y.shape[1]) < 3, y, next_sub(y)) * (1.0 / 9.0)


def gather_main(pieces):
    lane = 3 * lane_iota()
    out = []
    for j in range(len(pieces) // 3):
        total = None
        for k in range(3):
            got = None
            for t in range(3):
                g = gather_lanes(pieces[3 * j + t], (lane + k) & (LANES - 1))
                got = g if got is None else jnp.where(lane + k >= LANES * t, g, got)
            total = got if total is None else total + got
        out.append(total)
    return out


def gather_sides(piece):
    lane = lane_iota()
    first = LANES - MHALO
    inside = (lane < MHALO) | (lane >= first)
    index = jnp.where(lane < MHALO, 3 * lane, jnp.where(lane >= first, LANES - 9 + 3 * (lane - first), 0))
    total = gather_lanes(piece, index) + gather_lanes(piece, index + 1) + gather_lanes(piece, index + 2)
    return jnp.where(inside, total, 0.0)


def restrict_columns(x):
    pieces = tiles(x)
    return to_solid_layers(jnp.concatenate(gather_main(pieces[:-1]) + [gather_sides(pieces[-1])], axis=1))


def first_sweep(s_ref, q0_ref, i, power, h, closed=False):
    s = row8(s_ref, i)
    inv = 1.0 / (h + s * conduct_sum(s_ref, i, closed))
    return inv, s * ((power + s * conduct_sum(q0_ref, i, closed)) * inv)


def second_sweep(s_ref, q1_ref, di_ref, i, power, closed=False):
    return (power + row8(s_ref, i) * conduct_sum(q1_ref, i, closed)) * row8(di_ref, i)


def k_inner(n_edges, n_col, rows, tab, w_ref, src_ref, *refs):
    sides = Sides(n_col, rows, rows // 6, refs[0], refs[n_edges - 1])
    s_ref, al_ref, q0_ref, q1_ref, di_ref, t_ref, ea_ref, strain_ref, pw_ref = refs[n_edges:]
    own = rows - 1
    width = src_ref.shape[1] + LANES
    t_al = expansion_table(tab)
    v_s = splats(tab, 0)
    side_power = jnp.concatenate([sides.power(k) for k in range(rows // 8)], axis=0)
    n_p = s_ref.shape[0] // 8
    spread_power(pw_ref, n_p, [(FRONT, jnp.concatenate([src_ref[...], side_power], axis=1))])
    h = sink(width)

    for i in range(0, own + 2 * STEP + 2, STEP):
        later = []
        for g in range(i, min(i + STEP, own)):
            temp = jnp.concatenate([w_ref[16 * g : 16 * g + 8, :], sides.cell(g, 0)], axis=1)
            code = jnp.concatenate([w_ref[16 * g + 8 : 16 * g + 16, :], sides.cell(g, 1)], axis=1)
            s, al = choose([v_s], code)[0], lookup(t_al, code)
            later += [(s_ref, FRONT + g, s), (q0_ref, FRONT + g, s * temp), (al_ref, FRONT + g, al)]
        for g in range(max(1, i - STEP - 1), min(i - 1, own - 1)):
            r = FRONT + g
            inv, q1 = first_sweep(s_ref, q0_ref, r, power_row(pw_ref, n_p, r), h)
            later += [(di_ref, r, inv), (q1_ref, r, q1)]
        for g in range(max(2, i - 2 * STEP - 2), min(i - STEP - 2, own - 2)):
            r = FRONT + g
            t2 = second_sweep(s_ref, q1_ref, di_ref, r, power_row(pw_ref, n_p, r))
            later += [(t_ref, r, t2), (ea_ref, r, row8(al_ref, r) * t2)]
        for ref, r, x in later:
            ref[at8(r), :] = x

    def strain(m, carry):
        i = FRONT + 3 * m
        x = row8(ea_ref, i) + row8(ea_ref, i + 1) + row8(ea_ref, i + 2)
        strain_ref[at8(m), :] = restrict_columns(x)
        return carry

    lax.fori_loop(1, (own - 2) // 3, strain, 0, unroll=UNROLL_STRAIN)


def couple_sum(rows3):
    near = [[None] * 3 for _ in range(3)]
    for j in range(3):
        below, mid, above = rows3[j]
        near[0][j] = next_sub(mid) + prev_sub(mid)
        near[1][j] = above + below
        near[2][j] = next_lane(mid) + prev_lane(mid)
    out = []
    for i in range(3):
        j, k = [x for x in range(3) if x != i]
        main = near[i][i] + 0.5 * (near[j][i] + near[k][i])
        side = (near[i][j] + near[j][j]) + (near[i][k] + near[k][k])
        out.append(main + 0.25 * side)
    return out


def moduli(values, code):
    (mod,) = choose([values], code)
    inside = mod > 0.0
    root = jnp.sqrt(mod)
    return mod, root, jnp.where(inside, 1.0 / jnp.where(inside, root, 1.0), 0.0)


def k_mech(n_edges, n_col, rows, tab, mw_ref, *refs):
    sides = Sides(n_col, rows, rows // 6, refs[0], refs[n_edges - 1])
    mi_ref, mod_ref = refs[n_edges : n_edges + 2]
    uu_refs = refs[n_edges + 2 : n_edges + 5]
    pre_refs = refs[n_edges + 5 : n_edges + 8]
    values = splats(tab, 1)
    count = mw_ref.shape[0] // 32
    for m in range(count):
        fields = []
        for f in range(4):
            side = sides.field(m, f)
            fields.append(jnp.concatenate([mw_ref[32 * m + 8 * f : 32 * m + 8 * f + 8, :], side], axis=1))
        mod_ref[at8(m), :], root, mi_ref[at8(m), :] = moduli(values, fields[3])
        for f in range(3):
            uu_refs[f][at8(m), :] = root * fields[f]
    for m in range(1, count - 1):
        near = couple_sum([[row8(r, m - 1), row8(r, m), row8(r, m + 1)] for r in uu_refs])
        for d in range(3):
            pre_refs[d][at8(m), :] = near[d] * (1.0 / STIFF_DIAG) - row8(uu_refs[d], m)


def edge_patch(n_edges, e, corners, zr_ref, v_s, t_al, scratch):
    s_ref, q0_ref, q1_ref, di_ref = scratch
    side = edge_side(n_edges, e)
    lanes = edge_tile(side, zr_ref.shape[1])
    lane = lane_iota()
    mine = ((lane >= LANES - HALO) & (side == 1)) | ((lane < HALO) & (side == 0))
    per = LANES // SPAN

    def strip(i):
        x = zr_ref[far_place(e, i // per, zr_ref.shape[1])]
        return pltpu.roll(x, LANES - SPAN * (i % per) - side * HALO, 1)

    def cell(j, kind):
        held = 2 + kind
        if j < held:
            at = (Z_TEMP, Z_CODE)[kind] + 8 * j
            x = zr_ref[at : at + 8, lanes]
        else:
            x = strip(kind * (HALO - 2) + j - held)
        return jnp.where(mine, x, corners.cell(j, kind))

    codes = {}
    for j in range(HALO):
        codes[j] = cell(j, 1)
        (s,) = choose([v_s], codes[j])
        s_ref[at8(j), :] = s
        q0_ref[at8(j), :] = s * cell(j, 0)
    power = [
        jnp.where(mine, zr_ref[Z_POWER : Z_POWER + 8, lanes], corners.power(0)),
        jnp.where(mine, strip(2 * HALO - 5), corners.power(1)),
    ]
    top = sub_iota(LANES) == 0
    h = sink(LANES)

    def power_of(j):
        x = power[j // 8][j % 8 : j % 8 + 1, :]
        return jnp.where(top, jnp.broadcast_to(x, (8, LANES)), 0.0)

    heat = {}
    for j in range(1, HALO - 1):
        di_ref[at8(j), :], heat[j] = first_sweep(s_ref, q0_ref, j, power_of(j), h)
        q1_ref[at8(j), :] = heat[j]

    def expansion(j):
        return lookup(t_al, codes[j]) * second_sweep(s_ref, q1_ref, di_ref, j, power_of(j))

    out = [heat[1], heat[2], expansion(2)]
    for f in range(FAR):
        j = FAR_ROW + 3 * f
        out.append(expansion(j) + expansion(j + 1) + expansion(j + 2))
    return out


def k_outer(n_edges, n_col, rows, tab, zr_ref, *refs):
    sides = Sides(n_col, rows, rows // 6, refs[0], refs[n_edges - 1])
    corners = Sides(n_col, rows, rows // 6, refs[n_edges], refs[2 * n_edges - 1])
    rest = refs[2 * n_edges :]
    s_in, al_in, q0_in, q1_in, di_in, t_in, ea_in, strain_in, src_ref = rest[:9]
    mi_in, mod_in = rest[9:11]
    uu_in, pre_in = rest[11:14], rest[14:17]
    x_ref, keep_ref, u_ref = rest[17:20]
    s_ref, q0_ref, q1_ref, di_ref, al_ref, ea_ref, t_keep, pw_ref = rest[20:28]
    st_ref, mi_ref, mod_ref, sf_ref = rest[28:32]
    uu_refs, p_refs, d_refs = rest[32:35], rest[35:38], rest[38:41]
    own = rows - 1
    wide = zr_ref.shape[1]
    half = wide // 2
    width = wide + LANES
    mcols = mod_in.shape[1] - LANES
    t_al = expansion_table(tab)
    v_s = splats(tab, 0)
    for g in range(3):
        k = AHEAD - 1 - g
        for dst, src in ((s_ref, s_in), (al_ref, al_in), (q0_ref, q0_in)):
            dst[at8(k), :] = row8(src, FRONT + g)
    ea_ref[at8(AHEAD - 3), :] = row8(ea_in, FRONT + 2)
    for g in (1, 2):
        q1_ref[at8(AHEAD - 1 - g), :] = row8(q1_in, FRONT + g)
    di_ref[at8(AHEAD - 2), :] = row8(di_in, FRONT + 1)
    n_p = s_ref.shape[0] // 8
    near = jnp.concatenate([src_ref[0:8, :], sides.power(0)], axis=1)
    far = jnp.concatenate([zr_ref[Z_POWER : Z_POWER + 8, :], corners.power(0)], axis=1)
    spread_power(
        pw_ref,
        n_p,
        [(AHEAD - 1, near[0:1, :]), (AHEAD - 2, near[1:2, :]), (AHEAD, far)],
    )
    h = sink(width)

    lane = lane_iota()
    has_left, has_right = sides.side > 0, sides.side < n_col - 1
    patches = [edge_patch(n_edges, e, corners, zr_ref, v_s, t_al, rest[41:45]) for e in range(n_edges)]

    def mend(x, k, near, reach):
        pieces = tiles(x)
        right, left = patches[0][k], patches[-1][k]
        pieces[0] = jnp.where((lane < near) & has_left, left, pieces[0])
        pieces[-1] = jnp.where((lane >= LANES - near) & has_right, right, pieces[-1])
        beside = jnp.where((lane < reach) & has_right, right, jnp.where((lane >= LANES - reach) & has_left, left, 0.0))
        return jnp.concatenate(pieces + [beside], axis=1)

    for j in range(KEEP):
        code = jnp.concatenate([zr_ref[Z_CODE + 8 * j : Z_CODE + 8 * j + 8, :], corners.cell(j, 1)], axis=1)
        s = choose([v_s], code)[0]
        s_ref[at8(AHEAD + j), :] = s
        if j < 2:
            temp = jnp.concatenate([zr_ref[Z_TEMP + 8 * j : Z_TEMP + 8 * j + 8, :], corners.cell(j, 0)], axis=1)
            q0_ref[at8(AHEAD + j), :] = s * temp
            al_ref[at8(AHEAD + j), :] = lookup(t_al, code)
            at = Z_HEAT + 8 * j
            q1_ref[at8(AHEAD + 1 + j), :] = mend(zr_ref[at : at + 8, :], j, KEEP, HALO)
    for r in (AHEAD - 1, AHEAD):
        di_ref[at8(r), :], q1_ref[at8(r), :] = first_sweep(s_ref, q0_ref, r, power_row(pw_ref, n_p, r), h)
    r = AHEAD + 1
    di_ref[at8(r), :] = 1.0 / (h + row8(s_ref, r) * conduct_sum(s_ref, r))
    for r in range(AHEAD - 2, AHEAD + 2):
        t2 = second_sweep(s_ref, q1_ref, di_ref, r, power_row(pw_ref, n_p, r))
        t_keep[at8(r), :] = t2
        ea_ref[at8(r), :] = row8(al_ref, r) * t2
    ea_ref[at8(AHEAD + 2), :] = mend(zr_ref[Z_STRAIN : Z_STRAIN + 8, :], 2, KEEP, HALO)

    core = lax.axis_index(CORE)

    def other_half(x):
        return jnp.where(core == 0, x[:, half:wide], x[:, 0:half])

    def own_half(x):
        return jnp.where(core == 0, x[:, 0:half], x[:, half:wide])

    for g in range(2):
        t2 = row8(t_keep, AHEAD - 1 - g)
        keep_ref[8 * g : 8 * g + 8, :] = own_half(t2)
        x_ref[8 * g : 8 * g + 8, :] = other_half(t2)
    x_ref[16:24, :] = other_half(row8(t_in, FRONT + 2))

    count = mod_in.shape[0] // 8
    mrows = count - MHALO
    mwidth = mod_in.shape[1]
    n_m = count + MHALO
    for m in range(MHALO + 1 - FAR):
        i = AHEAD - 3 + 3 * m
        x = row8(ea_ref, i) + row8(ea_ref, i + 1) + row8(ea_ref, i + 2)
        st_ref[at8(MHALO - m), :] = restrict_columns(x)
    for f in range(FAR):
        at = Z_SUM + 8 * f
        st_ref[at8(FAR - 1 - f), :] = restrict_columns(mend(zr_ref[at : at + 8, :], 3 + f, KEEP, HALO))
    for m in range(1, count):
        st_ref[at8(MHALO + m), :] = row8(strain_in, m)
    values = splats(tab, 1)
    for i in range(MHALO):
        j = MHALO - 1 - i
        fields = []
        for f in range(4):
            body = zr_ref[Z_SOLID + ML * f : Z_SOLID + ML * f + 8, mcols * j : mcols * (j + 1)]
            body = jnp.where(sub_iota(mcols) < ML, body, 0.0)
            side = corners.field(j, f)
            fields.append(jnp.concatenate([body, side], axis=1))
        mod_ref[at8(i), :], root, mi_ref[at8(i), :] = moduli(values, fields[3])
        for f in range(3):
            uu_refs[f][at8(i), :] = root * fields[f]
    for ref, src in zip((mi_ref, mod_ref, *uu_refs), (mi_in, mod_in, *uu_in)):
        ref[8 * MHALO : 8 * n_m, :] = src[...]
    for i in range(n_m):
        sf_ref[at8(i), :] = row8(mod_ref, i) * row8(st_ref, i)
    sign = jnp.where(core == 0, 0.5, -0.5).astype(jnp.float32)
    for i in range(1, n_m - 1):
        load = row8(sf_ref, i)
        force = [
            0.5 * (next_sub(load) - prev_sub(load)),
            sign * (row8(sf_ref, i + 1) - row8(sf_ref, i - 1)),
            0.5 * (next_lane(load) - prev_lane(load)),
        ]
        inv = row8(mi_ref, i)
        inside = inv > 0.0
        if i <= MHALO:
            near = couple_sum([[row8(r, i - 1), row8(r, i), row8(r, i + 1)] for r in uu_refs])
            pre = [near[d] * (1.0 / STIFF_DIAG) - row8(uu_refs[d], i) for d in range(3)]
        else:
            pre = [row8(r, i - MHALO) for r in pre_in]
        inv = inv * (1.0 / STIFF_DIAG)
        for d in range(3):
            p_refs[d][at8(i), :] = jnp.where(inside, force[d] * inv + pre[d], 0.0)
    c_near = 2.0 * RHO1 / DELTA / STIFF_DIAG
    c_self = 1.0 + RHO1 * RHO0
    for i in range(2, n_m - 2):
        near = couple_sum([[row8(r, i - 1), row8(r, i), row8(r, i + 1)] for r in p_refs])
        inv = row8(mi_ref, i)
        for d in range(3):
            moved = row8(uu_refs[d], i) + c_self * row8(p_refs[d], i) + c_near * near[d]
            d_refs[d][at8(i), :] = moved * inv
    sub = sub_iota(mwidth)
    weight = jnp.where(sub < ML, (ML - sub).astype(jnp.float32) * (1.0 / (ML * (ML + 1) / 2.0)), 0.0)
    x_ref[24:32, :] = jnp.zeros((8, x_ref.shape[1]), jnp.float32)
    for g in range(mrows):
        i = MHALO + g
        u0, u2 = row8(d_refs[0], i), row8(d_refs[2], i)
        div = 0.5 * (next_sub(u0) - prev_sub(u0)) + 0.5 * (next_lane(u2) - prev_lane(u2))
        div = div + sign * (row8(d_refs[1], i + 1) - row8(d_refs[1], i - 1))
        stress = row8(mod_ref, i) * (div - 3.0 * row8(st_ref, i))
        die = jnp.sum(weight * stress, axis=0, keepdims=True)
        first, second = die[:, 0:LANES], die[:, LANES : 2 * LANES]
        keep_ref[16 + g : 17 + g, 0:LANES] = jnp.where(core == 0, first, second)
        x_ref[24 + g : 25 + g, 0:LANES] = jnp.where(core == 0, second, first)
        for d in range(3):
            u_ref[8 * (mrows * d + g) : 8 * (mrows * d + g) + 8, :] = row8(d_refs[d], i)[:, 0:mcols]


def put(ref, at, x):
    count = ref.shape[0] * LANES // x.shape[1]
    for t, piece in enumerate(tiles(x)):
        ref[count * t + at : count * t + at + piece.shape[0], :] = piece


def k_most(rows, mrows, t_in, keep_ref, u_in, t_out, u_out, warm_ref, buf, ubuf, t_vm, u_vm, sem):
    half = keep_ref.shape[1]
    mcols = u_in.shape[1]
    core = lax.axis_index(CORE)

    def build(rev):
        lo = half if rev else 0
        for g in range(rows - 8):
            i = rows - 1 - g if rev else g
            if g < 2:
                x = keep_ref[8 * g : 8 * g + 8, :]
            else:
                x = t_in[8 * (FRONT + g) : 8 * (FRONT + g) + 8, lo : lo + half]
            put(buf, 8 * (i - 8 if rev else i), x)
        for g in range(mrows):
            i = mrows - 1 - g if rev else g
            for d in range(3):
                put(ubuf, 8 * (mrows * d + i), row8(u_in, mrows * d + g))

    @pl.when(core == 0)
    def _():
        build(False)

    @pl.when(core != 0)
    def _():
        build(True)

    most = rows - 8
    for t in range(half // LANES):
        for l in range(DEPTH):
            t_vm[l, :, tile_lanes(t)] = buf[pl.ds(8 * most * t + l, most, stride=8), :]
    first = pl.ds(pl.multiple_of(8 * core, 8), most)
    out = pltpu.make_async_copy(t_vm, t_out.at[:, first, :], sem.at[0])
    out.start()
    for t in range(mcols // LANES):
        for d in range(3):
            for l in range(ML):
                u_vm[d, l, :, tile_lanes(t)] = ubuf[pl.ds(8 * mrows * (3 * t + d) + l, mrows, stride=8), :]
    u_copy = pltpu.make_async_copy(u_vm, u_out, sem.at[1])
    u_copy.start()
    warm_ref[first, :] = 1.0 + 0.2 * t_vm[0]
    out.wait()
    u_copy.wait()


def k_last(rows, mrows, t_in, keep_ref, xr_ref, warm_ref, t_old, t_out, slow_ref, buf, die, wide_die, t_vm, s_vm, sem):
    half = keep_ref.shape[1]
    core = lax.axis_index(CORE)

    def build(rev):
        lo = half if rev else 0
        for g in range(rows - 8, rows):
            if g < rows - 3:
                x = t_in[8 * (FRONT + g) : 8 * (FRONT + g) + 8, lo : lo + half]
            else:
                k = rows - 1 - g
                x = xr_ref[8 * k : 8 * k + 8, :]
            put(buf, 8 * (rows - 1 - g if rev else g - rows + 8), x)
        for g in range(mrows):
            mine = 2 * mrows - 1 - g if rev else g
            theirs = g if rev else 2 * mrows - 1 - g
            die[mine : mine + 1, :] = keep_ref[16 + g : 17 + g, 0:LANES]
            die[theirs : theirs + 1, :] = xr_ref[24 + g : 25 + g, 0:LANES]

    @pl.when(core == 0)
    def _():
        build(False)

    @pl.when(core != 0)
    def _():
        build(True)

    for t in range(half // LANES):
        for l in range(DEPTH):
            t_vm[l, :, tile_lanes(t)] = buf[pl.ds(64 * t + l, 8, stride=8), :]
    at = pl.ds(pl.multiple_of((rows - 8) * (1 - core), 8), 8)
    out = pltpu.make_async_copy(t_vm, t_out.at[:, at, :], sem.at[0])
    out.start()
    s_vm[...] = warm_ref[...]
    s_vm[at, :] = 1.0 + 0.2 * t_vm[0]
    lane = lane_iota(2 * mrows)
    for t in range(half // LANES):
        x = gather_lanes(die[...], (lane + LANES * t) // 3)
        for b in range(3):
            wide_die[pl.ds(b, 2 * mrows, stride=3), :] = x
        s_vm[:, tile_lanes(t)] = s_vm[:, tile_lanes(t)] + 0.5 * wide_die[...]
    slow = pltpu.make_async_copy(s_vm, slow_ref, sem.at[1])
    slow.start()
    out.wait()
    slow.wait()


def pairs(dims, sends):
    index = {}
    for r in range(dims[0]):
        for c in range(dims[1]):
            for a in range(dims[2]):
                index[(r, c, a)] = (r * dims[1] + c) * dims[2] + a
    out = []
    for source in index:
        target = sends(*source)
        if target in index:
            out.append((index[source], index[target]))
    return out


def per_device(temp, ids, power, mat, offset, heat_table, growth_table, modulus_table):
    axes = ("row", "col", "lay")
    dims = tuple(lax.axis_size(x) for x in axes)
    n_col = dims[1]
    _, rows, half = temp.shape
    _, _, mrows, mcols = offset.shape
    n_edges = 1 if n_col == 2 else 2
    n_t = half // LANES
    m_t = mcols // LANES

    def send(x, sends):
        return lax.ppermute(x, axes, pairs(dims, sends))

    def swap(r, c, a):
        return (r, c, 1 - a)

    def along(r, c, a):
        return (r + 1, c, 0) if a == 1 else (r - 1, c, 1)

    wide = 2 * half
    own = rows - 1
    kind = lax.broadcasted_iota(jnp.int32, (2, *temp.shape), 0)
    both = jnp.where(kind == 0, temp[None], power[None, None])
    tab = jnp.stack([heat_table, growth_table, modulus_table])
    tab = jnp.pad(tab, ((0, 0), (1, LANES - 1 - tab.shape[1])))
    (tab,) = call(k_tables, [(16 * (NMAT + 1) + 8, LANES)], [tab])
    n = 16 * HALO
    n_far = 8 * far_rows(rows)
    cells, one = call(k_rows, [(16 * rows * n_t, LANES), ((n + 16) * n_t, LANES)], [both, ids])
    got1 = send(one, swap)
    two, mg = call(
        functools.partial(k_rest, n_edges),
        [
            ((16 * (rows - 1 - HALO) + rows - 16) * n_t + 4 * ML * MHALO * m_t + n_far + 8 * n_edges, LANES),
            (32 * mrows, mcols),
        ],
        [both, cells, offset, mat],
        scratch=[(32 * mrows * m_t, LANES)],
    )
    got2 = send(two, swap)
    *own_part, far = call(
        functools.partial(k_half, n_edges),
        [(8 * HALO, half)] * 3 + [(n_far * n_edges, LANES)],
        [tab, both, cells],
    )
    n_c = 32 + n_far - 8 * (-4 * (mrows - MHALO) * MSPAN // LANES) + 8
    z, first_rows, *edges = call(
        functools.partial(k_edge, n_edges),
        [(far_place(n_edges, -1, wide)[0].stop, wide), (n + 16, wide)] + [(32, LANES)] * n_edges,
        [tab, both, cells, got1, mg, *own_part],
        cost=EDGE_COST,
        scratch=[(8 * HALO, wide)] * 5,
    )
    leaving = [z, *edges]
    leaving = call(
        functools.partial(k_beside, n_edges, rows),
        [(n_c, LANES)] * n_edges + [x.shape for x in leaving],
        [far, got2, mg] + leaving,
        aliases={3 + k: n_edges + k for k in range(len(leaving))},
    )
    beside, z, near = leaving[:n_edges], leaving[n_edges], leaving[n_edges + 1 :]
    zr = send(z, along)
    if n_edges == 1:
        sides = [send(beside[0], lambda r, c, a: (r, 1 - c, a))]
        corners = [send(near[0], lambda r, c, a: along(r, 1 - c, a))]
    else:
        sides = [send(beside[0], lambda r, c, a: (r, c + 1, a)), send(beside[1], lambda r, c, a: (r, c - 1, a))]
        corners = [
            send(near[0], lambda r, c, a: along(r, c + 1, a)),
            send(near[1], lambda r, c, a: along(r, c - 1, a)),
        ]
    w, src, mw = call(
        functools.partial(k_chip, rows),
        [(16 * own, wide), (rows, wide), (32 * (mrows + MHALO), mcols)],
        [both, cells, got2, mg, first_rows],
    )
    width = wide + LANES
    mwidth = mcols + LANES
    n_w = 8 * (rows + FRONT + 4)
    inner = call(
        functools.partial(k_inner, n_edges, n_col, rows),
        [(n_w, width)] * 7 + [(8 * (mrows + MHALO), mwidth)],
        [tab, w, src] + sides,
        scratch=[(n_w * (width // LANES), LANES)],
    )
    t2 = inner[5]
    solid = call(
        functools.partial(k_mech, n_edges, n_col, rows), [(8 * (mrows + MHALO), mwidth)] * 8, [tab, mw] + sides
    )
    n_h = 8 * (AHEAD + HALO + 5)
    n_m = 8 * (mrows + 2 * MHALO)
    x, keep, u = call(
        functools.partial(k_outer, n_edges, n_col, rows),
        [(32, half), (24, half), (24 * mrows, mcols)],
        [tab, zr] + sides + corners + list(inner) + [src] + list(solid),
        scratch=[(n_h, width)] * 7
        + [(n_h * (width // LANES), LANES)]
        + [(n_m, mwidth)] * 13
        + [(8 * HALO, LANES)] * 4,
    )
    xr = send(x, swap)
    t_most, u_out, warm = call(
        functools.partial(k_most, rows, mrows),
        [temp.shape, offset.shape, power.shape],
        [t2, keep, u],
        scratch=[
            (8 * (rows - 8) * n_t, LANES),
            (24 * mrows * m_t, LANES),
            (temp.shape[0], rows - 8, half),
            offset.shape,
            pltpu.SemaphoreType.DMA((2,)),
        ],
        out_specs=[HBM, HBM, VMEM],
    )
    t_out, slow = call(
        functools.partial(k_last, rows, mrows),
        [temp.shape, power.shape],
        [t2, keep, xr, warm, t_most],
        scratch=[
            (64 * n_t, LANES),
            (2 * mrows, LANES),
            (rows, LANES),
            (temp.shape[0], 8, half),
            power.shape,
            pltpu.SemaphoreType.DMA((2,)),
        ],
        specs=[VMEM] * 4 + [HBM],
        out_specs=[HBM, HBM],
        aliases={4: 0},
    )
    return t_out, u_out, slow


def solution(mesh):
    placed = (
        P("grp", "row", ("col", "lay")),
        P("grp", "row", ("col", "lay")),
        P(("grp", "row"), ("col", "lay")),
        P("grp", ("row", "lay"), "col"),
        P(None, "grp", ("row", "lay"), "col"),
        P(),
        P(),
        P(),
    )
    return jax.shard_map(
        per_device,
        mesh=mesh,
        in_specs=placed,
        out_specs=(
            P("grp", "row", ("col", "lay")),
            P(None, "grp", ("row", "lay"), "col"),
            P(("grp", "row"), ("col", "lay")),
        ),
        check_vma=False,
    )
```

```python
import functools

import jax
import jax.numpy as jnp
from jax import lax
from jax.experimental import pallas as pl
from jax.experimental.pallas import tpu as pltpu
from jax.sharding import PartitionSpec as P

DEPTH = 8
ML = 6
LANES = 128
HALO = 11
MHALO = 3

STIFF_DIAG = 12.0
THETA = 1.0
DELTA = 0.75
SIGMA = THETA / DELTA
RHO0 = 1.0 / SIGMA
RHO1 = 1.0 / (2.0 * SIGMA - RHO0)

VMEM = pl.BlockSpec(memory_space=pltpu.VMEM)
FRONT = 9
AHEAD = 5
STEP = 3
SPAN = 11
MSPAN = 8
NMAT = 16
FAR = 2
EDGE_COST = 10**10
FAR_ROW = 9 - 3 * FAR
KEEP = 3
Z_TEMP, Z_CODE, Z_HEAT, Z_STRAIN, Z_SUM, Z_SOLID, Z_POWER, Z_FAR = 0, 16, 40, 56, 64, 80, 104, 112
CORE = "lay"
UNROLL_STRAIN = 3


def call(kernel, outs, args, scratch=(), specs=None, aliases=None, cost=0):
    return pl.pallas_call(
        kernel,
        out_shape=[jax.ShapeDtypeStruct(s, jnp.float32) for s in outs],
        in_specs=specs or [VMEM] * len(args),
        out_specs=[VMEM] * len(outs),
        input_output_aliases=aliases or {},
        cost_estimate=pl.CostEstimate(flops=cost, bytes_accessed=0, transcendentals=0) if cost else None,
        scratch_shapes=[pltpu.VMEM(s, jnp.float32) if isinstance(s, tuple) else s for s in scratch],
        compiler_params=pltpu.CompilerParams(vmem_limit_bytes=16 * 1024 * 1024),
    )(*args)


def lane_iota(rows=8):
    return lax.broadcasted_iota(jnp.int32, (rows, LANES), 1)


def sub_iota(width):
    return lax.broadcasted_iota(jnp.int32, (8, width), 0)


def tile_lanes(t):
    return slice(LANES * t, LANES * (t + 1))


def tiles(x):
    return [x[:, tile_lanes(t)] for t in range(x.shape[1] // LANES)]


def table_of(ref, k):
    return jnp.broadcast_to(ref[k : k + 1, :], (8, LANES))


def gather_lanes(table, index):
    return jnp.take_along_axis(table, index, axis=1, mode="promise_in_bounds")


def lookup(table, code):
    return jnp.concatenate([gather_lanes(table, c.astype(jnp.int32)) for c in tiles(code)], axis=1)


def k_tables(tab, out_ref):
    for k, table in enumerate((jnp.sqrt(table_of(tab, 0)), table_of(tab, 2))):
        for m in range(NMAT + 1):
            at = 8 * ((NMAT + 1) * k + m)
            out_ref[at : at + 8, :] = jnp.broadcast_to(table[:, m : m + 1], (8, LANES))
    out_ref[16 * (NMAT + 1) : 16 * (NMAT + 1) + 8, :] = table_of(tab, 1)


def splats(tab, k):
    return [row8(tab, (NMAT + 1) * k + m) for m in range(NMAT + 1)]


def expansion_table(tab):
    return row8(tab, 2 * (NMAT + 1))


def choose(lists, code):
    out = [[] for _ in lists]
    for c in tiles(code):
        c = c.astype(jnp.int32)
        bits = [(c & (1 << k)) != 0 for k in range(5)]
        for n, values in enumerate(lists):
            level = values[:16]
            for k in range(4):
                level = [jnp.where(bits[k], b, a) for a, b in zip(level[::2], level[1::2])]
            out[n].append(jnp.where(bits[4], values[16], level[0]))
    return [jnp.concatenate(x, axis=1) for x in out]


def prev_lane(x):
    return pltpu.roll(x, 1, 1)


def next_lane(x):
    return pltpu.roll(x, x.shape[1] - 1, 1)


def prev_sub(x):
    return pltpu.roll(x, 1, 0)


def next_sub(x):
    return pltpu.roll(x, 7, 0)


def at8(i):
    return pl.ds(8 * i, 8) if isinstance(i, int) else pl.ds(pl.multiple_of(8 * i, 8), 8)


def row8(ref, i):
    return ref[at8(i), :]


def turned(core, last, g):
    return core * last + (1 - 2 * core) * g


def k_rows(in_ref, id_ref, a_ref, one_ref):
    other = 1 - lax.axis_index(CORE)
    rows = in_ref.shape[2]
    n_t = in_ref.shape[3] // LANES
    n = 16 * HALO
    for t in range(n_t):
        at = 16 * rows * t
        for l in range(DEPTH):
            a_ref[pl.ds(at + l, rows, stride=16), :] = in_ref[0, l, :, tile_lanes(t)]
            a_ref[pl.ds(at + DEPTH + l, rows, stride=16), :] = (id_ref[l, :, tile_lanes(t)] + 1).astype(jnp.float32)
    for t in range(n_t):
        to = (n + 16) * t
        for g in range(HALO):
            i = 16 * (rows * t + turned(other, rows - 1, g))
            one_ref[to + 16 * g : to + 16 * g + 16, :] = a_ref[pl.ds(pl.multiple_of(i, 16), 16), :]
        for b in range(2):
            one_ref[to + n + 8 * b : to + n + 8 * b + 8, :] = power_rows(in_ref, other, b, t)


def k_rest(n_edges, in_ref, a_ref, u_ref, mat_ref, two_ref, mg_ref, m_ref):
    core = lax.axis_index(CORE)
    other = 1 - core
    rows = in_ref.shape[2]
    n_t = in_ref.shape[3] // LANES
    mrows = mat_ref.shape[1]
    mcols = mat_ref.shape[2]
    m_t = mcols // LANES
    m_ref[...] = jnp.zeros(m_ref.shape, jnp.float32)
    for t in range(m_t):
        at = 32 * mrows * t
        for l in range(ML):
            for f in range(3):
                m_ref[pl.ds(at + 8 * f + l, mrows, stride=32), :] = u_ref[f, l, :, tile_lanes(t)]
            m_ref[pl.ds(at + 24 + l, mrows, stride=32), :] = (mat_ref[l, :, tile_lanes(t)] + 1).astype(jnp.float32)
        for g in range(mrows):
            i = 32 * (mrows * t + turned(core, mrows - 1, g))
            mg_ref[32 * g : 32 * g + 32, tile_lanes(t)] = m_ref[pl.ds(pl.multiple_of(i, 32), 32), :]
    for e in range(n_edges):
        side = edge_side(n_edges, e)
        fields = []
        for g in range(MHALO):
            i = 32 * (mrows * side * (m_t - 1) + turned(core, mrows - 1, mrows - 1 - g))
            fields += [m_ref[pl.ds(pl.multiple_of(i + 8 * f, 8), 8), :] for f in range(4)]
        at = two_ref.shape[0] - 8 * (n_edges - e)
        (two_ref[at : at + 8, :],) = packed(side, fields, MSPAN, MHALO)
    for k, x in enumerate(far_strip(in_ref, a_ref, other, core * (n_t - 1), core)):
        at = two_ref.shape[0] - 8 * (n_edges + far_rows(rows) - k)
        two_ref[at : at + 8, :] = x
    rest = 16 * (rows - 1 - HALO)
    for t in range(n_t):
        to = (rest + rows - 16) * t
        for g in range(HALO, rows - 1):
            i = 16 * (rows * t + turned(other, rows - 1, g))
            k = to + 16 * (g - HALO)
            two_ref[k : k + 16, :] = a_ref[pl.ds(pl.multiple_of(i, 16), 16), :]
        for b in range(2, rows // 8):
            two_ref[to + rest + 8 * (b - 2) : to + rest + 8 * (b - 1), :] = power_rows(in_ref, other, b, t)
    for t in range(m_t):
        for g in range(MHALO):
            i = 32 * (mrows * t + turned(core, mrows - 1, mrows - 1 - g))
            k = (rest + rows - 16) * n_t + 32 * (MHALO * t + g)
            two_ref[k : k + 32, :] = m_ref[pl.ds(pl.multiple_of(i, 32), 32), :]


def power_rows(in_ref, turn, b, t):
    rows = in_ref.shape[2]
    lanes = tile_lanes(t) if isinstance(t, int) else pl.ds(pl.multiple_of(LANES * t, LANES), LANES)
    x = in_ref[1, 0, at8(turned(turn, rows // 8 - 1, b)), lanes]
    return jnp.take_along_axis(x, turned(turn, 7, sub_iota(LANES)), axis=0, mode="promise_in_bounds")


def far_strip(in_ref, a_ref, turn, t, side):
    rows = in_ref.shape[2]
    blocks = []
    for g in range(HALO, rows - 1):
        i = 16 * (rows * t + turned(turn, rows - 1, g))
        blocks += [a_ref[pl.ds(pl.multiple_of(i + k, 8), 8), :] for k in (0, 8)]
    blocks += [power_rows(in_ref, turn, b, t) for b in range(2, rows // 8)]
    return packed(side, blocks, SPAN, HALO)


def edge_side(n_edges, e):
    return 1 - lax.axis_index("col") if n_edges == 1 else 1 - e


def edge_tile(side, width):
    if isinstance(side, int):
        return tile_lanes(side * (width // LANES - 1))
    return pl.ds(pl.multiple_of(side * (width - LANES), LANES), LANES)


def packed(side, blocks, span, keep):
    lane = lane_iota()
    per = LANES // span
    out = []
    for i in range(0, len(blocks), per):
        acc = jnp.zeros((8, LANES), jnp.float32)
        for k, x in enumerate(blocks[i : i + per]):
            acc = jnp.where(lane // span == k, pltpu.roll(x, span * k + side * keep, 1), acc)
        out.append(acc)
    return out


def far_rows(rows):
    return -(-(2 * (rows - 1 - HALO) + rows // 8 - 2) // (LANES // SPAN))


def k_half(n_edges, tab, in_ref, a_ref, s_ref, q0_ref, al_ref, far_ref):
    core = lax.axis_index(CORE)
    rows = in_ref.shape[2]
    n_t = in_ref.shape[3] // LANES
    v_s = splats(tab, 0)
    t_al = expansion_table(tab)
    for t in range(n_t):
        for g in range(HALO):
            i = 16 * (rows * t + turned(core, rows - 1, g))
            code = a_ref[pl.ds(pl.multiple_of(i + 8, 8), 8), :]
            (x,) = choose([v_s], code)
            s_ref[at8(g), tile_lanes(t)] = x
            q0_ref[at8(g), tile_lanes(t)] = x * a_ref[pl.ds(pl.multiple_of(i, 16), 8), :]
            if 2 <= g < 9:
                al_ref[at8(g), tile_lanes(t)] = lookup(t_al, code)
    for e in range(n_edges):
        side = edge_side(n_edges, e)
        for k, x in enumerate(far_strip(in_ref, a_ref, core, side * (n_t - 1), side)):
            at = 8 * (far_rows(rows) * e + k)
            far_ref[at : at + 8, :] = x


def k_edge(n_edges, tab, in_ref, a_ref, got_ref, mg_ref, s_own, q0_own, al_own, z_ref, w_ref, *refs):
    core = lax.axis_index(CORE)
    wide = z_ref.shape[1]
    half = wide // 2
    n_t = half // LANES
    rows = in_ref.shape[2]
    mcols = mg_ref.shape[1]
    n = 16 * HALO
    edge_refs, (s_ref, q0_ref, al_ref, q1_ref, di_ref) = refs[:n_edges], refs[n_edges:]
    v_s = splats(tab, 0)
    t_al = expansion_table(tab)

    def build(first):
        for t in range(n_t):
            lanes = tile_lanes(t if first else n_t + t)
            for g in range(HALO):
                i = 16 * (rows * t + (g if first else rows - 1 - g))
                w_ref[16 * g : 16 * g + 16, lanes] = a_ref[i : i + 16, :]
            for b in range(2):
                w_ref[n + 8 * b : n + 8 * b + 8, lanes] = power_rows(in_ref, 0 if first else 1, b, t)
            lanes = tile_lanes(n_t + t if first else t)
            at = (n + 16) * t
            w_ref[0 : n + 16, lanes] = got_ref[at : at + n + 16, :]
            for g in range(HALO):
                code = got_ref[at + 16 * g + 8 : at + 16 * g + 16, :]
                (x,) = choose([v_s], code)
                s_ref[at8(g), lanes] = x
                q0_ref[at8(g), lanes] = x * got_ref[at + 16 * g : at + 16 * g + 8, :]
                if 2 <= g < 9:
                    al_ref[at8(g), lanes] = lookup(t_al, code)
        lanes = slice(0, half) if first else slice(half, wide)
        for dst, src in ((s_ref, s_own), (q0_ref, q0_own), (al_ref, al_own)):
            dst[:, lanes] = src[...]

    @pl.when(core == 0)
    def _():
        build(True)

    @pl.when(core != 0)
    def _():
        build(False)

    for g in range(2):
        z_ref[Z_TEMP + 8 * g : Z_TEMP + 8 * g + 8, :] = w_ref[16 * g : 16 * g + 8, :]
    for g in range(3):
        z_ref[Z_CODE + 8 * g : Z_CODE + 8 * g + 8, :] = w_ref[16 * g + 8 : 16 * g + 16, :]
    z_ref[Z_POWER : Z_POWER + 8, :] = w_ref[n : n + 8, :]
    z_ref[Z_FAR:, :] = jnp.zeros((z_ref.shape[0] - Z_FAR, wide), jnp.float32)
    for g in range(MHALO):
        for f in range(4):
            at = Z_SOLID + ML * f
            z_ref[at : at + ML, mcols * g : mcols * (g + 1)] = mg_ref[32 * g + 8 * f : 32 * g + 8 * f + ML, :]
    for e in range(n_edges):
        side = edge_side(n_edges, e)
        lanes, mlanes = edge_tile(side, wide), edge_tile(side, mcols)
        blocks = [w_ref[8 * i : 8 * i + 8, lanes] for i in range(2 * HALO)]
        blocks += [w_ref[n + 8 * b : n + 8 * b + 8, lanes] for b in range(2)]
        fields = [mg_ref[8 * i : 8 * i + 8, mlanes] for i in range(4 * MHALO)]
        near = packed(side, blocks, SPAN, HALO) + packed(side, fields, MSPAN, MHALO)
        strip = blocks[4 : 2 * HALO : 2] + blocks[7 : 2 * HALO : 2] + blocks[2 * HALO + 1 :]
        for k, x in enumerate(packed(side, strip, SPAN, HALO)):
            z_ref[far_place(e, k, wide)] = x
        for k, x in enumerate(near):
            edge_refs[e][8 * k : 8 * k + 8, :] = x
    h = sink(wide)
    top = sub_iota(wide) == 0
    powers = {
        g: jnp.where(top, jnp.broadcast_to(w_ref[n + g : n + g + 1, :], (8, wide)), 0.0) for g in range(1, HALO - 1)
    }
    for g in range(1, HALO - 1):
        di_ref[at8(g), :], q1_ref[at8(g), :] = first_sweep(s_ref, q0_ref, g, powers[g], h, True)
    z_ref[Z_HEAT : Z_HEAT + 16, :] = q1_ref[8:24, :]

    def expansion(g):
        return row8(al_ref, g) * second_sweep(s_ref, q1_ref, di_ref, g, powers[g], True)

    z_ref[Z_STRAIN : Z_STRAIN + 8, :] = expansion(2)
    for f in range(FAR):
        g = FAR_ROW + 3 * f
        x = expansion(g) + expansion(g + 1) + expansion(g + 2)
        z_ref[Z_SUM + 8 * f : Z_SUM + 8 * f + 8, :] = x


def far_tiles():
    return -(-(2 * HALO - 4) // (LANES // SPAN))


def far_place(e, k, wide):
    q = far_tiles() * e + k
    at = Z_FAR + 8 * (q // (wide // LANES))
    return slice(at, at + 8), tile_lanes(q % (wide // LANES))


def k_beside(n_edges, rows, far_ref, got_ref, mg_ref, *refs):
    near_refs, c_refs = refs[:n_edges], refs[n_edges : 2 * n_edges]
    core = lax.axis_index(CORE)
    mrows = mg_ref.shape[0] // 32
    for e in range(n_edges):
        side = edge_side(n_edges, e)
        mlanes = edge_tile(side, mg_ref.shape[1])
        fields = [mg_ref[8 * i : 8 * i + 8, mlanes] for i in range(4 * MHALO, 4 * mrows)]
        far = [near_refs[e][8 * k : 8 * k + 8, :] for k in range(4)]
        for k in range(far_rows(rows)):
            at = got_ref.shape[0] - 8 * (n_edges + far_rows(rows) - k)
            x = row8(far_ref, far_rows(rows) * e + k)
            far.append(jnp.where(core == side, x, got_ref[at : at + 8, :]))
        far += packed(side, fields, MSPAN, MHALO)
        at = got_ref.shape[0] - 8 * (n_edges - e)
        far.append(got_ref[at : at + 8, :])
        for k, x in enumerate(far):
            c_refs[e][8 * k : 8 * k + 8, :] = x


def k_chip(rows, in_ref, a_ref, got_ref, mg_ref, first_ref, w_ref, src_ref, mw_ref):
    core = lax.axis_index(CORE)
    n_t = w_ref.shape[1] // LANES // 2
    mrows = mg_ref.shape[0] // 32
    n = 16 * HALO
    rest = 16 * (rows - 1 - HALO)
    w_ref[0:n, :] = first_ref[0:n, :]
    src_ref[0:16, :] = first_ref[n : n + 16, :]

    def build(first):
        for t in range(n_t):
            lanes = tile_lanes(t if first else n_t + t)
            for g in range(HALO, rows - 1):
                i = 16 * (rows * t + (g if first else rows - 1 - g))
                w_ref[16 * g : 16 * g + 16, lanes] = a_ref[i : i + 16, :]
            for b in range(2, rows // 8):
                src_ref[8 * b : 8 * b + 8, lanes] = power_rows(in_ref, 0 if first else 1, b, t)
            lanes = tile_lanes(n_t + t if first else t)
            at = (rest + rows - 16) * t
            w_ref[n : n + rest, lanes] = got_ref[at : at + rest, :]
            src_ref[16:rows, lanes] = got_ref[at + rest : at + rest + rows - 16, :]

    @pl.when(core == 0)
    def _():
        build(True)

    @pl.when(core != 0)
    def _():
        build(False)

    mw_ref[0 : 32 * mrows, :] = mg_ref[...]
    for t in range(mw_ref.shape[1] // LANES):
        at = (rest + rows - 16) * n_t + 32 * MHALO * t
        mw_ref[32 * mrows : 32 * (mrows + MHALO), tile_lanes(t)] = got_ref[at : at + 32 * MHALO, :]


class Sides:
    def __init__(self, n_col, rows, mrows, from_left, from_right):
        self.left = from_left
        self.right = from_right
        self.rows = rows
        self.mrows = mrows
        lane = lane_iota()
        col = lax.axis_index("col")
        self.masks = {
            w: ((lane < w) & (col < n_col - 1), (lane >= LANES - w) & (col > 0)) for w in (HALO, MHALO)
        }
        self.only = self.left is self.right
        self.side = col

    def take(self, v, k, span, width):
        right_mask, left_mask = self.masks[width]
        x = row8(self.right, v)
        if self.only:
            x = pltpu.roll(x, LANES - span * k - self.side * width, 1)
            return jnp.where(right_mask | left_mask, x, 0.0)
        r = pltpu.roll(x, (LANES - span * k) % LANES, 1)
        l = pltpu.roll(row8(self.left, v), LANES - span * k - width, 1)
        return jnp.where(right_mask, r, jnp.where(left_mask, l, 0.0))

    def block(self, first, i, span, width):
        per = LANES // span
        return self.take(first + i // per, i % per, span, width)

    def cell(self, g, kind):
        if g < HALO:
            return self.block(0, 2 * g + kind, SPAN, HALO)
        return self.block(4, 2 * (g - HALO) + kind, SPAN, HALO)

    def power(self, b):
        if b < 2:
            return self.block(0, 2 * HALO + b, SPAN, HALO)
        return self.block(4, 2 * (self.rows - 1 - HALO) + b - 2, SPAN, HALO)

    def field(self, m, f):
        if m < MHALO:
            return self.block(3, 4 * m + f, MSPAN, MHALO)
        first = 4 + far_rows(self.rows)
        if m < self.mrows:
            return self.block(first, 4 * (m - MHALO) + f, MSPAN, MHALO)
        first += -(-4 * (self.mrows - MHALO) * MSPAN // LANES)
        return self.block(first, 4 * (m - self.mrows) + f, MSPAN, MHALO)


def spread_power(ref, n, blocks):
    ref[...] = jnp.zeros(ref.shape, jnp.float32)
    count = ref.shape[0] // (n * 8)
    for first, x in blocks:
        for t, piece in enumerate(tiles(x)):
            ref[pl.ds(8 * (n * t + first), piece.shape[0], stride=8), :] = piece
    return count


def power_row(ref, n, i):
    count = ref.shape[0] // (n * 8)
    return jnp.concatenate([row8(ref, n * t + i) for t in range(count)], axis=1)


def conduct_sum(ref, i, closed=False):
    x = row8(ref, i)
    sub = sub_iota(x.shape[1])
    before, after = prev_lane(x), next_lane(x)
    if closed:
        lane = lax.broadcasted_iota(jnp.int32, x.shape, 1)
        before = jnp.where(lane > 0, before, 0.0)
        after = jnp.where(lane < x.shape[1] - 1, after, 0.0)
    total = row8(ref, i - 1) + row8(ref, i + 1) + before + after
    total = total + jnp.where(sub < DEPTH - 1, next_sub(x), 0.0)
    return total + jnp.where(sub > 0, prev_sub(x), 0.0)


def sink(width):
    return jnp.where(sub_iota(width) == DEPTH - 1, 2.0, 0.2).astype(jnp.float32)


def to_solid_layers(y):
    return jnp.where(sub_iota(y.shape[1]) < 3, y, next_sub(y)) * (1.0 / 9.0)


def gather_main(pieces):
    lane = 3 * lane_iota()
    out = []
    for j in range(len(pieces) // 3):
        total = None
        for k in range(3):
            got = None
            for t in range(3):
                g = gather_lanes(pieces[3 * j + t], (lane + k) & (LANES - 1))
                got = g if got is None else jnp.where(lane + k >= LANES * t, g, got)
            total = got if total is None else total + got
        out.append(total)
    return out


def gather_sides(piece):
    lane = lane_iota()
    first = LANES - MHALO
    inside = (lane < MHALO) | (lane >= first)
    index = jnp.where(lane < MHALO, 3 * lane, jnp.where(lane >= first, LANES - 9 + 3 * (lane - first), 0))
    total = gather_lanes(piece, index) + gather_lanes(piece, index + 1) + gather_lanes(piece, index + 2)
    return jnp.where(inside, total, 0.0)


def restrict_columns(x):
    pieces = tiles(x)
    return to_solid_layers(jnp.concatenate(gather_main(pieces[:-1]) + [gather_sides(pieces[-1])], axis=1))


def first_sweep(s_ref, q0_ref, i, power, h, closed=False):
    s = row8(s_ref, i)
    inv = 1.0 / (h + s * conduct_sum(s_ref, i, closed))
    return inv, s * ((power + s * conduct_sum(q0_ref, i, closed)) * inv)


def second_sweep(s_ref, q1_ref, di_ref, i, power, closed=False):
    return (power + row8(s_ref, i) * conduct_sum(q1_ref, i, closed)) * row8(di_ref, i)


def k_inner(n_edges, n_col, rows, tab, w_ref, src_ref, *refs):
    sides = Sides(n_col, rows, rows // 6, refs[0], refs[n_edges - 1])
    s_ref, al_ref, q0_ref, q1_ref, di_ref, t_ref, ea_ref, strain_ref, pw_ref = refs[n_edges:]
    own = rows - 1
    width = src_ref.shape[1] + LANES
    t_al = expansion_table(tab)
    v_s = splats(tab, 0)
    side_power = jnp.concatenate([sides.power(k) for k in range(rows // 8)], axis=0)
    n_p = s_ref.shape[0] // 8
    spread_power(pw_ref, n_p, [(FRONT, jnp.concatenate([src_ref[...], side_power], axis=1))])
    h = sink(width)

    for i in range(0, own + 2 * STEP + 2, STEP):
        later = []
        for g in range(i, min(i + STEP, own)):
            temp = jnp.concatenate([w_ref[16 * g : 16 * g + 8, :], sides.cell(g, 0)], axis=1)
            code = jnp.concatenate([w_ref[16 * g + 8 : 16 * g + 16, :], sides.cell(g, 1)], axis=1)
            s, al = choose([v_s], code)[0], lookup(t_al, code)
            later += [(s_ref, FRONT + g, s), (q0_ref, FRONT + g, s * temp), (al_ref, FRONT + g, al)]
        for g in range(max(1, i - STEP - 1), min(i - 1, own - 1)):
            r = FRONT + g
            inv, q1 = first_sweep(s_ref, q0_ref, r, power_row(pw_ref, n_p, r), h)
            later += [(di_ref, r, inv), (q1_ref, r, q1)]
        for g in range(max(2, i - 2 * STEP - 2), min(i - STEP - 2, own - 2)):
            r = FRONT + g
            t2 = second_sweep(s_ref, q1_ref, di_ref, r, power_row(pw_ref, n_p, r))
            later += [(t_ref, r, t2), (ea_ref, r, row8(al_ref, r) * t2)]
        for ref, r, x in later:
            ref[at8(r), :] = x

    def strain(m, carry):
        i = FRONT + 3 * m
        x = row8(ea_ref, i) + row8(ea_ref, i + 1) + row8(ea_ref, i + 2)
        strain_ref[at8(m), :] = restrict_columns(x)
        return carry

    lax.fori_loop(1, (own - 2) // 3, strain, 0, unroll=UNROLL_STRAIN)


def couple_sum(rows3):
    near = [[None] * 3 for _ in range(3)]
    for j in range(3):
        below, mid, above = rows3[j]
        near[0][j] = next_sub(mid) + prev_sub(mid)
        near[1][j] = above + below
        near[2][j] = next_lane(mid) + prev_lane(mid)
    out = []
    for i in range(3):
        j, k = [x for x in range(3) if x != i]
        main = near[i][i] + 0.5 * (near[j][i] + near[k][i])
        side = (near[i][j] + near[j][j]) + (near[i][k] + near[k][k])
        out.append(main + 0.25 * side)
    return out


def moduli(values, code):
    (mod,) = choose([values], code)
    inside = mod > 0.0
    root = jnp.sqrt(mod)
    return mod, root, jnp.where(inside, 1.0 / jnp.where(inside, root, 1.0), 0.0)


def k_mech(n_edges, n_col, rows, tab, mw_ref, *refs):
    sides = Sides(n_col, rows, rows // 6, refs[0], refs[n_edges - 1])
    mi_ref, mod_ref = refs[n_edges : n_edges + 2]
    uu_refs = refs[n_edges + 2 : n_edges + 5]
    pre_refs = refs[n_edges + 5 : n_edges + 8]
    values = splats(tab, 1)
    count = mw_ref.shape[0] // 32
    for m in range(count):
        fields = []
        for f in range(4):
            side = sides.field(m, f)
            fields.append(jnp.concatenate([mw_ref[32 * m + 8 * f : 32 * m + 8 * f + 8, :], side], axis=1))
        mod_ref[at8(m), :], root, mi_ref[at8(m), :] = moduli(values, fields[3])
        for f in range(3):
            uu_refs[f][at8(m), :] = root * fields[f]
    for m in range(1, count - 1):
        near = couple_sum([[row8(r, m - 1), row8(r, m), row8(r, m + 1)] for r in uu_refs])
        for d in range(3):
            pre_refs[d][at8(m), :] = near[d] * (1.0 / STIFF_DIAG) - row8(uu_refs[d], m)


def edge_patch(n_edges, e, corners, zr_ref, v_s, t_al, scratch):
    s_ref, q0_ref, q1_ref, di_ref = scratch
    side = edge_side(n_edges, e)
    lanes = edge_tile(side, zr_ref.shape[1])
    lane = lane_iota()
    mine = ((lane >= LANES - HALO) & (side == 1)) | ((lane < HALO) & (side == 0))
    per = LANES // SPAN

    def strip(i):
        x = zr_ref[far_place(e, i // per, zr_ref.shape[1])]
        return pltpu.roll(x, LANES - SPAN * (i % per) - side * HALO, 1)

    def cell(j, kind):
        held = 2 + kind
        if j < held:
            at = (Z_TEMP, Z_CODE)[kind] + 8 * j
            x = zr_ref[at : at + 8, lanes]
        else:
            x = strip(kind * (HALO - 2) + j - held)
        return jnp.where(mine, x, corners.cell(j, kind))

    codes = {}
    for j in range(HALO):
        codes[j] = cell(j, 1)
        (s,) = choose([v_s], codes[j])
        s_ref[at8(j), :] = s
        q0_ref[at8(j), :] = s * cell(j, 0)
    power = [
        jnp.where(mine, zr_ref[Z_POWER : Z_POWER + 8, lanes], corners.power(0)),
        jnp.where(mine, strip(2 * HALO - 5), corners.power(1)),
    ]
    top = sub_iota(LANES) == 0
    h = sink(LANES)

    def power_of(j):
        x = power[j // 8][j % 8 : j % 8 + 1, :]
        return jnp.where(top, jnp.broadcast_to(x, (8, LANES)), 0.0)

    heat = {}
    for j in range(1, HALO - 1):
        di_ref[at8(j), :], heat[j] = first_sweep(s_ref, q0_ref, j, power_of(j), h)
        q1_ref[at8(j), :] = heat[j]

    def expansion(j):
        return lookup(t_al, codes[j]) * second_sweep(s_ref, q1_ref, di_ref, j, power_of(j))

    out = [heat[1], heat[2], expansion(2)]
    for f in range(FAR):
        j = FAR_ROW + 3 * f
        out.append(expansion(j) + expansion(j + 1) + expansion(j + 2))
    return out


def k_outer(n_edges, n_col, rows, tab, zr_ref, *refs):
    sides = Sides(n_col, rows, rows // 6, refs[0], refs[n_edges - 1])
    corners = Sides(n_col, rows, rows // 6, refs[n_edges], refs[2 * n_edges - 1])
    rest = refs[2 * n_edges :]
    s_in, al_in, q0_in, q1_in, di_in, t_in, ea_in, strain_in, src_ref = rest[:9]
    mi_in, mod_in = rest[9:11]
    uu_in, pre_in = rest[11:14], rest[14:17]
    x_ref, keep_ref, u_ref = rest[17:20]
    s_ref, q0_ref, q1_ref, di_ref, al_ref, ea_ref, t_keep, pw_ref = rest[20:28]
    st_ref, mi_ref, mod_ref, sf_ref = rest[28:32]
    uu_refs, p_refs, d_refs = rest[32:35], rest[35:38], rest[38:41]
    own = rows - 1
    wide = zr_ref.shape[1]
    half = wide // 2
    width = wide + LANES
    mcols = mod_in.shape[1] - LANES
    t_al = expansion_table(tab)
    v_s = splats(tab, 0)
    for g in range(3):
        k = AHEAD - 1 - g
        for dst, src in ((s_ref, s_in), (al_ref, al_in), (q0_ref, q0_in)):
            dst[at8(k), :] = row8(src, FRONT + g)
    ea_ref[at8(AHEAD - 3), :] = row8(ea_in, FRONT + 2)
    for g in (1, 2):
        q1_ref[at8(AHEAD - 1 - g), :] = row8(q1_in, FRONT + g)
    di_ref[at8(AHEAD - 2), :] = row8(di_in, FRONT + 1)
    n_p = s_ref.shape[0] // 8
    near = jnp.concatenate([src_ref[0:8, :], sides.power(0)], axis=1)
    far = jnp.concatenate([zr_ref[Z_POWER : Z_POWER + 8, :], corners.power(0)], axis=1)
    spread_power(
        pw_ref,
        n_p,
        [(AHEAD - 1, near[0:1, :]), (AHEAD - 2, near[1:2, :]), (AHEAD, far)],
    )
    h = sink(width)

    lane = lane_iota()
    has_left, has_right = sides.side > 0, sides.side < n_col - 1
    patches = [edge_patch(n_edges, e, corners, zr_ref, v_s, t_al, rest[41:45]) for e in range(n_edges)]

    def mend(x, k, near, reach):
        pieces = tiles(x)
        right, left = patches[0][k], patches[-1][k]
        pieces[0] = jnp.where((lane < near) & has_left, left, pieces[0])
        pieces[-1] = jnp.where((lane >= LANES - near) & has_right, right, pieces[-1])
        beside = jnp.where((lane < reach) & has_right, right, jnp.where((lane >= LANES - reach) & has_left, left, 0.0))
        return jnp.concatenate(pieces + [beside], axis=1)

    for j in range(KEEP):
        code = jnp.concatenate([zr_ref[Z_CODE + 8 * j : Z_CODE + 8 * j + 8, :], corners.cell(j, 1)], axis=1)
        s = choose([v_s], code)[0]
        s_ref[at8(AHEAD + j), :] = s
        if j < 2:
            temp = jnp.concatenate([zr_ref[Z_TEMP + 8 * j : Z_TEMP + 8 * j + 8, :], corners.cell(j, 0)], axis=1)
            q0_ref[at8(AHEAD + j), :] = s * temp
            al_ref[at8(AHEAD + j), :] = lookup(t_al, code)
            at = Z_HEAT + 8 * j
            q1_ref[at8(AHEAD + 1 + j), :] = mend(zr_ref[at : at + 8, :], j, KEEP, HALO)
    for r in (AHEAD - 1, AHEAD):
        di_ref[at8(r), :], q1_ref[at8(r), :] = first_sweep(s_ref, q0_ref, r, power_row(pw_ref, n_p, r), h)
    r = AHEAD + 1
    di_ref[at8(r), :] = 1.0 / (h + row8(s_ref, r) * conduct_sum(s_ref, r))
    for r in range(AHEAD - 2, AHEAD + 2):
        t2 = second_sweep(s_ref, q1_ref, di_ref, r, power_row(pw_ref, n_p, r))
        t_keep[at8(r), :] = t2
        ea_ref[at8(r), :] = row8(al_ref, r) * t2
    ea_ref[at8(AHEAD + 2), :] = mend(zr_ref[Z_STRAIN : Z_STRAIN + 8, :], 2, KEEP, HALO)

    core = lax.axis_index(CORE)

    def other_half(x):
        return jnp.where(core == 0, x[:, half:wide], x[:, 0:half])

    def own_half(x):
        return jnp.where(core == 0, x[:, 0:half], x[:, half:wide])

    for g in range(2):
        t2 = row8(t_keep, AHEAD - 1 - g)
        keep_ref[8 * g : 8 * g + 8, :] = own_half(t2)
        x_ref[8 * g : 8 * g + 8, :] = other_half(t2)
    x_ref[16:24, :] = other_half(row8(t_in, FRONT + 2))

    count = mod_in.shape[0] // 8
    mrows = count - MHALO
    mwidth = mod_in.shape[1]
    n_m = count + MHALO
    for m in range(MHALO + 1 - FAR):
        i = AHEAD - 3 + 3 * m
        x = row8(ea_ref, i) + row8(ea_ref, i + 1) + row8(ea_ref, i + 2)
        st_ref[at8(MHALO - m), :] = restrict_columns(x)
    for f in range(FAR):
        at = Z_SUM + 8 * f
        st_ref[at8(FAR - 1 - f), :] = restrict_columns(mend(zr_ref[at : at + 8, :], 3 + f, KEEP, HALO))
    for m in range(1, count):
        st_ref[at8(MHALO + m), :] = row8(strain_in, m)
    values = splats(tab, 1)
    for i in range(MHALO):
        j = MHALO - 1 - i
        fields = []
        for f in range(4):
            body = zr_ref[Z_SOLID + ML * f : Z_SOLID + ML * f + 8, mcols * j : mcols * (j + 1)]
            body = jnp.where(sub_iota(mcols) < ML, body, 0.0)
            side = corners.field(j, f)
            fields.append(jnp.concatenate([body, side], axis=1))
        mod_ref[at8(i), :], root, mi_ref[at8(i), :] = moduli(values, fields[3])
        for f in range(3):
            uu_refs[f][at8(i), :] = root * fields[f]
    for ref, src in zip((mi_ref, mod_ref, *uu_refs), (mi_in, mod_in, *uu_in)):
        ref[8 * MHALO : 8 * n_m, :] = src[...]
    for i in range(n_m):
        sf_ref[at8(i), :] = row8(mod_ref, i) * row8(st_ref, i)
    sign = jnp.where(core == 0, 0.5, -0.5).astype(jnp.float32)
    for i in range(1, n_m - 1):
        load = row8(sf_ref, i)
        force = [
            0.5 * (next_sub(load) - prev_sub(load)),
            sign * (row8(sf_ref, i + 1) - row8(sf_ref, i - 1)),
            0.5 * (next_lane(load) - prev_lane(load)),
        ]
        inv = row8(mi_ref, i)
        inside = inv > 0.0
        if i <= MHALO:
            near = couple_sum([[row8(r, i - 1), row8(r, i), row8(r, i + 1)] for r in uu_refs])
            pre = [near[d] * (1.0 / STIFF_DIAG) - row8(uu_refs[d], i) for d in range(3)]
        else:
            pre = [row8(r, i - MHALO) for r in pre_in]
        inv = inv * (1.0 / STIFF_DIAG)
        for d in range(3):
            p_refs[d][at8(i), :] = jnp.where(inside, force[d] * inv + pre[d], 0.0)
    c_near = 2.0 * RHO1 / DELTA / STIFF_DIAG
    c_self = 1.0 + RHO1 * RHO0
    for i in range(2, n_m - 2):
        near = couple_sum([[row8(r, i - 1), row8(r, i), row8(r, i + 1)] for r in p_refs])
        inv = row8(mi_ref, i)
        for d in range(3):
            moved = row8(uu_refs[d], i) + c_self * row8(p_refs[d], i) + c_near * near[d]
            d_refs[d][at8(i), :] = moved * inv
    sub = sub_iota(mwidth)
    weight = jnp.where(sub < ML, (ML - sub).astype(jnp.float32) * (1.0 / (ML * (ML + 1) / 2.0)), 0.0)
    x_ref[24:32, :] = jnp.zeros((8, x_ref.shape[1]), jnp.float32)
    for g in range(mrows):
        i = MHALO + g
        u0, u2 = row8(d_refs[0], i), row8(d_refs[2], i)
        div = 0.5 * (next_sub(u0) - prev_sub(u0)) + 0.5 * (next_lane(u2) - prev_lane(u2))
        div = div + sign * (row8(d_refs[1], i + 1) - row8(d_refs[1], i - 1))
        stress = row8(mod_ref, i) * (div - 3.0 * row8(st_ref, i))
        die = jnp.sum(weight * stress, axis=0, keepdims=True)
        first, second = die[:, 0:LANES], die[:, LANES : 2 * LANES]
        keep_ref[16 + g : 17 + g, 0:LANES] = jnp.where(core == 0, first, second)
        x_ref[24 + g : 25 + g, 0:LANES] = jnp.where(core == 0, second, first)
        for d in range(3):
            u_ref[8 * (mrows * d + g) : 8 * (mrows * d + g) + 8, :] = row8(d_refs[d], i)[:, 0:mcols]


def k_out(rows, mrows, t_in, keep_ref, xr_ref, u_in, t_out, u_out, slow_ref, buf, die, wide_die, ubuf):
    half = slow_ref.shape[1]
    mcols = u_in.shape[1]
    core = lax.axis_index(CORE)

    def put(ref, at, x):
        count = ref.shape[0] * LANES // x.shape[1]
        for t, piece in enumerate(tiles(x)):
            ref[count * t + at : count * t + at + piece.shape[0], :] = piece

    def build(rev):
        lo = half if rev else 0
        for g in range(rows):
            i = rows - 1 - g if rev else g
            if g < 2:
                x = keep_ref[8 * g : 8 * g + 8, :]
            elif g < rows - 3:
                x = t_in[8 * (FRONT + g) : 8 * (FRONT + g) + 8, lo : lo + half]
            else:
                k = rows - 1 - g
                x = xr_ref[8 * k : 8 * k + 8, :]
            put(buf, 8 * i, x)
        for g in range(mrows):
            mine = 2 * mrows - 1 - g if rev else g
            theirs = g if rev else 2 * mrows - 1 - g
            die[mine : mine + 1, :] = keep_ref[16 + g : 17 + g, 0:LANES]
            die[theirs : theirs + 1, :] = xr_ref[24 + g : 25 + g, 0:LANES]
            for d in range(3):
                i = mrows - 1 - g if rev else g
                put(ubuf, 8 * (mrows * d + i), row8(u_in, mrows * d + g))

    @pl.when(core == 0)
    def _():
        build(False)

    @pl.when(core != 0)
    def _():
        build(True)

    for t in range(half // LANES):
        at = 8 * rows * t
        for l in range(DEPTH):
            t_out[l, :, tile_lanes(t)] = buf[pl.ds(at + l, rows, stride=8), :]
    for t in range(mcols // LANES):
        for d in range(3):
            for l in range(ML):
                u_out[d, l, :, tile_lanes(t)] = ubuf[pl.ds(8 * mrows * (3 * t + d) + l, mrows, stride=8), :]
    lane = lane_iota(2 * mrows)
    for t in range(half // LANES):
        x = gather_lanes(die[...], (lane + LANES * t) // 3)
        for b in range(3):
            wide_die[pl.ds(b, 2 * mrows, stride=3), :] = x
        slow = 1.0 + 0.2 * buf[pl.ds(8 * rows * t, rows, stride=8), :] + 0.5 * wide_die[...]
        slow_ref[:, tile_lanes(t)] = slow


def pairs(dims, sends):
    index = {}
    for r in range(dims[0]):
        for c in range(dims[1]):
            for a in range(dims[2]):
                index[(r, c, a)] = (r * dims[1] + c) * dims[2] + a
    out = []
    for source in index:
        target = sends(*source)
        if target in index:
            out.append((index[source], index[target]))
    return out


def per_device(temp, ids, power, mat, offset, heat_table, growth_table, modulus_table):
    axes = ("row", "col", "lay")
    dims = tuple(lax.axis_size(x) for x in axes)
    n_col = dims[1]
    _, rows, half = temp.shape
    _, _, mrows, mcols = offset.shape
    n_edges = 1 if n_col == 2 else 2
    n_t = half // LANES
    m_t = mcols // LANES

    def send(x, sends):
        return lax.ppermute(x, axes, pairs(dims, sends))

    def swap(r, c, a):
        return (r, c, 1 - a)

    def along(r, c, a):
        return (r + 1, c, 0) if a == 1 else (r - 1, c, 1)

    wide = 2 * half
    own = rows - 1
    kind = lax.broadcasted_iota(jnp.int32, (2, *temp.shape), 0)
    both = jnp.where(kind == 0, temp[None], power[None, None])
    tab = jnp.stack([heat_table, growth_table, modulus_table])
    tab = jnp.pad(tab, ((0, 0), (1, LANES - 1 - tab.shape[1])))
    (tab,) = call(k_tables, [(16 * (NMAT + 1) + 8, LANES)], [tab])
    n = 16 * HALO
    n_far = 8 * far_rows(rows)
    cells, one = call(k_rows, [(16 * rows * n_t, LANES), ((n + 16) * n_t, LANES)], [both, ids])
    got1 = send(one, swap)
    two, mg = call(
        functools.partial(k_rest, n_edges),
        [
            ((16 * (rows - 1 - HALO) + rows - 16) * n_t + 32 * MHALO * m_t + n_far + 8 * n_edges, LANES),
            (32 * mrows, mcols),
        ],
        [both, cells, offset, mat],
        scratch=[(32 * mrows * m_t, LANES)],
    )
    got2 = send(two, swap)
    *own_part, far = call(
        functools.partial(k_half, n_edges),
        [(8 * HALO, half)] * 3 + [(n_far * n_edges, LANES)],
        [tab, both, cells],
    )
    n_c = 32 + n_far - 8 * (-4 * (mrows - MHALO) * MSPAN // LANES) + 8
    z, first_rows, *edges = call(
        functools.partial(k_edge, n_edges),
        [(far_place(n_edges, -1, wide)[0].stop, wide), (n + 16, wide)] + [(32, LANES)] * n_edges,
        [tab, both, cells, got1, mg, *own_part],
        cost=EDGE_COST,
        scratch=[(8 * HALO, wide)] * 5,
    )
    zr = send(z, along)
    leaving = edges
    leaving = call(
        functools.partial(k_beside, n_edges, rows),
        [(n_c, LANES)] * n_edges + [x.shape for x in leaving],
        [far, got2, mg] + leaving,
        aliases={3 + k: n_edges + k for k in range(len(leaving))},
    )
    beside, near = leaving[:n_edges], leaving[n_edges:]
    if n_edges == 1:
        sides = [send(beside[0], lambda r, c, a: (r, 1 - c, a))]
        corners = [send(near[0], lambda r, c, a: along(r, 1 - c, a))]
    else:
        sides = [send(beside[0], lambda r, c, a: (r, c + 1, a)), send(beside[1], lambda r, c, a: (r, c - 1, a))]
        corners = [
            send(near[0], lambda r, c, a: along(r, c + 1, a)),
            send(near[1], lambda r, c, a: along(r, c - 1, a)),
        ]
    w, src, mw = call(
        functools.partial(k_chip, rows),
        [(16 * own, wide), (rows, wide), (32 * (mrows + MHALO), mcols)],
        [both, cells, got2, mg, first_rows],
    )
    width = wide + LANES
    mwidth = mcols + LANES
    n_w = 8 * (rows + FRONT + 4)
    inner = call(
        functools.partial(k_inner, n_edges, n_col, rows),
        [(n_w, width)] * 7 + [(8 * (mrows + MHALO), mwidth)],
        [tab, w, src] + sides,
        scratch=[(n_w * (width // LANES), LANES)],
    )
    t2 = inner[5]
    solid = call(
        functools.partial(k_mech, n_edges, n_col, rows), [(8 * (mrows + MHALO), mwidth)] * 8, [tab, mw] + sides
    )
    n_h = 8 * (AHEAD + HALO + 5)
    n_m = 8 * (mrows + 2 * MHALO)
    x, keep, u = call(
        functools.partial(k_outer, n_edges, n_col, rows),
        [(32, half), (24, half), (24 * mrows, mcols)],
        [tab, zr] + sides + corners + list(inner) + [src] + list(solid),
        scratch=[(n_h, width)] * 7
        + [(n_h * (width // LANES), LANES)]
        + [(n_m, mwidth)] * 13
        + [(8 * HALO, LANES)] * 4,
    )
    xr = send(x, swap)
    t_out, u_out, slow = call(
        functools.partial(k_out, rows, mrows),
        [temp.shape, offset.shape, power.shape],
        [t2, keep, xr, u],
        scratch=[
            (8 * rows * n_t, LANES),
            (2 * mrows, LANES),
            (rows, LANES),
            (24 * mrows * m_t, LANES),
        ],
    )
    return t_out, u_out, slow


def solution(mesh):
    placed = (
        P("grp", "row", ("col", "lay")),
        P("grp", "row", ("col", "lay")),
        P(("grp", "row"), ("col", "lay")),
        P("grp", ("row", "lay"), "col"),
        P(None, "grp", ("row", "lay"), "col"),
        P(),
        P(),
        P(),
    )
    return jax.shard_map(
        per_device,
        mesh=mesh,
        in_specs=placed,
        out_specs=(
            P("grp", "row", ("col", "lay")),
            P(None, "grp", ("row", "lay"), "col"),
            P(("grp", "row"), ("col", "lay")),
        ),
        check_vma=False,
    )
```
